32 devices in a mesh: seq: 8 (over z, y), wshard: 4 (over x, core).
Axes of the slice: x: 2, y: 2, z: 4, core: 2. Of those that a mesh axis runs over, the one named last changes fastest.
Arguments:
- block_in: bfloat16 [4, 8192, 1024], P('wshard', 'seq'), may hold values from -6 to 6
- norm_gain: float32 [1024], replicated, may hold values from 0.5 to 1.5
- in_weight: bfloat16 [1024, 4384], P('wshard'), may hold values from -0.1875 to 0.1875
- conv_x: float32 [4, 2048], P(None, 'seq'), may hold values from -3 to 3
- conv_x_bias: float32 [2048], P('seq'), may hold values from -3 to 3
- conv_bc: float32 [4, 256], replicated, may hold values from -3 to 3
- conv_bc_bias: float32 [256], replicated, may hold values from -3 to 3
- a_log: float32 [32], P('seq'), may hold values from -12 to 1
- skip: float32 [32], P('seq'), may hold values from -4 to 4
- dt_bias: float32 [32], P('seq'), may hold values from -5 to -2
- out_gain: float32 [2048], replicated, may hold values from 0.5 to 1.5
- out_weight: bfloat16 [2048, 1024], P('wshard'), may hold values from -0.125 to 0.125
- cotangent: bfloat16 [4, 8192, 1024], P('wshard', 'seq'), may hold values from -6 to 6
Outputs:
- output: bfloat16 [4, 8192, 1024], P('wshard', 'seq')
- input_grad: float32 [4, 8192, 1024], P('wshard', 'seq')
- norm_gain_grad: float32 [1024], replicated
- in_weight_grad: float32 [1024, 4384], P('wshard')
- conv_x_grad: float32 [4, 2048], P(None, 'seq')
- conv_x_bias_grad: float32 [2048], P('seq')
- conv_bc_grad: float32 [4, 256], replicated
- conv_bc_bias_grad: float32 [256], replicated
- a_log_grad: float32 [32], P('seq')
- skip_grad: float32 [32], P('seq')
- dt_bias_grad: float32 [32], P('seq')
- out_gain_grad: float32 [2048], replicated
- out_weight_grad: float32 [2048, 1024], P('wshard')
The draws below stay inside these ranges and needn't reach their ends.
All inputs are finite; a program needn't handle non-finite values.
Results may differ from the reference program's by a relative error of at most 0.012.
The reference program's roundings to bfloat16 on the way count: a program that leaves them out, or rounds other values in their place, can miss the bound.
Values may be sent and summed in bfloat16 or wider, within the bound.
No kernel may reach another device: no remote copies, remote signals or barrier semaphores. Data moves between devices by JAX's collectives and lax.ppermute only.
A program may use at most 640 MiB of HBM per device.

```python
import jax
import jax.numpy as jnp
from jax import lax

D = 1024
HEADS = 32
HEAD_DIM = 64
STATE = 128
KERNEL = 4
BLOCK = 256
INNER = 2048
PROJ = 4384
SEQLEN = 8192
SEQS = 4


def draw_a_log(key, part):
    key = jax.random.fold_in(key, 7)
    low_end = 20.0 / SEQLEN
    high_end = 2.0
    uniform_part = jax.random.uniform(key, (HEADS,), jnp.float32)
    return jnp.log(low_end) + uniform_part * (jnp.log(high_end) - jnp.log(low_end))


def steps_of(key, extent, split, smallest, largest):
    loudness, own = 1.0, jax.random.fold_in(key, 6)
    for axis_at, parts in split:
        heights = jnp.exp(jax.random.uniform(jax.random.fold_in(own, axis_at), (parts,), jnp.float32, smallest / len(split), largest / len(split)))
        loudness = loudness * jnp.repeat(heights, extent[axis_at] // parts).reshape([-1 if axis == axis_at else 1 for axis in range(len(extent))])
    return loudness


def noise(own_key, dims, spread, reach, pieces=(), dtype=jnp.bfloat16):
    gain = steps_of(own_key, dims, pieces, -0.22, 0.18) if pieces else 1.0
    array = jax.random.normal(own_key, dims, jnp.float32) * spread * gain
    return jnp.minimum(jnp.maximum(array, -reach), reach).astype(dtype)


def setup_inputs(seed: int = 0) -> dict:
    seeds = jax.random.split(jax.random.key(seed), 14)
    return {
        "block_in": noise(seeds[0], (SEQS, SEQLEN, D), 1.0, 6.0, ((0, 4), (1, 8))),
        "norm_gain": jnp.clip(1.0 + 0.1 * jax.random.normal(seeds[1], (D,), jnp.float32), 0.5, 1.5),
        "in_weight": noise(seeds[2], (D, PROJ), D ** -0.5, 0.1875, ((0, 4),)),
        "conv_x": noise(seeds[3], (KERNEL, INNER), 0.5, 3.0, ((1, 8),), jnp.float32),
        "conv_x_bias": noise(seeds[4], (INNER,), 0.5, 3.0, ((0, 8),), jnp.float32),
        "conv_bc": noise(seeds[5], (KERNEL, 2 * STATE), 0.5, 3.0, (), jnp.float32),
        "conv_bc_bias": noise(seeds[6], (2 * STATE,), 0.5, 3.0, (), jnp.float32),
        "a_log": draw_a_log(jax.random.fold_in(seeds[13], 71), 0),
        "skip": noise(seeds[8], (HEADS,), 1.0, 4.0, ((0, 8),), jnp.float32),
        "dt_bias": jnp.clip(-5.0 + 3.0 * jax.random.uniform(seeds[9], (HEADS,), jnp.float32) ** steps_of(seeds[9], (HEADS,), ((0, 8),), -0.2, 0.2), -5.0, -2.0),
        "out_gain": jnp.clip(1.0 + 0.1 * jax.random.normal(seeds[10], (INNER,), jnp.float32), 0.5, 1.5),
        "out_weight": noise(seeds[11], (INNER, D), INNER ** -0.5, 0.125, ((0, 4),)),
        "cotangent": noise(seeds[12], (SEQS, SEQLEN, D), 1.0, 6.0, ((0, 4), (1, 8))),
    }


@jax.custom_vjp
def low(v):
    return lax.optimization_barrier(v.astype(jnp.bfloat16)).astype(jnp.float32)

@jax.custom_vjp
def low_back(v):
    return v

def low_keep(v):
    return (low(v), None)

def low_pass(kept, grad):
    return (grad,)

def back_keep(v):
    return (v, None)

def back_low(kept, grad):
    return (low(grad),)
low.defvjp(low_keep, low_pass)
low_back.defvjp(back_keep, back_low)
epsilon = 1e-05
highest = lax.Precision.HIGHEST

def causal_conv(values, kernel, bias):
    taps = kernel.shape[0]
    length = values.shape[0]
    padded = jnp.concatenate([jnp.zeros((taps - 1, values.shape[1]), jnp.float32), values], axis=0)
    summed = jnp.zeros_like(values) + bias[None, :]
    for offset in range(taps):
        summed = summed + kernel[offset][None, :] * padded[offset:offset + length]
    return summed

def block_step(state, inputs):
    x_block, step_block, decay_block, b_block, c_block = inputs
    cumulative = jnp.cumsum(decay_block, axis=0)
    positions = jnp.arange(BLOCK)
    lower_mask = positions[:, None] >= positions[None, :]
    differences = cumulative[:, None, :] - cumulative[None, :, :]
    weights = jnp.exp(jnp.where(lower_mask[:, :, None], differences, -jnp.inf))
    scores = jnp.dot(c_block, b_block.T, precision=highest, preferred_element_type=jnp.float32)
    scaled = x_block * step_block[:, :, None]
    within = jnp.einsum('tsh,shp->thp', scores[:, :, None] * weights, scaled, precision=highest)
    carried = jnp.exp(cumulative)[:, :, None] * jnp.einsum('tn,hpn->thp', c_block, state, precision=highest)
    tail_decay = jnp.exp(cumulative[-1][None, :] - cumulative)
    new_state = jnp.exp(cumulative[-1])[:, None, None] * state + jnp.einsum('sn,shp->hpn', b_block, scaled * tail_decay[:, :, None], precision=highest)
    return (new_state, within + carried)

def state_mixer(x_raw, dt_raw, bc_raw, conv_x, conv_x_bias, conv_bc, conv_bc_bias, a_log, skip, dt_bias):
    length = x_raw.shape[0]
    count = length // BLOCK
    x_act = jax.nn.silu(causal_conv(x_raw, conv_x, conv_x_bias))
    bc_act = jax.nn.silu(causal_conv(bc_raw, conv_bc, conv_bc_bias))
    step_sizes = jax.nn.softplus(dt_raw + dt_bias[None, :])
    log_decay = -jnp.exp(a_log)[None, :] * step_sizes
    inputs = (x_act.reshape(count, BLOCK, HEADS, HEAD_DIM), step_sizes.reshape(count, BLOCK, HEADS), log_decay.reshape(count, BLOCK, HEADS), bc_act[:, :STATE].reshape(count, BLOCK, STATE), bc_act[:, STATE:].reshape(count, BLOCK, STATE))
    start = jnp.zeros((HEADS, HEAD_DIM, STATE), jnp.float32)
    last_state, outputs = lax.scan(jax.checkpoint(block_step), start, inputs)
    heads_view = outputs.reshape(length, HEADS, HEAD_DIM) + skip[None, :, None] * x_act.reshape(length, HEADS, HEAD_DIM)
    return heads_view.reshape(length, INNER)

def residual_block(sequence, norm_gain, in_weight, conv_x, conv_x_bias, conv_bc, conv_bc_bias, a_log, skip, dt_bias, out_gain, out_weight):
    scale_first = lax.rsqrt(lax.optimization_barrier(jnp.mean(sequence * sequence, axis=-1, keepdims=True)) + epsilon)
    normed = low(sequence * scale_first * norm_gain[None, :])
    projected = low(low_back(jnp.dot(normed, in_weight, precision=highest, preferred_element_type=jnp.float32)))
    gate_part = projected[:, :INNER]
    x_raw = projected[:, INNER:2 * INNER]
    bc_raw = projected[:, 2 * INNER:2 * INNER + 2 * STATE]
    dt_raw = projected[:, 2 * INNER + 2 * STATE:]
    mixed = low(low_back(state_mixer(x_raw, dt_raw, bc_raw, conv_x, conv_x_bias, conv_bc, conv_bc_bias, a_log, skip, dt_bias)))
    gated = mixed * jax.nn.silu(gate_part)
    scale_second = lax.rsqrt(lax.optimization_barrier(jnp.mean(gated * gated, axis=-1, keepdims=True)) + epsilon)
    normed_out = low(gated * scale_second * out_gain[None, :])
    return sequence + jnp.dot(normed_out, out_weight, precision=highest, preferred_element_type=jnp.float32)

def reference(block_in, norm_gain, in_weight, conv_x, conv_x_bias, conv_bc, conv_bc_bias, a_log, skip, dt_bias, out_gain, out_weight, cotangent):
    params = (norm_gain.astype(jnp.float32), in_weight.astype(jnp.float32), conv_x, conv_x_bias, conv_bc, conv_bc_bias, a_log, skip, dt_bias, out_gain, out_weight.astype(jnp.float32))

    def forward(inputs, *weights):
        return lax.map(lambda sequence: residual_block(sequence, *weights), inputs)
    result, pullback = jax.vjp(forward, block_in.astype(jnp.float32), *params)
    grads = pullback(cotangent.astype(jnp.float32))
    return (result.astype(jnp.bfloat16), grads[0], grads[1], grads[2], grads[3], grads[4], grads[5], grads[6], grads[7], grads[8], grads[9], grads[10], grads[11])
```

```python
import functools

import jax
import jax.numpy as jnp
from jax import lax
from jax.experimental import pallas as pl
from jax.experimental.pallas import tpu as pltpu
from jax.sharding import PartitionSpec as P

INNER = 2048
STATE = 128
HEADS = 32
TAPS = 4
BC = 2 * STATE
CH = INNER + BC
XCOLS = 2432
XUSED = 2336
Q = 256
TILE = 256
TILES = INNER // TILE
PAIRS = HEADS // 2
EDGE = 16
EPS = 1e-05

f32 = jnp.float32
bf16 = jnp.bfloat16
highest = lax.Precision.HIGHEST


def cparams(megabytes=56):
    return pltpu.CompilerParams(
        dimension_semantics=("arbitrary",), vmem_limit_bytes=megabytes * 2**20
    )


def dot(a, b):
    return lax.dot_general(a, b, (((1,), (0,)), ((), ())), preferred_element_type=f32)


def dot_lanes(a, b):
    return lax.dot_general(a, b, (((1,), (1,)), ((), ())), preferred_element_type=f32)


def dot_rows(a, b):
    return lax.dot_general(a, b, (((0,), (0,)), ((), ())), preferred_element_type=f32)


def sigmoid(v):
    return 0.5 * jnp.tanh(0.5 * v) + 0.5


def lane_iota(rows, lanes):
    return lax.broadcasted_iota(jnp.int32, (rows, lanes), 1)


def row_iota(rows, lanes):
    return lax.broadcasted_iota(jnp.int32, (rows, lanes), 0)


def pair_of(cols, first):
    rows = cols.shape[0]
    low = lane_iota(rows, 128) < 64
    return jnp.where(low, cols[:, first : first + 1], cols[:, first + 1 : first + 2])


def four_of(cols, first):
    return jnp.concatenate([pair_of(cols, first), pair_of(cols, first + 2)], axis=1)


def split_dot(value, select):
    high = value.astype(bf16)
    low = (value - high.astype(f32)).astype(bf16)
    return dot(high, select) + dot(low, select)


def halves(value):
    high = value.astype(bf16)
    return high, (value - high.astype(f32)).astype(bf16)


def fine(product, a, b):
    a_high, a_low = halves(a)
    b_high, b_low = halves(b)
    return product(a_high, b_high) + (product(a_high, b_low) + product(a_low, b_high))


def head_select(tile):
    lanes = row_iota(TILE, 128) >> 6
    return jnp.where(lanes + tile * (TILE // 64) == lane_iota(TILE, 128), 1.0, 0.0).astype(bf16)


def shifted(current, before):
    joined = jnp.concatenate([before[EDGE - 8 :], current], axis=0)
    rows = current.shape[0]
    return [joined[5 + k : 5 + k + rows] for k in range(TAPS - 1)] + [current]


def conv_of(parts, taps, bias):
    total = bias + taps[0:1] * parts[0]
    for k in range(1, TAPS):
        total = total + taps[k : k + 1] * parts[k]
    return total


def conv_back(grad, after, taps):
    joined = jnp.concatenate([grad, after], axis=0)
    rows = grad.shape[0]
    total = taps[TAPS - 1 : TAPS] * grad
    for k in range(TAPS - 1):
        total = total + taps[k : k + 1] * joined[TAPS - 1 - k : TAPS - 1 - k + rows]
    return total


def tile_at(j, width=TILE):
    return pl.ds(pl.multiple_of(j * width, width), width)


def project_kernel(order, tokens, edge, gain, w0, w1, w2, w3, normed, out, out_edge, full):
    rows = w0.shape[0]

    def norm(values):
        wide = values.astype(f32)
        scale = lax.rsqrt(jnp.mean(wide * wide, axis=1, keepdims=True) + EPS)
        return (wide * scale * gain[...]).astype(bf16)

    @pl.when(pl.program_id(0) == 0)
    def _():
        for k, piece in enumerate((w0, w1, w2, w3)):
            full[pl.ds(pl.multiple_of(order[k] * rows, rows), rows), :] = piece[...]
        early = norm(edge[...])
        out_edge[...] = dot(early, full[...]).astype(bf16)

    now = norm(tokens[...])
    normed[...] = now
    for start in range(0, XCOLS, TILE):
        stop = min(start + TILE, XCOLS)
        out[:, start:stop] = dot(now, full[:, start:stop]).astype(bf16)


def project(order, tokens, edge, gain, pieces):
    length, width = tokens.shape
    rows = pieces[0].shape[0]
    whole = lambda shape: pl.BlockSpec(shape, lambda i, o: (0,) * len(shape), pipeline_mode=pl.Buffered(1))
    return pl.pallas_call(
        project_kernel,
        grid_spec=pltpu.PrefetchScalarGridSpec(
            num_scalar_prefetch=1,
            grid=(length // Q,),
            in_specs=[
                pl.BlockSpec((Q, width), lambda i, o: (i, 0)),
                whole((EDGE, width)),
                whole((1, width)),
            ]
            + [whole((rows, XCOLS))] * 4,
            out_specs=[
                pl.BlockSpec((Q, width), lambda i, o: (i, 0)),
                pl.BlockSpec((Q, XCOLS), lambda i, o: (i, 0)),
                pl.BlockSpec((EDGE, XCOLS), lambda i, o: (0, 0)),
            ],
            scratch_shapes=[pltpu.VMEM((4 * rows, XCOLS), bf16)],
        ),
        out_shape=[
            jax.ShapeDtypeStruct((length, width), bf16),
            jax.ShapeDtypeStruct((length, XCOLS), bf16),
            jax.ShapeDtypeStruct((EDGE, XCOLS), bf16),
        ],
        compiler_params=cparams(),
        cost_estimate=pl.CostEstimate(flops=2 * length * width * XCOLS, bytes_accessed=14 * 2**20, transcendentals=0),
        name="project",
    )(order, tokens, edge, gain, *pieces)


def gate_kernel(order, normed, w0, w1, w2, w3, out, full):
    rows = w0.shape[0]

    @pl.when(pl.program_id(0) == 0)
    def _():
        for k, piece in enumerate((w0, w1, w2, w3)):
            full[pl.ds(pl.multiple_of(order[k] * rows, rows), rows), :] = piece[...]

    for j in range(TILES):
        cols = slice(j * TILE, (j + 1) * TILE)
        out[:, cols] = dot(normed[...], full[:, cols]).astype(bf16)


def gate_project(order, normed, pieces):
    length, width = normed.shape
    rows = pieces[0].shape[0]
    return pl.pallas_call(
        gate_kernel,
        grid_spec=pltpu.PrefetchScalarGridSpec(
            num_scalar_prefetch=1,
            grid=(length // Q,),
            in_specs=[pl.BlockSpec((Q, width), lambda i, o: (i, 0))]
            + [pl.BlockSpec((rows, INNER), lambda i, o: (0, 0), pipeline_mode=pl.Buffered(1))] * 4,
            out_specs=pl.BlockSpec((Q, INNER), lambda i, o: (i, 0)),
            scratch_shapes=[pltpu.VMEM((4 * rows, INNER), bf16)],
        ),
        out_shape=jax.ShapeDtypeStruct((length, INNER), bf16),
        compiler_params=cparams(),
        cost_estimate=pl.CostEstimate(flops=2 * length * width * INNER, bytes_accessed=10 * 2**20, transcendentals=0),
        name="gate_project",
    )(order, normed, *pieces)


def states_kernel(
    now, prior, edge, taps, bias, taps_bc, bias_bc, heads,
    x_act, bc_act, aux_out, cum_t, local, payload,
    run, total, b_rows,
):
    c = pl.program_id(0)
    first = c == 0

    @pl.when(first)
    def _():
        run[...] = jnp.zeros_like(run)
        total[...] = jnp.zeros_like(total)

    def before(cols):
        return jnp.where(first, edge[:, cols], prior[:, cols]).astype(f32)

    band = slice(INNER, CH)
    parts = shifted(now[:, band].astype(f32), before(band))
    pre = conv_of(parts, taps_bc[...], bias_bc[...])
    act = pre * sigmoid(pre)
    bc_act[...] = act
    b_rows[...] = act[:, :STATE].T

    raw = now[:, CH : CH + HEADS].astype(f32) + heads[2:3, :HEADS]
    step = jnp.maximum(raw, 0.0) + jnp.log1p(jnp.exp(-jnp.abs(raw)))
    decay = -jnp.exp(heads[0:1, :HEADS]) * step
    lower = jnp.where(row_iota(Q, Q) >= lane_iota(Q, Q), 1.0, 0.0)
    cumulative = jnp.dot(lower, decay, precision=highest, preferred_element_type=f32)
    last = cumulative[Q - 1 : Q]
    aux = jnp.concatenate([cumulative, step, jnp.exp(last - cumulative), jnp.exp(cumulative)], axis=1)
    aux_out[...] = aux
    cum_t[...] = aux.T[:HEADS]

    def body(j, carry):
        cols = tile_at(j)
        x_parts = shifted(now[:, cols].astype(f32), before(cols))
        pre_x = conv_of(x_parts, taps[:, cols], bias[:, cols])
        x = pre_x * sigmoid(pre_x)
        x_act[:, cols] = x
        turned = pltpu.roll(aux, lax.rem(128 - 4 * j, 128), 1)
        state = fine(dot, b_rows[...], x * (four_of(turned, 32) * four_of(turned, 64)))
        local[0, j] = state
        end = turned[Q - 1 : Q]
        run[j] = four_of(end, 96) * run[j] + state
        total[:, cols] += four_of(end, 0)
        return carry

    lax.fori_loop(0, TILES, body, 0)

    @pl.when(c == pl.num_programs(0) - 1)
    def _():
        for j in range(TILES):
            payload[j, :STATE, :] = run[j]
            payload[j, STATE:, :] = jnp.broadcast_to(total[:, j * TILE : (j + 1) * TILE], (8, TILE))


def whole_spec(shape):
    return pl.BlockSpec(shape, lambda i: (0,) * len(shape), pipeline_mode=pl.Buffered(1))


def states(proj, proj_edge, taps, bias, taps_bc, bias_bc, heads):
    length = proj.shape[0]
    chunks = length // Q
    per = Q // EDGE
    return pl.pallas_call(
        states_kernel,
        grid=(chunks,),
        in_specs=[
            pl.BlockSpec((Q, XCOLS), lambda i: (i, 0)),
            pl.BlockSpec((EDGE, XCOLS), lambda i: (jnp.maximum(i * per - 1, 0), 0)),
            whole_spec((EDGE, XCOLS)),
            whole_spec((TAPS, INNER)),
            whole_spec((1, INNER)),
            whole_spec((TAPS, BC)),
            whole_spec((1, BC)),
            whole_spec((8, 128)),
        ],
        out_specs=[
            pl.BlockSpec((Q, INNER), lambda i: (i, 0)),
            pl.BlockSpec((Q, BC), lambda i: (i, 0)),
            pl.BlockSpec((Q, 128), lambda i: (i, 0)),
            pl.BlockSpec((HEADS, Q), lambda i: (0, i)),
            pl.BlockSpec((1, TILES, STATE, TILE), lambda i: (i, 0, 0, 0)),
            pl.BlockSpec((TILES, STATE + 8, TILE), lambda i: (0, 0, 0)),
        ],
        out_shape=[
            jax.ShapeDtypeStruct((length, INNER), f32),
            jax.ShapeDtypeStruct((length, BC), f32),
            jax.ShapeDtypeStruct((length, 128), f32),
            jax.ShapeDtypeStruct((HEADS, length), f32),
            jax.ShapeDtypeStruct((chunks, TILES, STATE, TILE), f32),
            jax.ShapeDtypeStruct((TILES, STATE + 8, TILE), f32),
        ],
        scratch_shapes=[
            pltpu.VMEM((TILES, STATE, TILE), f32),
            pltpu.VMEM((1, INNER), f32),
            pltpu.VMEM((STATE, Q), f32),
        ],
        compiler_params=cparams(),
        cost_estimate=pl.CostEstimate(flops=2 * 10**10, bytes_accessed=20 * 2**20, transcendentals=0),
        name="states",
    )(proj, proj, proj_edge, taps, bias, taps_bc, bias_bc, heads)


def chain_kernel(forward, values, totals, out):
    count = out.shape[0]
    order = range(count) if forward else range(count - 1, -1, -1)
    state = jnp.zeros(out.shape[1:], f32)
    for i in order:
        out[i] = state
        state = jnp.exp(totals[i, 0:1, :]) * state + values[i, :STATE, :]


def chain(forward, values, totals):
    count, _, width = values.shape
    return pl.pallas_call(
        functools.partial(chain_kernel, forward),
        out_shape=jax.ShapeDtypeStruct((count, STATE, width), f32),
        compiler_params=pltpu.CompilerParams(vmem_limit_bytes=56 * 2**20),
        name="chain",
    )(values, totals)


def within_kernel(x_act, bc_act, aux, cum_t, skip, out, scores):
    lower = row_iota(Q, Q) >= lane_iota(Q, Q)
    scores[...] = jnp.where(lower, fine(dot_lanes, bc_act[:, STATE:], bc_act[:, :STATE]), 0.0)
    low = lane_iota(Q, 128) < 64

    def body(p, carry):
        cols = tile_at(p, 128)
        turned = pltpu.roll(aux[...], lax.rem(128 - 2 * p, 128), 1)
        x = x_act[:, cols]
        u = x * pair_of(turned, 32)
        results = []
        for i in range(2):
            difference = turned[:, i : i + 1] - cum_t[pl.ds(2 * p + i, 1), :]
            weights = jnp.exp(jnp.minimum(difference, 0.0))
            results.append(fine(dot, weights * scores[...], u))
        out[:, cols] = jnp.where(low, results[0], results[1]) + skip[:, cols] * x
        return carry

    lax.fori_loop(0, PAIRS, body, 0)


def within(x_act, bc_act, aux, cum_t, skip):
    length = x_act.shape[0]
    return pl.pallas_call(
        within_kernel,
        grid=(length // Q,),
        in_specs=[
            pl.BlockSpec((Q, INNER), lambda i: (i, 0)),
            pl.BlockSpec((Q, BC), lambda i: (i, 0)),
            pl.BlockSpec((Q, 128), lambda i: (i, 0)),
            pl.BlockSpec((HEADS, Q), lambda i: (0, i)),
            whole_spec((1, INNER)),
        ],
        out_specs=pl.BlockSpec((Q, INNER), lambda i: (i, 0)),
        out_shape=jax.ShapeDtypeStruct((length, INNER), f32),
        scratch_shapes=[pltpu.VMEM((Q, Q), f32)],
        compiler_params=cparams(),
        cost_estimate=pl.CostEstimate(flops=2 * 10**10, bytes_accessed=20 * 2**20, transcendentals=0),
        name="within",
    )(x_act, bc_act, aux, cum_t, skip)


def within_back_kernel(x_act, bc_act, aux, cum_t, dy, out, out_bc, scores, grad_scores):
    act = bc_act[...].astype(bf16)
    upper = row_iota(Q, Q) <= lane_iota(Q, Q)
    scores[...] = jnp.where(upper, dot_lanes(act[:, :STATE], act[:, STATE:]), 0.0)
    grad_scores[...] = jnp.zeros_like(grad_scores)
    low = lane_iota(Q, 128) < 64

    def body(p, carry):
        cols = tile_at(p, 128)
        turned = pltpu.roll(aux[...], lax.rem(128 - 2 * p, 128), 1)
        u = x_act[:, cols] * pair_of(turned, 32)
        grad = dy[:, cols]
        results = []
        for i in range(2):
            difference = cum_t[pl.ds(2 * p + i, 1), :] - turned[:, i : i + 1]
            weights = jnp.exp(jnp.minimum(difference, 0.0))
            mine = jnp.where(low if i == 0 else ~low, u, 0.0).astype(bf16)
            grad_scores[...] += weights * dot_lanes(mine, grad)
            results.append(dot((weights * scores[...]).astype(bf16), grad))
        out[:, cols] = jnp.where(low, results[0], results[1])
        return carry

    lax.fori_loop(0, PAIRS, body, 0)
    masked = jnp.where(upper, grad_scores[...], 0.0).astype(bf16)
    out_bc[:, :STATE] = dot(masked, act[:, STATE:])
    out_bc[:, STATE:] = dot_rows(masked, act[:, :STATE])


def within_back(x_act, bc_act, aux, cum_t, dy):
    length = x_act.shape[0]
    return pl.pallas_call(
        within_back_kernel,
        grid=(length // Q,),
        in_specs=[
            pl.BlockSpec((Q, INNER), lambda i: (i, 0)),
            pl.BlockSpec((Q, BC), lambda i: (i, 0)),
            pl.BlockSpec((Q, 128), lambda i: (i, 0)),
            pl.BlockSpec((HEADS, Q), lambda i: (0, i)),
            pl.BlockSpec((Q, INNER), lambda i: (i, 0)),
        ],
        out_specs=[
            pl.BlockSpec((Q, INNER), lambda i: (i, 0)),
            pl.BlockSpec((Q, BC), lambda i: (i, 0)),
        ],
        out_shape=[
            jax.ShapeDtypeStruct((length, INNER), f32),
            jax.ShapeDtypeStruct((length, BC), f32),
        ],
        scratch_shapes=[pltpu.VMEM((Q, Q), f32), pltpu.VMEM((Q, Q), f32)],
        compiler_params=cparams(),
        cost_estimate=pl.CostEstimate(flops=3 * 10**10, bytes_accessed=24 * 2**20, transcendentals=0),
        name="within_back",
    )(x_act, bc_act, aux, cum_t, dy)


def middle_kernel(
    order, y_in, bc_act, aux, local, entering, gate, tokens, cot, gain, w0, w1, w2, w3,
    normed_out, output, dy_out, grad_gate, ends, back_states, payload, y_dot, gain_grad,
    full, state, back, before, y_keep, gated_keep, grad_keep,
):
    c = pl.program_id(0)
    rows = w0.shape[0]

    @pl.when(c == 0)
    def _():
        for k, piece in enumerate((w0, w1, w2, w3)):
            full[pl.ds(pl.multiple_of(order[k] * rows, rows), rows), :] = piece[...]
        state[...] = entering[...]
        back[...] = jnp.zeros_like(back)
        before[...] = jnp.zeros_like(before)
        gain_grad[...] = jnp.zeros_like(gain_grad)

    keep = aux[...]
    c_cols = bc_act[:, STATE:]
    c_rows = bc_act[:, STATE:].T

    def turn(j):
        return pltpu.roll(keep, lax.rem(128 - 4 * j, 128), 1)

    def mix(j, squares):
        cols = tile_at(j)
        turned = turn(j)
        carried = fine(dot, c_cols, state[j])
        y = y_in[:, cols] + four_of(turned, 96) * carried
        y_keep[:, cols] = y
        raw = gate[:, cols].astype(f32)
        gated = y.astype(bf16).astype(f32) * (raw * sigmoid(raw))
        gated_keep[:, cols] = gated
        moved = four_of(turned[Q - 1 : Q], 96) * state[j] + local[0, j]
        state[j] = moved
        ends[0, j] = moved
        both = gated * gated
        return squares + (both[:, :128] + both[:, 128:])

    squares = lax.fori_loop(0, TILES, mix, jnp.zeros((Q, 128), f32))
    scale = lax.rsqrt(jnp.sum(squares, axis=1, keepdims=True) / INNER + EPS)

    def back_out(j, products):
        cols = tile_at(j)
        gated = gated_keep[:, cols]
        gains = gain[:, cols]
        normed_out[:, cols] = (gated * scale * gains).astype(bf16)
        grad = dot_lanes(cot[...], full[cols, :])
        grad_keep[:, cols] = grad
        gain_grad[:, cols] += jnp.sum(grad * gated * scale, axis=0, keepdims=True)
        both = grad * gains * gated
        return products + (both[:, :128] + both[:, 128:])

    products = lax.fori_loop(0, TILES, back_out, jnp.zeros((Q, 128), f32))
    shared = jnp.sum(products, axis=1, keepdims=True) / INNER * (scale * scale * scale)
    for start in range(0, output.shape[1], TILE):
        cols = slice(start, start + TILE)
        branch = dot(normed_out[...], full[:, cols])
        output[:, cols] = (tokens[:, cols].astype(f32) + branch).astype(bf16)

    def finish(j, y_sum):
        cols = tile_at(j)
        turned = turn(j)
        raw = gate[:, cols].astype(f32)
        sig = sigmoid(raw)
        grad_gated = scale * (grad_keep[:, cols] * gain[:, cols]) - gated_keep[:, cols] * shared
        y = y_keep[:, cols]
        dy = (grad_gated * (raw * sig)).astype(bf16)
        dy_out[:, cols] = dy
        mixed = y.astype(bf16).astype(f32)
        grad_gate[:, cols] = (grad_gated * mixed * (sig * (1.0 + raw * (1.0 - sig)))).astype(bf16)
        wide = dy.astype(f32)
        piece = fine(dot, c_rows, wide * four_of(turned, 96))
        back_states[0, j] = piece
        back[j] += jnp.exp(before[:, cols]) * piece
        before[:, cols] += four_of(turned[Q - 1 : Q], 0)
        return y_sum + split_dot(wide * y, head_select(j))

    y_dot[...] = lax.fori_loop(0, TILES, finish, jnp.zeros((Q, 128), f32))

    @pl.when(c == pl.num_programs(0) - 1)
    def _():
        payload[...] = back[...]


def middle(order, y_in, bc_act, aux, local, entering, gate, tokens, cot, gain, pieces):
    length, width = tokens.shape
    rows = pieces[0].shape[0]
    chunks = length // Q
    block = lambda cols: pl.BlockSpec((Q, cols), lambda i, o: (i, 0))
    whole = lambda shape: pl.BlockSpec(shape, lambda i, o: (0,) * len(shape), pipeline_mode=pl.Buffered(1))
    per_chunk = pl.BlockSpec((1, TILES, STATE, TILE), lambda i, o: (i, 0, 0, 0))
    return pl.pallas_call(
        middle_kernel,
        grid_spec=pltpu.PrefetchScalarGridSpec(
            num_scalar_prefetch=1,
            grid=(chunks,),
            in_specs=[
                block(INNER),
                block(BC),
                block(128),
                per_chunk,
                whole((TILES, STATE, TILE)),
                block(INNER),
                block(width),
                block(width),
                whole((1, INNER)),
            ]
            + [whole((rows, width))] * 4,
            out_specs=[
                block(INNER),
                block(width),
                block(INNER),
                block(INNER),
                per_chunk,
                per_chunk,
                pl.BlockSpec((TILES, STATE, TILE), lambda i, o: (0, 0, 0)),
                block(128),
                pl.BlockSpec((1, INNER), lambda i, o: (0, 0)),
            ],
            scratch_shapes=[
                pltpu.VMEM((4 * rows, width), bf16),
                pltpu.VMEM((TILES, STATE, TILE), f32),
                pltpu.VMEM((TILES, STATE, TILE), f32),
                pltpu.VMEM((1, INNER), f32),
                pltpu.VMEM((Q, INNER), f32),
                pltpu.VMEM((Q, INNER), f32),
                pltpu.VMEM((Q, INNER), f32),
            ],
        ),
        out_shape=[
            jax.ShapeDtypeStruct((length, INNER), bf16),
            jax.ShapeDtypeStruct((length, width), bf16),
            jax.ShapeDtypeStruct((length, INNER), bf16),
            jax.ShapeDtypeStruct((length, INNER), bf16),
            jax.ShapeDtypeStruct((chunks, TILES, STATE, TILE), f32),
            jax.ShapeDtypeStruct((chunks, TILES, STATE, TILE), f32),
            jax.ShapeDtypeStruct((TILES, STATE, TILE), f32),
            jax.ShapeDtypeStruct((length, 128), f32),
            jax.ShapeDtypeStruct((1, INNER), f32),
        ],
        compiler_params=cparams(),
        cost_estimate=pl.CostEstimate(flops=4 * 10**10, bytes_accessed=40 * 2**20, transcendentals=0),
        name="middle",
    )(order, y_in, bc_act, aux, local, entering, gate, tokens, cot, gain, *pieces)


def back_kernel(
    now, prior, edge, taps, bias, taps_bc, bias_bc, heads, skip,
    dy, du_in, bc_act, bc_in, aux, y_dot, ends_before, ends_now, entering, back_states, leaving,
    grad, grad_taps, grad_taps_bc, grad_heads, tail, start,
    later, after, x_dot, k_dot, edge_dot, b_sum, c_sum,
):
    step_id = pl.program_id(0)
    c = pl.num_programs(0) - 1 - step_id
    first = c == 0

    @pl.when(step_id == 0)
    def _():
        later[...] = leaving[...]
        after[...] = jnp.zeros_like(after)
        grad_taps[...] = jnp.zeros_like(grad_taps)
        grad_taps_bc[...] = jnp.zeros_like(grad_taps_bc)
        grad_heads[...] = jnp.zeros_like(grad_heads)

    def before(cols):
        return jnp.where(first, edge[:, cols], prior[:, cols]).astype(f32)

    keep = aux[...]
    act = bc_act[...].astype(bf16)
    x_dot[...] = jnp.zeros_like(x_dot)
    k_dot[...] = jnp.zeros_like(k_dot)
    edge_dot[...] = jnp.zeros_like(edge_dot)
    b_sum[...] = bc_in[:, :STATE]
    c_sum[...] = bc_in[:, STATE:]

    def through(cols, dv, parts, tap_values):
        sums = [jnp.sum(dv * part, axis=0, keepdims=True) for part in parts]
        sums.append(jnp.sum(dv, axis=0, keepdims=True))
        result = conv_back(dv, after[:, cols], tap_values)
        after[:, cols] = dv[:8]
        grad[:, cols] = result.astype(bf16)

        @pl.when(step_id == 0)
        def _():
            tail[:, cols] = result[Q - EDGE :]

        return jnp.concatenate(sums + [jnp.zeros((3, sums[0].shape[1]), f32)], axis=0)

    def body(j, carry):
        cols = tile_at(j)
        turned = pltpu.roll(keep, lax.rem(128 - 4 * j, 128), 1)
        step = four_of(turned, 32)
        tail_decay = four_of(turned, 64)
        parts = shifted(now[:, cols].astype(f32), before(cols))
        tap_values = taps[:, cols]
        pre = conv_of(parts, tap_values, bias[:, cols])
        sig = sigmoid(pre)
        x = pre * sig
        wide = dy[:, cols].astype(f32)
        later_state = later[j]
        later_low = later_state.astype(bf16)
        du = du_in[:, cols] + tail_decay * dot(act[:, :STATE], later_low)
        select = head_select(j)
        x_dot[...] += split_dot(x * du, select)
        k_dot[...] += split_dot(x * wide, select)
        enter = jnp.where(first, entering[j], ends_before[0, j])
        b_sum[...] += fine(dot_lanes, x * step * tail_decay, later_state)
        c_sum[...] += fine(dot_lanes, wide * four_of(turned, 96), enter)
        meet = jnp.sum(ends_now[0, j] * later_state, axis=0, keepdims=True)
        edge_dot[...] += split_dot(jnp.broadcast_to(meet, (8, TILE)), select)
        later[j] = four_of(turned[Q - 1 : Q], 96) * later_state + back_states[0, j]
        dx = step * du + skip[:, cols] * wide
        dv = dx * (sig * (1.0 + pre * (1.0 - sig)))
        grad_taps[:, cols] += through(cols, dv, parts, tap_values)
        return carry

    lax.fori_loop(0, TILES, body, 0)

    band = slice(INNER, CH)
    parts = shifted(now[:, band].astype(f32), before(band))
    pre = conv_of(parts, taps_bc[...], bias_bc[...])
    sig = sigmoid(pre)
    grad_act = jnp.concatenate([b_sum[...], c_sum[...]], axis=1)
    dv = grad_act * (sig * (1.0 + pre * (1.0 - sig)))
    grad_taps_bc[...] += through(band, dv, parts, taps_bc[...])

    step = keep[:, HEADS : 2 * HEADS]
    by_step = x_dot[:, :HEADS]
    by_skip = k_dot[:, :HEADS]
    rate = -jnp.exp(heads[0:1, :HEADS])
    by_sum = y_dot[:, :HEADS] - heads[1:2, :HEADS] * by_skip - step * by_step
    upper = jnp.where(row_iota(Q, Q) <= lane_iota(Q, Q), 1.0, 0.0)
    by_decay = jnp.dot(upper, by_sum, precision=highest, preferred_element_type=f32) + edge_dot[0:1, :HEADS]
    raw = now[:, CH : CH + HEADS].astype(f32) + heads[2:3, :HEADS]
    grad_dt = (by_step + by_decay * rate) * sigmoid(raw)
    full_dt = jnp.concatenate([grad_dt, jnp.zeros((Q, 128 - HEADS), f32)], axis=1)
    grad[:, CH:] = full_dt.astype(bf16)
    sums = [
        jnp.sum(by_decay * (rate * step), axis=0, keepdims=True),
        jnp.sum(by_skip, axis=0, keepdims=True),
        jnp.sum(grad_dt, axis=0, keepdims=True),
        jnp.zeros((5, HEADS), f32),
    ]
    grad_heads[:, :HEADS] += jnp.concatenate(sums, axis=0)

    @pl.when(first)
    def _():
        start[...] = after[...]


def backward(
    proj, proj_edge, taps, bias, taps_bc, bias_bc, heads, skip,
    dy, du, bc_act, grad_bc, aux, y_dot, ends, entering, back_states, leaving,
):
    length = proj.shape[0]
    chunks = length // Q
    per = Q // EDGE
    at = lambda i: chunks - 1 - i
    block = lambda cols: pl.BlockSpec((Q, cols), lambda i: (at(i), 0))
    per_chunk = pl.BlockSpec((1, TILES, STATE, TILE), lambda i: (at(i), 0, 0, 0))
    return pl.pallas_call(
        back_kernel,
        grid=(chunks,),
        in_specs=[
            block(XCOLS),
            pl.BlockSpec((EDGE, XCOLS), lambda i: (jnp.maximum(at(i) * per - 1, 0), 0)),
            whole_spec((EDGE, XCOLS)),
            whole_spec((TAPS, INNER)),
            whole_spec((1, INNER)),
            whole_spec((TAPS, BC)),
            whole_spec((1, BC)),
            whole_spec((8, 128)),
            whole_spec((1, INNER)),
            block(INNER),
            block(INNER),
            block(BC),
            block(BC),
            block(128),
            block(128),
            pl.BlockSpec((1, TILES, STATE, TILE), lambda i: (jnp.maximum(at(i) - 1, 0), 0, 0, 0)),
            per_chunk,
            whole_spec((TILES, STATE, TILE)),
            per_chunk,
            whole_spec((TILES, STATE, TILE)),
        ],
        out_specs=[
            block(XCOLS),
            pl.BlockSpec((8, INNER), lambda i: (0, 0)),
            pl.BlockSpec((8, BC), lambda i: (0, 0)),
            pl.BlockSpec((8, 128), lambda i: (0, 0)),
            pl.BlockSpec((EDGE, CH), lambda i: (0, 0)),
            pl.BlockSpec((8, CH), lambda i: (0, 0)),
        ],
        out_shape=[
            jax.ShapeDtypeStruct((length, XCOLS), bf16),
            jax.ShapeDtypeStruct((8, INNER), f32),
            jax.ShapeDtypeStruct((8, BC), f32),
            jax.ShapeDtypeStruct((8, 128), f32),
            jax.ShapeDtypeStruct((EDGE, CH), f32),
            jax.ShapeDtypeStruct((8, CH), f32),
        ],
        scratch_shapes=[
            pltpu.VMEM((TILES, STATE, TILE), f32),
            pltpu.VMEM((8, CH), f32),
            pltpu.VMEM((Q, 128), f32),
            pltpu.VMEM((Q, 128), f32),
            pltpu.VMEM((8, 128), f32),
            pltpu.VMEM((Q, STATE), f32),
            pltpu.VMEM((Q, STATE), f32),
        ],
        compiler_params=cparams(),
        cost_estimate=pl.CostEstimate(flops=4 * 10**10, bytes_accessed=40 * 2**20, transcendentals=0),
        name="backward",
    )(
        proj, proj, proj_edge, taps, bias, taps_bc, bias_bc, heads, skip,
        dy, du, bc_act, grad_bc, aux, y_dot, ends, ends, entering, back_states, leaving,
    )


def input_kernel(order, grad_gate, grad_x, tokens, cot, gain, g0, g1, g2, g3, x0, x1, x2, x3, out, gain_grad):
    rows = g0.shape[0]

    @pl.when(pl.program_id(0) == 0)
    def _():
        gain_grad[...] = jnp.zeros_like(gain_grad)

    for k, (gate_w, x_w) in enumerate(((g0, x0), (g1, x1), (g2, x2), (g3, x3))):
        cols = pl.ds(pl.multiple_of(order[k] * rows, rows), rows)
        out[:, cols] = dot_lanes(grad_gate[...], gate_w[...]) + dot_lanes(grad_x[...], x_w[...])
    grad = out[...]
    wide = tokens[...].astype(f32)
    width = wide.shape[1]
    scale = lax.rsqrt(jnp.mean(wide * wide, axis=1, keepdims=True) + EPS)
    gain_grad[...] += jnp.sum(grad * wide * scale, axis=0, keepdims=True)
    scaled = grad * gain[...]
    shared = jnp.sum(scaled * wide, axis=1, keepdims=True) / width
    out[...] = cot[...].astype(f32) + (scale * scaled - wide * (scale * scale * scale * shared))


def input_back(order, grad_gate, grad_x, tokens, cot, gain, gate_pieces, x_pieces):
    length, width = tokens.shape
    rows = gate_pieces[0].shape[0]
    block = lambda cols: pl.BlockSpec((Q, cols), lambda i, o: (i, 0))
    whole = lambda shape: pl.BlockSpec(shape, lambda i, o: (0,) * len(shape), pipeline_mode=pl.Buffered(1))
    return pl.pallas_call(
        input_kernel,
        grid_spec=pltpu.PrefetchScalarGridSpec(
            num_scalar_prefetch=1,
            grid=(length // Q,),
            in_specs=[block(INNER), block(XCOLS), block(width), block(width), whole((1, width))]
            + [whole((rows, INNER))] * 4
            + [whole((rows, XCOLS))] * 4,
            out_specs=[block(width), pl.BlockSpec((1, width), lambda i, o: (0, 0))],
        ),
        out_shape=[
            jax.ShapeDtypeStruct((length, width), f32),
            jax.ShapeDtypeStruct((1, width), f32),
        ],
        compiler_params=cparams(),
        cost_estimate=pl.CostEstimate(flops=2 * length * width * (INNER + XCOLS), bytes_accessed=20 * 2**20, transcendentals=0),
        name="input_back",
    )(order, grad_gate, grad_x, tokens, cot, gain, *gate_pieces, *x_pieces)


def swap(value, axis, bit):
    count = lax.axis_size(axis)
    return lax.ppermute(value, axis, [(i, i ^ bit) for i in range(count)])


def gather_pieces(piece):
    across = swap(piece, "wshard", 2)
    beside = swap(piece, "wshard", 1)
    return piece, beside, across, swap(across, "wshard", 1)


def exchange(value, axis):
    return lax.all_to_all(value, axis, split_axis=0, concat_axis=0, tiled=True)


def to_owners(value, count):
    if count == TILES:
        return value
    rows = value.shape[1]
    width = INNER // count
    lanes = value.reshape(TILES, rows, TILE // width, width)
    return lanes.transpose(0, 2, 1, 3).reshape(count, rows, width)


def from_owners(value):
    count, rows, width = value.shape
    if count == TILES:
        return value
    lanes = value.reshape(TILES, TILE // width, rows, width)
    return lanes.transpose(0, 2, 1, 3).reshape(TILES, rows, TILE)


def sum_to_rows(partial):
    rows = partial.shape[0] // 4
    cols = partial.shape[1]
    me = lax.axis_index("wshard")
    blocks = [
        lax.dynamic_slice_in_dim(partial, (me ^ k) * rows, rows, axis=0) for k in range(4)
    ]
    sent = jnp.stack([blocks[1], blocks[3]]).astype(bf16)
    got = swap(sent, "wshard", 1).astype(f32)
    mine = blocks[0] + got[0]
    other = (blocks[2] + got[1]).astype(bf16)
    mine = mine + swap(other, "wshard", 2).astype(f32)
    count = lax.axis_size("seq")
    place = lax.axis_index("seq")
    half = rows // 2
    group = count // 2
    bit = place & 1
    theirs = lax.dynamic_slice_in_dim(mine, (1 - bit) * half, half, axis=0).astype(bf16)
    kept = lax.dynamic_slice_in_dim(mine, bit * half, half, axis=0)
    kept = kept + swap(theirs, "seq", 1).astype(f32)
    groups = [[2 * i + b for i in range(group)] for b in range(2)]
    spread = lambda v: lax.all_to_all(
        v, "seq", split_axis=0, concat_axis=0, tiled=True, axis_index_groups=groups
    )
    parts = spread(kept.astype(bf16).reshape(group, half // group, cols))
    owned = jnp.sum(parts.astype(f32), axis=0).astype(bf16)
    full_half = spread(jnp.broadcast_to(owned[None], (group,) + owned.shape)).reshape(half, cols)
    other_half = swap(full_half, "seq", 1)
    first = jnp.where(bit == 0, full_half, other_half)
    second = jnp.where(bit == 0, other_half, full_half)
    return jnp.concatenate([first, second], axis=0).astype(f32)


def local(
    block_in, norm_gain, in_weight, conv_x, conv_x_bias, conv_bc, conv_bc_bias,
    a_log, skip, dt_bias, out_gain, out_weight, cotangent,
):
    tokens = block_in[0]
    cot = cotangent[0]
    length, width = tokens.shape
    seq = lax.axis_size("seq")
    shards = lax.axis_size("wshard")
    own_heads = HEADS // seq
    own_ch = INNER // seq
    me = lax.axis_index("wshard")
    order = jnp.stack([me ^ k for k in range(4)]).astype(jnp.int32)

    x_piece = jnp.pad(in_weight[:, INNER:], ((0, 0), (0, XCOLS - XUSED)))
    edge = lax.ppermute(tokens[length - EDGE :], "seq", [(i, i + 1) for i in range(seq - 1)])
    small = jnp.concatenate(
        [
            conv_x,
            conv_x_bias[None],
            jnp.pad(jnp.stack([a_log, skip, dt_bias]), ((0, 0), (0, own_ch - own_heads))),
        ],
        axis=0,
    )
    small_all = exchange(jnp.broadcast_to(small[None], (seq,) + small.shape), "seq")
    x_pieces = gather_pieces(x_piece)
    x_params = small_all[:, :5].transpose(1, 0, 2).reshape(5, INNER)
    head_params = small_all[:, 5:, :own_heads].transpose(1, 0, 2).reshape(3, HEADS)
    taps, bias = x_params[:4], x_params[4:5]
    heads = jnp.pad(head_params, ((0, 5), (0, 128 - HEADS)))
    skip_row = jnp.repeat(head_params[1], INNER // HEADS)[None]

    normed, proj, proj_edge = project(order, tokens, edge, norm_gain[None], x_pieces)
    gate_pieces = gather_pieces(in_weight[:, :INNER])
    out_pieces = gather_pieces(out_weight)
    x_act, bc_act, aux, cum_t, chunk_states, payload = states(
        proj, proj_edge, taps, bias, conv_bc, conv_bc_bias[None], heads
    )
    arrived = exchange(to_owners(payload, seq), "seq")
    gate = gate_project(order, normed, gate_pieces)
    y_within = within(x_act, bc_act, aux, cum_t, skip_row)
    totals = arrived[:, STATE:, :]
    entering = from_owners(exchange(chain(True, arrived, totals), "seq"))
    normed_out, output, dy, grad_gate, ends, back_states, back_payload, y_dot, out_gain_grad = middle(
        order, y_within, bc_act, aux, chunk_states, entering, gate, tokens, cot, out_gain[None], out_pieces
    )
    back_arrived = exchange(to_owners(back_payload, seq), "seq")
    du, grad_bc = within_back(x_act, bc_act, aux, cum_t, dy)
    out_weight_grad = dot_rows(normed_out, cot)
    gate_weight_grad = dot_rows(normed, grad_gate)
    leaving = from_owners(exchange(chain(False, back_arrived, totals), "seq"))
    grad_x, grad_taps, grad_taps_bc, grad_heads, tail, start = backward(
        proj, proj_edge, taps, bias, conv_bc, conv_bc_bias[None], heads, skip_row,
        dy, du, bc_act, grad_bc, aux, y_dot, ends, entering, back_states, leaving,
    )
    out_owned = sum_to_rows(out_weight_grad)
    gate_owned = sum_to_rows(gate_weight_grad)
    after = lax.ppermute(start, "seq", [(i, i - 1) for i in range(1, seq)])
    all_taps = jnp.concatenate([taps, conv_bc], axis=1)
    fixes = [
        tail[EDGE - 3 + a] + sum(all_taps[k] * after[a - k] for k in range(a + 1)) for a in range(3)
    ]
    fixed = jnp.concatenate([tail[: EDGE - 3], jnp.stack(fixes)], axis=0).astype(bf16)
    grad_x = lax.dynamic_update_slice(grad_x, fixed, (length - EDGE, 0))
    x_weight_grad = dot_rows(normed, grad_x)
    x_owned = sum_to_rows(x_weight_grad)
    input_grad, norm_gain_grad = input_back(
        order, grad_gate, grad_x, tokens, cot, norm_gain[None], gate_pieces, x_pieces
    )

    shared = jnp.concatenate(
        [norm_gain_grad[0], out_gain_grad[0], grad_taps_bc[:5].reshape(-1)]
    )
    mine = jnp.concatenate(
        [
            grad_taps[:5].reshape(5, seq, own_ch).transpose(1, 0, 2).reshape(seq, 5 * own_ch),
            grad_heads[:3, :HEADS].reshape(3, seq, own_heads).transpose(1, 0, 2).reshape(seq, 3 * own_heads),
        ],
        axis=1,
    )
    shared_size, mine_size = shared.shape[0], mine.shape[1]
    pad = -(shared_size + mine_size) % 1024
    small_out = jnp.concatenate(
        [jnp.broadcast_to(shared[None], (seq, shared_size)), mine, jnp.zeros((seq, pad), f32)], axis=1
    )
    small_out = jnp.broadcast_to(small_out[:, None], (seq, shards, small_out.shape[1]))
    small_sum = jnp.sum(
        exchange(small_out.reshape(seq * shards, 8, -1), ("seq", "wshard")), axis=0
    ).reshape(-1)
    in_owned = jnp.concatenate([gate_owned, x_owned[:, :XUSED]], axis=1)
    pos = [0]

    def take(shape):
        size = 1
        for extent in shape:
            size *= extent
        out = small_sum[pos[0] : pos[0] + size].reshape(shape)
        pos[0] += size
        return out

    norm_gain_sum = take((width,))
    out_gain_sum = take((INNER,))
    bc_sum = take((5, BC))
    x_sum = take((5, own_ch))
    head_sum = take((3, own_heads))
    return (
        output[None],
        input_grad[None],
        norm_gain_sum,
        in_owned,
        x_sum[:4],
        x_sum[4],
        bc_sum[:4],
        bc_sum[4],
        head_sum[0],
        head_sum[1],
        head_sum[2],
        out_gain_sum,
        out_owned,
    )


def solution(mesh):
    in_specs = (
        P("wshard", "seq", None),
        P(),
        P("wshard", None),
        P(None, "seq"),
        P("seq"),
        P(),
        P(),
        P("seq"),
        P("seq"),
        P("seq"),
        P(),
        P("wshard", None),
        P("wshard", "seq", None),
    )
    out_specs = (
        P("wshard", "seq", None),
        P("wshard", "seq", None),
        P(),
        P("wshard", None),
        P(None, "seq"),
        P("seq"),
        P(),
        P(),
        P("seq"),
        P("seq"),
        P("seq"),
        P(),
        P("wshard", None),
    )
    return jax.shard_map(local, mesh=mesh, in_specs=in_specs, out_specs=out_specs, check_vma=False)
```

```python
import functools

import jax
import jax.numpy as jnp
from jax import lax
from jax.experimental import pallas as pl
from jax.experimental.pallas import tpu as pltpu
from jax.sharding import PartitionSpec as P

INNER = 2048
STATE = 128
HEADS = 32
TAPS = 4
BC = 2 * STATE
CH = INNER + BC
XCOLS = 2432
XUSED = 2336
Q = 256
HALF = Q // 2
TILE = 256
TILES = INNER // TILE
GROUPS = 2
GT = TILES // GROUPS
GW = INNER // GROUPS
REST = XCOLS - INNER
PIECES = 2 * GT
EDGE = 16
EPS = 1e-05

f32 = jnp.float32
bf16 = jnp.bfloat16
highest = lax.Precision.HIGHEST


def cparams(megabytes=56):
    return pltpu.CompilerParams(
        dimension_semantics=("arbitrary",), vmem_limit_bytes=megabytes * 2**20
    )


def dot(a, b):
    return lax.dot_general(a, b, (((1,), (0,)), ((), ())), preferred_element_type=f32)


def dot_lanes(a, b):
    return lax.dot_general(a, b, (((1,), (1,)), ((), ())), preferred_element_type=f32)


def dot_rows(a, b):
    return lax.dot_general(a, b, (((0,), (0,)), ((), ())), preferred_element_type=f32)


def sigmoid(v):
    return 0.5 * jnp.tanh(0.5 * v) + 0.5


def lane_iota(rows, lanes):
    return lax.broadcasted_iota(jnp.int32, (rows, lanes), 1)


def row_iota(rows, lanes):
    return lax.broadcasted_iota(jnp.int32, (rows, lanes), 0)


def spread(terms, width, first, shift):
    rows = row_iota(terms * HEADS, width) & (HEADS - 1)
    return jnp.where(rows == first + (lane_iota(terms * HEADS, width) >> shift), 1.0, 0.0).astype(bf16)


def halves(value):
    high = value.astype(bf16)
    return high, (value - high.astype(f32)).astype(bf16)


def terms2(value):
    return jnp.concatenate(halves(value), axis=1)


def terms4(value):
    high = value.astype(bf16)
    rest = value - high.astype(f32)
    middle, low = halves(rest)
    return jnp.concatenate([high, middle, low, jnp.zeros_like(high)], axis=1)


def split_dot(value, select):
    high = value.astype(bf16)
    low = (value - high.astype(f32)).astype(bf16)
    return dot(high, select) + dot(low, select)


def fine(product, a, b):
    a_high, a_low = halves(a)
    b_high, b_low = halves(b)
    return product(a_high, b_high) + (product(a_high, b_low) + product(a_low, b_high))


def head_select(tile):
    lanes = row_iota(TILE, 128) >> 6
    return jnp.where(lanes + tile * (TILE // 64) == lane_iota(TILE, 128), 1.0, 0.0).astype(bf16)


def shifted(current, before):
    joined = jnp.concatenate([before[EDGE - 8 :], current], axis=0)
    rows = current.shape[0]
    return [joined[5 + k : 5 + k + rows] for k in range(TAPS - 1)] + [current]


def conv_of(parts, taps, bias):
    total = bias + taps[0:1] * parts[0]
    for k in range(1, TAPS):
        total = total + taps[k : k + 1] * parts[k]
    return total


def later_rows(grad, after):
    joined = jnp.concatenate([grad, after], axis=0)
    rows = grad.shape[0]
    return [joined[TAPS - 1 - k : TAPS - 1 - k + rows] for k in range(TAPS - 1)] + [grad]


def tap_sums(parts, raw, grad, early):
    first = grad[:8]
    sums = []
    for k in range(TAPS):
        total = jnp.sum(parts[k] * raw, axis=0, keepdims=True)
        if k < TAPS - 1:
            total = total + jnp.sum(first[: TAPS - 1 - k] * early[8 - TAPS + 1 + k :], axis=0, keepdims=True)
        sums.append(total)
    sums.append(jnp.sum(grad, axis=0, keepdims=True))
    sums.append(jnp.zeros((3, grad.shape[1]), f32))
    return jnp.concatenate(sums, axis=0)


def tile_at(j, width=TILE):
    return pl.ds(pl.multiple_of(j * width, width), width)


def assemble(order, pieces, full):
    rows = pieces[0].shape[0]
    for k, piece in enumerate(pieces):
        full[pl.ds(pl.multiple_of(order[k] * rows, rows), rows), :] = piece[...]


def norm_rows(values, gain):
    wide = values.astype(f32)
    scale = lax.rsqrt(jnp.mean(wide * wide, axis=1, keepdims=True) + EPS)
    return (wide * scale * gain).astype(bf16)


def project_kernel(order, tokens, edge, gain, w0, w1, w2, w3, normed, out, out_rest, out_edge, out_edge_rest, full):
    @pl.when(pl.program_id(0) == 0)
    def _():
        assemble(order, (w0, w1, w2, w3), full)
        early = dot(norm_rows(edge[...], gain[...]), full[...]).astype(bf16)
        out_edge[...] = early[:, :GW]
        out_edge_rest[...] = early[:, GW:]

    now = norm_rows(tokens[...], gain[...])
    normed[...] = now
    for start in range(0, GW, TILE):
        out[:, start : start + TILE] = dot(now, full[:, start : start + TILE]).astype(bf16)
    out_rest[...] = dot(now, full[:, GW:]).astype(bf16)


def project_more_kernel(order, normed, edge, gain, w0, w1, w2, w3, out, out_edge, full):
    @pl.when(pl.program_id(0) == 0)
    def _():
        assemble(order, (w0, w1, w2, w3), full)
        out_edge[...] = dot(norm_rows(edge[...], gain[...]), full[...]).astype(bf16)

    for start in range(0, GW, TILE):
        out[:, start : start + TILE] = dot(normed[...], full[:, start : start + TILE]).astype(bf16)


def fixed(shape):
    return pl.BlockSpec(shape, lambda i, *o: (0,) * len(shape), pipeline_mode=pl.Buffered(1))


def kept(shape):
    return pl.BlockSpec(shape, lambda i, *o: (0,) * len(shape))


def rows_of(cols, group=0):
    return pl.BlockSpec((Q, cols), lambda i, *o: (i, group))


def shape_of(shape, dtype=f32):
    return jax.ShapeDtypeStruct(shape, dtype)


def cost(flops, megabytes):
    return pl.CostEstimate(flops=int(flops) // 50, bytes_accessed=int(megabytes * 2**20) // 50, transcendentals=0)


def project(order, tokens, edge, gain, pieces):
    length, width = tokens.shape
    rows = pieces[0].shape[0]
    return pl.pallas_call(
        project_kernel,
        grid_spec=pltpu.PrefetchScalarGridSpec(
            num_scalar_prefetch=1,
            grid=(length // Q,),
            in_specs=[rows_of(width), fixed((EDGE, width)), fixed((1, width))] + [fixed((rows, GW + REST))] * 4,
            out_specs=[rows_of(width), rows_of(GW), rows_of(REST), kept((EDGE, GW)), kept((EDGE, REST))],
            scratch_shapes=[pltpu.VMEM((4 * rows, GW + REST), bf16)],
        ),
        out_shape=[
            shape_of((length, width), bf16),
            shape_of((length, GW), bf16),
            shape_of((length, REST), bf16),
            shape_of((EDGE, GW), bf16),
            shape_of((EDGE, REST), bf16),
        ],
        compiler_params=cparams(),
        cost_estimate=cost(2 * length * width * (GW + REST), 9),
        name="project",
    )(order, tokens, edge, gain, *pieces)


def project_more(order, normed, edge, gain, pieces):
    length, width = normed.shape
    rows = pieces[0].shape[0]
    return pl.pallas_call(
        project_more_kernel,
        grid_spec=pltpu.PrefetchScalarGridSpec(
            num_scalar_prefetch=1,
            grid=(length // Q,),
            in_specs=[rows_of(width), fixed((EDGE, width)), fixed((1, width))] + [fixed((rows, GW))] * 4,
            out_specs=[rows_of(GW), kept((EDGE, GW))],
            scratch_shapes=[pltpu.VMEM((4 * rows, GW), bf16)],
        ),
        out_shape=[shape_of((length, GW), bf16), shape_of((EDGE, GW), bf16)],
        compiler_params=cparams(),
        cost_estimate=cost(2 * length * width * GW, 6),
        name="project_more",
    )(order, normed, edge, gain, *pieces)


def gate_kernel(order, normed, w0, w1, w2, w3, out, full):
    @pl.when(pl.program_id(0) == 0)
    def _():
        assemble(order, (w0, w1, w2, w3), full)

    for j in range(TILES):
        cols = slice(j * TILE, (j + 1) * TILE)
        out[:, cols] = dot(normed[...], full[:, cols]).astype(bf16)


def gate_project(order, normed, pieces):
    length, width = normed.shape
    rows = pieces[0].shape[0]
    return pl.pallas_call(
        gate_kernel,
        grid_spec=pltpu.PrefetchScalarGridSpec(
            num_scalar_prefetch=1,
            grid=(length // Q,),
            in_specs=[rows_of(width)] + [fixed((rows, INNER))] * 4,
            out_specs=rows_of(INNER),
            scratch_shapes=[pltpu.VMEM((4 * rows, INNER), bf16)],
        ),
        out_shape=shape_of((length, INNER), bf16),
        compiler_params=cparams(),
        cost_estimate=cost(2 * length * width * INNER, 10),
        name="gate_project",
    )(order, normed, *pieces)


def factors_kernel(now, prior, edge, taps_bc, bias_bc, heads, bc_act, aux_out, cum_t):
    first = pl.program_id(0) == 0
    early = jnp.where(first, edge[:, :BC], prior[:, :BC]).astype(f32)
    pre = conv_of(shifted(now[:, :BC].astype(f32), early), taps_bc[...], bias_bc[...])
    bc_act[...] = pre * sigmoid(pre)
    raw = now[:, BC : BC + HEADS].astype(f32) + heads[2:3, :HEADS]
    step = jnp.maximum(raw, 0.0) + jnp.log1p(jnp.exp(-jnp.abs(raw)))
    decay = -jnp.exp(heads[0:1, :HEADS]) * step
    lower = jnp.where(row_iota(Q, Q) >= lane_iota(Q, Q), 1.0, 0.0)
    cumulative = jnp.dot(lower, decay, precision=highest, preferred_element_type=f32)
    last = cumulative[Q - 1 : Q]
    aux = jnp.concatenate([cumulative, step, jnp.exp(last - cumulative), jnp.exp(cumulative)], axis=1)
    aux_out[...] = aux
    cum_t[...] = aux.T[:HEADS]


def states_kernel(
    group, now, prior, edge, taps, bias, bc_act, aux, x_act, local, payload, run, total, b_rows
):
    c = pl.program_id(0)
    first = c == 0

    @pl.when(first)
    def _():
        run[...] = jnp.zeros_like(run)
        total[...] = jnp.zeros_like(total)

    b_rows[...] = bc_act[:, :STATE].T
    weight2 = terms2(aux[:, HEADS : 2 * HEADS] * aux[:, 2 * HEADS : 3 * HEADS])
    ends4 = terms4(jnp.concatenate([aux[Q - 8 :, 3 * HEADS :], aux[Q - 8 :, :HEADS]], axis=0))

    def body(j, carry):
        cols = tile_at(j)
        early = jnp.where(first, edge[:, cols], prior[:, cols]).astype(f32)
        pre = conv_of(shifted(now[:, cols].astype(f32), early), taps[:, cols], bias[:, cols])
        x = pre * sigmoid(pre)
        x_act[:, cols] = x
        lead = 4 * (j + group * GT)
        state = fine(dot, b_rows[...], x * dot(weight2, spread(2, TILE, lead, 6)))
        local[0, j] = state
        end = dot(ends4, spread(4, TILE, lead, 6))
        run[j] = end[7:8] * run[j] + state
        total[:, cols] += end[15:16]
        return carry

    lax.fori_loop(0, GT, body, 0, unroll=GT)

    @pl.when(c == pl.num_programs(0) - 1)
    def _():
        for j in range(2 * GT):
            lanes = slice(128 * (j % 2), 128 * (j % 2) + 128)
            payload[j, :STATE, :] = run[j // 2, :, lanes]
            payload[j, STATE:, :] = jnp.broadcast_to(total[:, j * 128 : (j + 1) * 128], (8, 128))


def prior_rows(cols, group=0):
    per = Q // EDGE
    return pl.BlockSpec((EDGE, cols), lambda i, *o: (jnp.maximum(i * per - 1, 0), group))


def at_group(rows, group):
    return pl.BlockSpec((rows, GW), lambda i, *o: (0, group), pipeline_mode=pl.Buffered(1))


def factors(rest, rest_edge, taps_bc, bias_bc, heads):
    length = rest.shape[0]
    return pl.pallas_call(
        factors_kernel,
        grid=(length // Q,),
        in_specs=[
            rows_of(REST), prior_rows(REST), fixed((EDGE, REST)),
            fixed((TAPS, BC)), fixed((1, BC)), fixed((8, 128)),
        ],
        out_specs=[rows_of(BC), rows_of(128), pl.BlockSpec((HEADS, Q), lambda i: (0, i))],
        out_shape=[shape_of((length, BC)), shape_of((length, 128)), shape_of((HEADS, length))],
        compiler_params=cparams(),
        cost_estimate=cost(10**9, 4),
        name="factors",
    )(rest, rest, rest_edge, taps_bc, bias_bc, heads)


def states(group, proj, proj_edge, taps, bias, bc_act, aux):
    length = proj.shape[0]
    chunks = length // Q
    return pl.pallas_call(
        functools.partial(states_kernel, group),
        grid=(chunks,),
        in_specs=[
            rows_of(GW), prior_rows(GW), fixed((EDGE, GW)),
            at_group(TAPS, group), at_group(1, group), rows_of(BC), rows_of(128),
        ],
        out_specs=[
            rows_of(GW),
            pl.BlockSpec((1, GT, STATE, TILE), lambda i: (i, 0, 0, 0)),
            kept((2 * GT, STATE + 8, 128)),
        ],
        out_shape=[
            shape_of((length, GW)),
            shape_of((chunks, GT, STATE, TILE)),
            shape_of((2 * GT, STATE + 8, 128)),
        ],
        scratch_shapes=[
            pltpu.VMEM((GT, STATE, TILE), f32),
            pltpu.VMEM((1, GW), f32),
            pltpu.VMEM((STATE, Q), f32),
        ],
        compiler_params=cparams(),
        cost_estimate=cost(10**10, 10),
        name="states",
    )(proj, proj, proj_edge, taps, bias, bc_act, aux)


def chain_kernel(forward, values, totals, out):
    count = out.shape[0]
    order = range(count) if forward else range(count - 1, -1, -1)
    state = jnp.zeros(out.shape[1:], f32)
    for i in order:
        out[i] = state
        state = jnp.exp(totals[i, 0:1, :]) * state + values[i, :STATE, :]


def chain(forward, values, totals):
    count, _, width = values.shape
    return pl.pallas_call(
        functools.partial(chain_kernel, forward),
        out_shape=jax.ShapeDtypeStruct((count, STATE, width), f32),
        compiler_params=pltpu.CompilerParams(vmem_limit_bytes=56 * 2**20),
        cost_estimate=cost(10**8, 3),
        name="chain",
    )(values, totals)


def within_kernel(group, x_act, bc_act, aux, cum_t, skip, out, scores, columns):
    lower = row_iota(HALF, HALF) >= lane_iota(HALF, HALF)
    for b in range(2):
        rows = slice(b * HALF, (b + 1) * HALF)
        scores[rows, :] = jnp.where(lower, fine(dot_lanes, bc_act[rows, STATE:], bc_act[rows, :STATE]), 0.0)
    cross_high, cross_low = halves(fine(dot_lanes, bc_act[HALF:, STATE:], bc_act[:HALF, :STATE]))
    cross2 = jnp.concatenate([cross_high, cross_low], axis=1)
    cumulative = aux[:, :HEADS]
    middle_row = cumulative[HALF - 1 : HALF]
    step2 = terms2(aux[:, HEADS : 2 * HEADS])
    bridge2 = terms2(jnp.exp(jnp.concatenate([middle_row - cumulative[:HALF], cumulative[HALF:] - middle_row], axis=0)))
    cumulative4 = terms4(cumulative)
    for j in range(GT):
        columns[:, j * 512 : (j + 1) * 512] = dot(cumulative4, spread(4, 512, 4 * (j + group * GT), 7))
    low = lane_iota(HALF, HALF) < 64

    def body(j, carry):
        cols = tile_at(j)
        x = x_act[:, cols]
        select = spread(2, TILE, 4 * (j + group * GT), 6)
        u = x * dot(step2, select)
        bridge = dot(bridge2, select)
        u_high, u_low = halves(u)
        v_high, v_low = halves(u[:HALF] * bridge[:HALF])
        across = dot(cross2, jnp.concatenate([v_high, v_high], axis=0)) + dot(cross_high, v_low)
        across = across * bridge[HALF:]
        direct = skip[:, cols] * x
        for pair in range(2):
            lanes = slice(pair * 128, (pair + 1) * 128)
            place = pl.ds(pl.multiple_of(j * TILE + pair * 128, 128), 128)
            for b in range(2):
                rows = slice(b * HALF, (b + 1) * HALF)
                weights = []
                for i in range(2):
                    head = 4 * j + 2 * pair + i
                    column = columns[rows, pl.ds(pl.multiple_of(head * 128, 128), 128)]
                    row = cum_t[pl.ds(head + 4 * GT * group, 1), :][:, rows]
                    weights.append(jnp.exp(jnp.minimum(column - row, 0.0)) * scores[rows, :])
                w_high, w_low = halves(jnp.concatenate(weights, axis=1))
                top = both_heads(low, u_high[rows, lanes])
                bottom = both_heads(low, u_low[rows, lanes])
                twice = dot(w_high, jnp.concatenate([top, bottom], axis=1))
                y = twice[:, :128] + twice[:, 128:] + dot(w_low, top) + direct[rows, lanes]
                if b == 1:
                    y = y + across[:, lanes]
                out[rows, place] = y
        return carry

    lax.fori_loop(0, GT, body, 0, unroll=GT)


def both_heads(low, value):
    zero = jnp.zeros_like(value)
    return jnp.concatenate([jnp.where(low, value, zero), jnp.where(low, zero, value)], axis=0)


def within(group, x_act, bc_act, aux, cum_t, skip):
    length = x_act.shape[0]
    return pl.pallas_call(
        functools.partial(within_kernel, group),
        grid=(length // Q,),
        in_specs=[
            rows_of(GW), rows_of(BC), rows_of(128),
            pl.BlockSpec((HEADS, Q), lambda i: (0, i)), at_group(1, group),
        ],
        out_specs=rows_of(GW),
        out_shape=shape_of((length, GW)),
        scratch_shapes=[pltpu.VMEM((Q, HALF), f32), pltpu.VMEM((Q, GT * 512), f32)],
        compiler_params=cparams(),
        cost_estimate=cost(10**10, 10),
        name="within",
    )(x_act, bc_act, aux, cum_t, skip)


def within_back_kernel(
    group, x_act, bc_act, aux, cum_t, dy, now, prior, edge, taps, bias, ends, entering,
    out, slope, out_bc, k_dot, scores, grad_scores, grad_cross, columns,
):
    first = pl.program_id(0) == 0
    k_dot[...] = jnp.zeros_like(k_dot)
    out_bc[:, STATE:] = jnp.zeros((Q, STATE), f32)
    upper = row_iota(HALF, HALF) <= lane_iota(HALF, HALF)
    act = bc_act[...].astype(bf16)
    b_act, c_act = act[:, :STATE], act[:, STATE:]
    for b in range(2):
        rows = slice(b * HALF, (b + 1) * HALF)
        scores[rows, :] = jnp.where(upper, dot_lanes(b_act[rows], c_act[rows]), 0.0)
    grad_scores[...] = jnp.zeros_like(grad_scores)
    grad_cross[...] = jnp.zeros_like(grad_cross)
    cross = dot_lanes(b_act[:HALF], c_act[HALF:]).astype(bf16)
    cumulative = aux[:, :HEADS]
    middle_row = cumulative[HALF - 1 : HALF]
    step2 = terms2(aux[:, HEADS : 2 * HEADS])
    decayed2 = terms2(aux[:, 3 * HEADS :])
    bridge2 = terms2(jnp.exp(jnp.concatenate([middle_row - cumulative[:HALF], cumulative[HALF:] - middle_row], axis=0)))
    cumulative4 = terms4(cumulative)
    for j in range(GT):
        columns[:, j * 512 : (j + 1) * 512] = dot(cumulative4, spread(4, 512, 4 * (j + group * GT), 7))
    low = lane_iota(HALF, HALF) < 64

    def body(j, carry):
        cols = tile_at(j)
        lead = 4 * (j + group * GT)
        select = spread(2, TILE, lead, 6)
        x = x_act[:, cols]
        u = x * dot(step2, select)
        bridge = dot(bridge2, select)
        u_low = u.astype(bf16)
        grad = dy[:, cols]
        wide = grad.astype(f32)
        early_raw = jnp.where(first, edge[:, cols], prior[:, cols]).astype(f32)
        pre = conv_of(shifted(now[:, cols].astype(f32), early_raw), taps[:, cols], bias[:, cols])
        sig = sigmoid(pre)
        slope[:, cols] = (sig + x * (1.0 - sig)).astype(bf16)
        k_dot[...] += split_dot(x * wide, head_select(j + group * GT))
        enter = jnp.where(first, entering[j], ends[0, j])
        out_bc[:, STATE:] += fine(dot_lanes, wide * dot(decayed2, select), enter)
        early = (u[:HALF] * bridge[:HALF]).astype(bf16)
        late = (grad[HALF:].astype(f32) * bridge[HALF:]).astype(bf16)
        grad_cross[...] += dot_lanes(early, late)
        across = dot(cross, late) * bridge[:HALF]
        totals = [None, None]
        for pair in range(2):
            lanes = slice(pair * 128, (pair + 1) * 128)
            place = pl.ds(pl.multiple_of(j * TILE + pair * 128, 128), 128)
            for b in range(2):
                rows = slice(b * HALF, (b + 1) * HALF)
                spaced = both_heads(low, grad[rows, lanes])
                products = dot_lanes(u_low[rows, lanes], spaced)
                weights = []
                for i in range(2):
                    head = 4 * j + 2 * pair + i
                    column = columns[rows, pl.ds(pl.multiple_of(head * 128, 128), 128)]
                    row = cum_t[pl.ds(head + 4 * GT * group, 1), :][:, rows]
                    weight = jnp.exp(jnp.minimum(row - column, 0.0))
                    part = weight * products[:, i * 128 : (i + 1) * 128]
                    totals[b] = part if totals[b] is None else totals[b] + part
                    weights.append((weight * scores[rows, :]).astype(bf16))
                du = dot(jnp.concatenate(weights, axis=1), spaced)
                if b == 0:
                    du = du + across[:, lanes]
                out[rows, place] = du.astype(bf16)
        for b in range(2):
            grad_scores[b * HALF : (b + 1) * HALF, :] += totals[b]
        return carry

    lax.fori_loop(0, GT, body, 0, unroll=GT)
    far = grad_cross[...].astype(bf16)
    near0 = jnp.where(upper, grad_scores[:HALF, :], 0.0).astype(bf16)
    near1 = jnp.where(upper, grad_scores[HALF:, :], 0.0).astype(bf16)
    out_bc[:HALF, :STATE] = dot(near0, c_act[:HALF]) + dot(far, c_act[HALF:])
    out_bc[HALF:, :STATE] = dot(near1, c_act[HALF:])
    out_bc[:HALF, STATE:] += dot_rows(near0, b_act[:HALF])
    out_bc[HALF:, STATE:] += dot_rows(near1, b_act[HALF:]) + dot_rows(far, b_act[:HALF])


def within_back(group, x_act, bc_act, aux, cum_t, dy, proj, proj_edge, taps, bias, ends, entering):
    length = x_act.shape[0]
    return pl.pallas_call(
        functools.partial(within_back_kernel, group),
        grid=(length // Q,),
        in_specs=[
            rows_of(GW), rows_of(BC), rows_of(128),
            pl.BlockSpec((HEADS, Q), lambda i: (0, i)), rows_of(GW, group),
            rows_of(GW), prior_rows(GW), fixed((EDGE, GW)),
            at_group(TAPS, group), at_group(1, group),
            pl.BlockSpec((1, GT, STATE, TILE), lambda i: (jnp.maximum(i - 1, 0), group, 0, 0)),
            pl.BlockSpec((GT, STATE, TILE), lambda i: (group, 0, 0), pipeline_mode=pl.Buffered(1)),
        ],
        out_specs=[rows_of(GW), rows_of(GW), rows_of(BC), rows_of(128)],
        out_shape=[
            shape_of((length, GW), bf16), shape_of((length, GW), bf16),
            shape_of((length, BC)), shape_of((length, 128)),
        ],
        scratch_shapes=[
            pltpu.VMEM((Q, HALF), f32),
            pltpu.VMEM((Q, HALF), f32),
            pltpu.VMEM((HALF, HALF), f32),
            pltpu.VMEM((Q, GT * 512), f32),
        ],
        compiler_params=cparams(),
        cost_estimate=cost(2 * 10**10, 14),
        name="within_back",
    )(x_act, bc_act, aux, cum_t, dy, proj, proj, proj_edge, taps, bias, ends, entering)


def middle_kernel(
    order, y_in0, y_in1, bc_act, aux, local0, local1, entering0, entering1, gate, tokens, cot, gain, w0, w1, w2, w3,
    normed_out, output, dy_out, grad_gate, ends, back_states, begin, payload, y_dot, gain_grad,
    full, state, back, before, y_keep, gated_keep, grad_keep,
):
    c = pl.program_id(0)

    @pl.when(c == 0)
    def _():
        assemble(order, (w0, w1, w2, w3), full)
        for g, entering in enumerate((entering0, entering1)):
            for j in range(GT):
                state[g * GT + j, :, :128] = entering[2 * j]
                state[g * GT + j, :, 128:] = entering[2 * j + 1]
        begin[...] = state[...]
        back[...] = jnp.zeros_like(back)
        before[...] = jnp.zeros_like(before)
        gain_grad[...] = jnp.zeros_like(gain_grad)

    keep = aux[...]
    c_cols = bc_act[:, STATE:]
    c_rows = bc_act[:, STATE:].T

    decayed2 = terms2(keep[:, 3 * HEADS :])
    ends4 = terms4(jnp.concatenate([keep[Q - 8 :, 3 * HEADS :], keep[Q - 8 :, :HEADS]], axis=0))

    def mix(y_in, local, shift, place, squares):
        j = place + shift
        cols = tile_at(j)
        carried = fine(dot, c_cols, state[j])
        y = y_in[:, tile_at(place)] + dot(decayed2, spread(2, TILE, 4 * j, 6)) * carried
        y_keep[:, cols] = y
        raw = gate[:, cols].astype(f32)
        gated = y.astype(bf16).astype(f32) * (raw * sigmoid(raw))
        gated_keep[:, cols] = gated
        moved = dot(ends4, spread(4, TILE, 4 * j, 6))[7:8] * state[j] + local[0, place]
        state[j] = moved
        ends[0, j] = moved
        both = gated * gated
        return squares + (both[:, :128] + both[:, 128:])

    squares = jnp.zeros((Q, 128), f32)
    for g, (y_in, local) in enumerate(((y_in0, local0), (y_in1, local1))):
        squares = lax.fori_loop(0, GT, functools.partial(mix, y_in, local, g * GT), squares, unroll=GT)
    scale = lax.rsqrt(jnp.sum(squares, axis=1, keepdims=True) / INNER + EPS)

    def back_out(j, products):
        cols = tile_at(j)
        gated = gated_keep[:, cols]
        gains = gain[:, cols]
        normed_out[:, cols] = (gated * scale * gains).astype(bf16)
        grad = dot_lanes(cot[...], full[cols, :])
        grad_keep[:, cols] = grad
        gain_grad[:, cols] += jnp.sum(grad * gated * scale, axis=0, keepdims=True)
        both = grad * gains * gated
        return products + (both[:, :128] + both[:, 128:])

    products = lax.fori_loop(0, TILES, back_out, jnp.zeros((Q, 128), f32), unroll=4)
    shared = jnp.sum(products, axis=1, keepdims=True) / INNER * (scale * scale * scale)
    for start in range(0, output.shape[1], TILE):
        cols = slice(start, start + TILE)
        branch = dot(normed_out[...], full[:, cols])
        output[:, cols] = (tokens[:, cols].astype(f32) + branch).astype(bf16)

    def finish(j, y_sum):
        cols = tile_at(j)
        raw = gate[:, cols].astype(f32)
        sig = sigmoid(raw)
        grad_gated = scale * (grad_keep[:, cols] * gain[:, cols]) - gated_keep[:, cols] * shared
        y = y_keep[:, cols]
        dy = (grad_gated * (raw * sig)).astype(bf16)
        dy_out[:, cols] = dy
        mixed = y.astype(bf16).astype(f32)
        grad_gate[:, cols] = (grad_gated * mixed * (sig * (1.0 + raw * (1.0 - sig)))).astype(bf16)
        wide = dy.astype(f32)
        piece = fine(dot, c_rows, wide * dot(decayed2, spread(2, TILE, 4 * j, 6)))
        back_states[0, j] = piece
        back[j] += jnp.exp(before[:, cols]) * piece
        before[:, cols] += dot(ends4, spread(4, TILE, 4 * j, 6))[15:16]
        return y_sum + split_dot(wide * y, head_select(j))

    y_dot[...] = lax.fori_loop(0, TILES, finish, jnp.zeros((Q, 128), f32), unroll=4)

    @pl.when(c == pl.num_programs(0) - 1)
    def _():
        for g in range(GROUPS):
            for j in range(GT):
                payload[2 * j, :, g * 128 : (g + 1) * 128] = back[g * GT + j, :, :128]
                payload[2 * j + 1, :, g * 128 : (g + 1) * 128] = back[g * GT + j, :, 128:]


def middle(order, y_in, bc_act, aux, local, entering, gate, tokens, cot, gain, pieces):
    length, width = tokens.shape
    rows = pieces[0].shape[0]
    chunks = length // Q
    per_group = pl.BlockSpec((1, GT, STATE, TILE), lambda i, o: (i, 0, 0, 0))
    per_chunk = pl.BlockSpec((1, TILES, STATE, TILE), lambda i, o: (i, 0, 0, 0))
    return pl.pallas_call(
        middle_kernel,
        grid_spec=pltpu.PrefetchScalarGridSpec(
            num_scalar_prefetch=1,
            grid=(chunks,),
            in_specs=[rows_of(GW)] * 2
            + [rows_of(BC), rows_of(128)]
            + [per_group] * 2
            + [fixed((2 * GT, STATE, 128))] * 2
            + [rows_of(INNER), rows_of(width), rows_of(width), fixed((1, INNER))]
            + [fixed((rows, width))] * 4,
            out_specs=[
                rows_of(INNER), rows_of(width), rows_of(INNER), rows_of(INNER), per_chunk, per_chunk,
                kept((TILES, STATE, TILE)), kept((PIECES, STATE, TILE)), rows_of(128), kept((1, INNER)),
            ],
            scratch_shapes=[
                pltpu.VMEM((4 * rows, width), bf16),
                pltpu.VMEM((TILES, STATE, TILE), f32),
                pltpu.VMEM((TILES, STATE, TILE), f32),
                pltpu.VMEM((1, INNER), f32),
                pltpu.VMEM((Q, INNER), f32),
                pltpu.VMEM((Q, INNER), f32),
                pltpu.VMEM((Q, INNER), f32),
            ],
        ),
        out_shape=[
            shape_of((length, INNER), bf16),
            shape_of((length, width), bf16),
            shape_of((length, INNER), bf16),
            shape_of((length, INNER), bf16),
            shape_of((chunks, TILES, STATE, TILE)),
            shape_of((chunks, TILES, STATE, TILE)),
            shape_of((TILES, STATE, TILE)),
            shape_of((PIECES, STATE, TILE)),
            shape_of((length, 128)),
            shape_of((1, INNER)),
        ],
        compiler_params=cparams(),
        cost_estimate=cost(4 * 10**10, 40),
        name="middle",
    )(order, *y_in, bc_act, aux, *local, *entering, gate, tokens, cot, gain, *pieces)


def back_kernel(
    group, now, edge, taps, skip, dy, du_in, slope, x_act, bc_act, aux, ends, back_states, leaving, *others
):
    last_group = group == GROUPS - 1
    if last_group:
        (rest, rest_prior, rest_edge, taps_bc, bias_bc, heads, y_dot,
         k_dot0, k_dot1, x_before, edge_before, b_before, bc_in0, bc_in1,
         grad, grad_taps, tail, start, grad_taps_bc, grad_heads,
         later, after, x_dot, edge_dot, b_sum) = others
    else:
        (grad, grad_taps, tail, start, x_dot, edge_dot, b_sum, later, after) = others
    step_id = pl.program_id(0)
    first = step_id == pl.num_programs(0) - 1

    @pl.when(step_id == 0)
    def _():
        for j in range(GT):
            later[j, :, :128] = leaving[2 * j, :, group * 128 : (group + 1) * 128]
            later[j, :, 128:] = leaving[2 * j + 1, :, group * 128 : (group + 1) * 128]
        after[...] = jnp.zeros_like(after)
        grad_taps[...] = jnp.zeros_like(grad_taps)
        if last_group:
            grad_taps_bc[...] = jnp.zeros_like(grad_taps_bc)
            grad_heads[...] = jnp.zeros_like(grad_heads)

    keep = aux[...]
    b_act = bc_act[:, :STATE].astype(bf16)
    factors2 = terms2(
        jnp.concatenate([keep[:, HEADS * k : HEADS * (k + 1)] for k in range(1, 3)], axis=0)
    )
    ends4 = terms4(keep[Q - 8 :, 3 * HEADS :])
    x_dot[...] = jnp.zeros_like(x_dot)
    edge_dot[...] = jnp.zeros_like(edge_dot)
    b_sum[...] = jnp.zeros_like(b_sum)

    def through(cols, dv, raw, early, tap_values):
        parts = later_rows(dv, after[:, cols])
        result = conv_of(parts, tap_values, 0.0)
        after[:, cols] = dv[:8]
        grad[:, cols] = result.astype(bf16)

        @pl.when(step_id == 0)
        def _():
            tail[:, cols] = result[Q - EDGE :]

        early = jnp.where(first, early[EDGE - 8 :].astype(f32), 0.0)
        return tap_sums(parts, raw, dv, early)

    def body(j, carry):
        cols = tile_at(j)
        select = spread(2, TILE, 4 * (j + group * GT), 6)
        heads_of = head_select(j + group * GT)
        factors = dot(factors2, select)
        step, tail_decay = factors[:Q], factors[Q:]
        x = x_act[:, cols]
        later_state = later[j]
        du = du_in[:, cols].astype(f32) + tail_decay * dot(b_act, later_state.astype(bf16))
        x_dot[...] += split_dot(x * du, heads_of)
        b_sum[...] += fine(dot_lanes, x * step * tail_decay, later_state)
        meet = jnp.sum(ends[0, j] * later_state, axis=0, keepdims=True)
        edge_dot[...] += split_dot(jnp.broadcast_to(meet, (8, TILE)), heads_of)
        later[j] = dot(ends4, spread(4, TILE, 4 * (j + group * GT), 6))[7:8] * later_state + back_states[0, j]
        dv = (step * du + skip[:, cols] * dy[:, cols].astype(f32)) * slope[:, cols].astype(f32)
        grad_taps[:, cols] += through(cols, dv, now[:, cols].astype(f32), edge[:, cols], taps[:, cols])
        return carry

    lax.fori_loop(0, GT, body, 0, unroll=2)

    if last_group:
        band = slice(GW, GW + BC)
        current = rest[:, :BC].astype(f32)
        early = jnp.where(first, rest_edge[:, :BC], rest_prior[:, :BC])
        pre = conv_of(shifted(current, early.astype(f32)), taps_bc[...], bias_bc[...])
        sig = sigmoid(pre)
        grad_act = bc_in0[...] + bc_in1[...]
        grad_act = grad_act + jnp.concatenate([b_sum[...] + b_before[...], jnp.zeros((Q, STATE), f32)], axis=1)
        dv = grad_act * (sig * (1.0 + pre * (1.0 - sig)))
        grad_taps_bc[...] += through(band, dv, current, rest_edge[:, :BC], taps_bc[...])

        step = keep[:, HEADS : 2 * HEADS]
        by_step = x_dot[:, :HEADS] + x_before[:, :HEADS]
        by_skip = k_dot0[:, :HEADS] + k_dot1[:, :HEADS]
        rate = -jnp.exp(heads[0:1, :HEADS])
        by_sum = y_dot[:, :HEADS] - heads[1:2, :HEADS] * by_skip - step * by_step
        upper = jnp.where(row_iota(Q, Q) <= lane_iota(Q, Q), 1.0, 0.0)
        by_decay = jnp.dot(upper, by_sum, precision=highest, preferred_element_type=f32)
        by_decay = by_decay + (edge_dot[0:1, :HEADS] + edge_before[0:1, :HEADS])
        raw = rest[:, BC : BC + HEADS].astype(f32) + heads[2:3, :HEADS]
        grad_dt = (by_step + by_decay * rate) * sigmoid(raw)
        full_dt = jnp.concatenate([grad_dt, jnp.zeros((Q, 128 - HEADS), f32)], axis=1)
        grad[:, GW + BC :] = full_dt.astype(bf16)
        sums = [
            jnp.sum(by_decay * (rate * step), axis=0, keepdims=True),
            jnp.sum(by_skip, axis=0, keepdims=True),
            jnp.sum(grad_dt, axis=0, keepdims=True),
            jnp.zeros((5, HEADS), f32),
        ]
        grad_heads[:, :HEADS] += jnp.concatenate(sums, axis=0)

    @pl.when(first)
    def _():
        start[...] = after[...]


def backward(group, proj, proj_edge, taps, skip, dy, du, slope, x_act, bc_act, aux, ends, back_states, leaving, others=()):
    length = proj.shape[0]
    chunks = length // Q
    per = Q // EDGE
    last_group = group == GROUPS - 1
    at = lambda i: chunks - 1 - i
    block = lambda cols, g=0: pl.BlockSpec((Q, cols), lambda i: (at(i), g))
    per_chunk = pl.BlockSpec((1, GT, STATE, TILE), lambda i: (at(i), group, 0, 0))
    dots = pl.BlockSpec((8, 128), lambda i: (at(i), 0))
    in_specs = [
        block(GW), fixed((EDGE, GW)), at_group(TAPS, group), at_group(1, group),
        block(GW, group), block(GW), block(GW), block(GW), block(BC), block(128),
        per_chunk, per_chunk, fixed((PIECES, STATE, TILE)),
    ]
    width = GW + BC if last_group else GW
    cols = GW + REST if last_group else GW
    out_specs = [block(cols), kept((8, GW)), kept((EDGE, width)), kept((8, width))]
    out_shape = [
        shape_of((length, cols), bf16), shape_of((8, GW)), shape_of((EDGE, width)), shape_of((8, width)),
    ]
    scratch = [pltpu.VMEM((GT, STATE, TILE), f32), pltpu.VMEM((8, width), f32)]
    if last_group:
        in_specs += [
            block(REST),
            pl.BlockSpec((EDGE, REST), lambda i: (jnp.maximum(at(i) * per - 1, 0), 0)),
            fixed((EDGE, REST)), fixed((TAPS, BC)), fixed((1, BC)), fixed((8, 128)),
            block(128), block(128), block(128), block(128), dots, block(STATE), block(BC), block(BC),
        ]
        out_specs += [kept((8, BC)), kept((8, 128))]
        out_shape += [shape_of((8, BC)), shape_of((8, 128))]
        scratch += [pltpu.VMEM((Q, 128), f32), pltpu.VMEM((8, 128), f32), pltpu.VMEM((Q, STATE), f32)]
    else:
        out_specs += [block(128), dots, block(STATE)]
        out_shape += [shape_of((length, 128)), shape_of((8 * chunks, 128)), shape_of((length, STATE))]
    return pl.pallas_call(
        functools.partial(back_kernel, group),
        grid=(chunks,),
        in_specs=in_specs,
        out_specs=out_specs,
        out_shape=out_shape,
        scratch_shapes=scratch,
        compiler_params=cparams(),
        cost_estimate=cost(2 * 10**10, 20),
        name="backward",
    )(proj, proj_edge, taps, skip, dy, du, slope, x_act, bc_act, aux, ends, back_states, leaving, *others)


def quarters(left, order):
    rows = left.shape[1] // 4
    block = [lax.dynamic_slice_in_dim(left, order[k] * rows, rows, axis=1) for k in range(4)]
    return jnp.concatenate([block[1], block[3]], axis=1), jnp.concatenate([block[0], block[2]], axis=1)


def weight_grad(parts, right):
    sent, held = parts
    return dot_rows(right, sent).astype(bf16), dot_rows(right, held)


def out_weight_sums(parts, right):
    sent, held = parts
    return dot_rows(sent, right).astype(bf16), dot_rows(held, right)


def input_kernel(
    order, grad_gate, grad_x0, grad_x1, tokens, cot, gain,
    g0, g1, g2, g3, a0, a1, a2, a3, b0, b1, b2, b3, out, gain_grad,
):
    rows = g0.shape[0]

    @pl.when(pl.program_id(0) == 0)
    def _():
        gain_grad[...] = jnp.zeros_like(gain_grad)

    for k, (gate_w, a_w, b_w) in enumerate(((g0, a0, b0), (g1, a1, b1), (g2, a2, b2), (g3, a3, b3))):
        cols = pl.ds(pl.multiple_of(order[k] * rows, rows), rows)
        total = dot_lanes(grad_gate[...], gate_w[...]) + dot_lanes(grad_x0[...], a_w[:, :GW])
        total = total + dot_lanes(grad_x1[:, :GW], b_w[...])
        out[:, cols] = total + dot_lanes(grad_x1[:, GW:], a_w[:, GW:])
    grad = out[...]
    wide = tokens[...].astype(f32)
    width = wide.shape[1]
    scale = lax.rsqrt(jnp.mean(wide * wide, axis=1, keepdims=True) + EPS)
    gain_grad[...] += jnp.sum(grad * wide * scale, axis=0, keepdims=True)
    scaled = grad * gain[...]
    shared = jnp.sum(scaled * wide, axis=1, keepdims=True) / width
    out[...] = cot[...].astype(f32) + (scale * scaled - wide * (scale * scale * scale * shared))


def input_back(order, grad_gate, grad_x0, grad_x1, tokens, cot, gain, gate_pieces, a_pieces, b_pieces):
    length, width = tokens.shape
    rows = width // 4
    return pl.pallas_call(
        input_kernel,
        grid_spec=pltpu.PrefetchScalarGridSpec(
            num_scalar_prefetch=1,
            grid=(length // Q,),
            in_specs=[rows_of(INNER), rows_of(GW), rows_of(GW + REST), rows_of(width), rows_of(width), fixed((1, width))]
            + [fixed((rows, INNER))] * 4
            + [fixed((rows, GW + REST))] * 4
            + [fixed((rows, GW))] * 4,
            out_specs=[rows_of(width), kept((1, width))],
        ),
        out_shape=[shape_of((length, width)), shape_of((1, width))],
        compiler_params=cparams(),
        cost_estimate=cost(2 * length * width * (INNER + XCOLS), 26),
        name="input_back",
    )(order, grad_gate, grad_x0, grad_x1, tokens, cot, gain, *gate_pieces, *a_pieces, *b_pieces)


def swap(value, axis, bit):
    count = lax.axis_size(axis)
    return lax.ppermute(value, axis, [(i, i ^ bit) for i in range(count)])


def exchange(value, axis):
    return lax.all_to_all(value, axis, split_axis=0, concat_axis=0, tiled=True)


def tie(value, *others):
    return lax.optimization_barrier((value, others))[0]


def to_owners(value, groups=1):
    count = lax.axis_size("seq")
    pieces, rows, lanes = value.shape
    if count != pieces:
        lanes //= groups
        width = pieces * lanes // count
        split = value.reshape(pieces, rows, groups, lanes // width, width)
        value = split.transpose(0, 3, 1, 2, 4).reshape(count, rows, groups * width)
    return exchange(value, "seq")


def from_owners(value, groups=1, pieces=PIECES, lanes=128):
    value = exchange(value, "seq")
    count, rows, width = value.shape
    if count == pieces:
        return value
    width //= groups
    split = value.reshape(pieces, lanes // width, rows, groups, width)
    return split.transpose(0, 2, 3, 1, 4).reshape(pieces, rows, groups * lanes)


def send_core(grads):
    sent, held = grads
    return held, swap(sent, "wshard", 1)


def send_x(state, axis=1):
    held, got = state
    own, other = jnp.split(held, 2, axis=axis)
    got_own, got_other = jnp.split(got, 2, axis=axis)
    return (
        own + got_own.astype(f32),
        swap((other + got_other.astype(f32)).astype(bf16), "wshard", 2),
    )


def sum_pair(state):
    mine, got = state
    return (mine + got.astype(f32)).astype(bf16)


def send_near(state):
    mine, got = state
    total = mine + got.astype(f32)
    half = total.shape[0] // 2
    bit = lax.axis_index("seq") & 1
    theirs = lax.dynamic_slice_in_dim(total, (1 - bit) * half, half, axis=0).astype(bf16)
    return lax.dynamic_slice_in_dim(total, bit * half, half, axis=0), swap(theirs, "seq", 1)


def send_far(state):
    mine, got = state
    total = mine + got.astype(f32)
    group = lax.axis_size("seq") // 2
    place = lax.axis_index("seq") >> 1
    part = total.shape[0] // group
    piece = lambda k: lax.dynamic_slice_in_dim(total, (place ^ k) * part, part, axis=0)
    return piece(0), [swap(piece(k).astype(bf16), "seq", 2 * k) for k in range(1, group)]


def share_far(state):
    mine, got = state
    owned = (mine + sum(piece.astype(f32) for piece in got)).astype(bf16)
    return [owned] + [swap(owned, "seq", 2 * k) for k in range(1, len(got) + 1)]


def in_order(pieces, place):
    bit = 1
    while bit < len(pieces):
        odd = (place & bit) != 0
        pieces = [jnp.where(odd, pieces[k ^ bit], pieces[k]) for k in range(len(pieces))]
        bit *= 2
    return jnp.concatenate(pieces, axis=0)


def share_near(pieces):
    half = in_order(pieces, lax.axis_index("seq") >> 1)
    return [half, swap(half, "seq", 1)]


def whole_rows(pieces):
    return in_order(pieces, lax.axis_index("seq") & 1)


def local(
    block_in, norm_gain, in_weight, conv_x, conv_x_bias, conv_bc, conv_bc_bias,
    a_log, skip, dt_bias, out_gain, out_weight, cotangent,
):
    tokens = block_in[0]
    cot = cotangent[0]
    length, width = tokens.shape
    seq = lax.axis_size("seq")
    shards = lax.axis_size("wshard")
    own_heads = HEADS // seq
    own_ch = INNER // seq
    me = lax.axis_index("wshard")
    order = jnp.stack([me ^ k for k in range(4)]).astype(jnp.int32)

    a_piece = jnp.concatenate(
        [in_weight[:, INNER : INNER + GW], jnp.pad(in_weight[:, 2 * INNER :], ((0, 0), (0, XCOLS - XUSED)))], axis=1
    )
    b_piece = in_weight[:, INNER + GW : 2 * INNER]
    gate_piece = in_weight[:, :INNER]
    edge = lax.ppermute(tokens[length - EDGE :], "seq", [(i, i + 1) for i in range(seq - 1)])
    small = jnp.concatenate(
        [
            conv_x,
            conv_x_bias[None],
            jnp.pad(jnp.stack([a_log, skip, dt_bias]), ((0, 0), (0, own_ch - own_heads))),
        ],
        axis=0,
    )
    a_across, a_beside = swap(a_piece, "wshard", 2), swap(a_piece, "wshard", 1)
    small_all = exchange(jnp.broadcast_to(small[None], (seq,) + small.shape), "seq")
    x_params = small_all[:, :5].transpose(1, 0, 2).reshape(5, INNER)
    head_params = small_all[:, 5:, :own_heads].transpose(1, 0, 2).reshape(3, HEADS)
    taps, bias = x_params[:4], x_params[4:5]
    heads = jnp.pad(head_params, ((0, 5), (0, 128 - HEADS)))
    skip_row = jnp.repeat(head_params[1], INNER // HEADS)[None]
    bias_bc = conv_bc_bias[None]
    a_across = tie(a_across, small_all, edge, a_beside)
    a_pieces = (a_piece, a_beside, a_across, swap(a_across, "wshard", 1))
    b_piece, gate_piece, out_piece = tie((b_piece, gate_piece, out_weight), a_across)
    b_across, b_beside = swap(b_piece, "wshard", 2), swap(b_piece, "wshard", 1)

    normed, proj0, rest, proj_edge0, rest_edge = project(order, tokens, edge, norm_gain[None], a_pieces)
    gate_across, gate_beside = swap(gate_piece, "wshard", 2), swap(gate_piece, "wshard", 1)
    out_across, out_beside = swap(out_piece, "wshard", 2), swap(out_piece, "wshard", 1)
    bc_act, aux, cum_t = factors(rest, rest_edge, conv_bc, bias_bc, heads)
    b_across = tie(b_across, bc_act)
    b_pieces = (b_piece, b_beside, b_across, swap(b_across, "wshard", 1))
    x_act0, local0, payload0 = states(0, proj0, proj_edge0, taps, bias, bc_act, aux)
    arrived0 = to_owners(payload0)
    proj1, proj_edge1 = project_more(order, tie(normed, payload0), edge, norm_gain[None], b_pieces)
    x_act1, local1, payload1 = states(1, proj1, proj_edge1, taps, bias, bc_act, aux)
    arrived1 = to_owners(payload1)
    y0 = within(0, tie(x_act0, payload1), bc_act, aux, cum_t, skip_row)
    gate_pieces = (gate_piece, gate_beside, gate_across, swap(gate_across, "wshard", 1))
    gate = gate_project(order, tie(normed, y0), gate_pieces)
    entering0 = chain(True, *tie((arrived0, arrived0[:, STATE:, :]), gate))
    totals0, totals1 = arrived0[:, STATE:, :], arrived1[:, STATE:, :]
    back0 = from_owners(entering0)
    entering1 = chain(True, *tie((arrived1, totals1), entering0))
    back1 = from_owners(entering1)
    y1 = within(1, tie(x_act1, entering1), bc_act, aux, cum_t, skip_row)
    entering0, entering1 = tie((back0, back1), y1)
    out_pieces = (out_piece, out_beside, out_across, swap(out_across, "wshard", 1))
    (normed_out, output, dy, grad_gate, ends, back_states, begin, back_payload, y_dot, out_gain_grad) = middle(
        order, (y0, y1), bc_act, aux, (local0, local1), (entering0, entering1), gate, tokens, cot, out_gain[None], out_pieces
    )

    back_arrived = to_owners(back_payload, 2)
    totals = jnp.concatenate([totals0, totals1], axis=2)
    normed_parts = quarters(normed, order)
    out_grads = out_weight_sums(quarters(normed_out, order), cot)
    out_core = send_core(out_grads)
    gate_grads = weight_grad(normed_parts, tie(grad_gate, out_grads))
    gate_core = send_core(gate_grads)
    du0, slope0, grad_bc0, k_dot0 = within_back(
        0, tie(x_act0, gate_grads), bc_act, aux, cum_t, dy, proj0, proj_edge0, taps, bias, ends, begin
    )
    out_x = send_x(tie(out_core, du0), axis=0)
    gate_x = send_x(tie(gate_core, out_x[0]))
    leaving = chain(False, *tie((back_arrived, totals), gate_x[0]))
    leave = from_owners(leaving, 2)
    du1, slope1, grad_bc1, k_dot1 = within_back(
        1, tie(x_act1, leaving), bc_act, aux, cum_t, dy, proj1, proj_edge1, taps, bias, ends, begin
    )
    out_pair = sum_pair(tie(out_x, du1))
    leave = tie(leave, out_pair)
    grad_x0, grad_taps0, tail0, start0, x_dot0, edge_dot0, b_sum0 = backward(
        0, proj0, proj_edge0, taps, skip_row, dy, du0, slope0, x_act0, bc_act, aux, ends, back_states, leave
    )
    all_taps = jnp.concatenate([taps[:, GW:], conv_bc], axis=1)
    backwards = [(i, i - 1) for i in range(1, seq)]

    def fix(grad, tail, start, tap_values):
        fixes = [
            tail[EDGE - 3 + a] + sum(tap_values[k] * start[a - k] for k in range(a + 1)) for a in range(3)
        ]
        fixed_rows = jnp.concatenate([tail[: EDGE - 3], jnp.stack(fixes)], axis=0).astype(bf16)
        return lax.dynamic_update_slice(grad, fixed_rows, (length - EDGE, 0))

    after0 = lax.ppermute(start0, "seq", backwards)
    gate_pair = sum_pair(tie(gate_x, grad_x0))
    out_sum, gate_sum = lax.psum((out_pair, gate_pair), "seq")
    grad_x0 = fix(tie(grad_x0, gate_pair), tail0, after0, taps[:, :GW])
    x0_grads = weight_grad(normed_parts, grad_x0)
    x0_core = send_core(x0_grads)
    grad_x1, grad_taps1, tail1, start1, grad_taps_bc, grad_heads = backward(
        1, proj1, proj_edge1, taps, skip_row, tie(dy, x0_grads), du1, slope1, x_act1, bc_act, aux, ends, back_states,
        leave,
        (rest, rest, rest_edge, conv_bc, bias_bc, heads, y_dot, k_dot0, k_dot1, x_dot0, edge_dot0, b_sum0, grad_bc0, grad_bc1),
    )
    after1 = lax.ppermute(start1, "seq", backwards)
    x0_x = send_x(tie(x0_core, grad_x1))
    grad_x1 = fix(tie(grad_x1, x0_x[0]), tail1, after1, all_taps)
    x1_grads = weight_grad(normed_parts, grad_x1)
    x1_core = send_core(x1_grads)
    x0_near = send_near(tie(x0_x, x1_grads))
    x1_x = send_x(tie(x1_core, x0_near[0]))
    input_grad, norm_gain_grad = input_back(
        order, tie(grad_gate, x1_x[0]), grad_x0, grad_x1, tokens, cot, norm_gain[None], gate_pieces, a_pieces, b_pieces
    )
    x0_far = send_far(tie(x0_near, input_grad))
    x1_near = send_near(tie(x1_x, x0_far[0]))
    x0_all = share_far(tie(x0_far, x1_near[0]))
    x1_far = send_far(tie(x1_near, x0_all[0]))
    x0_half = share_near(tie(x0_all, x1_far[0]))
    x1_half = share_near(share_far(tie(x1_far, x0_half[0])))

    grad_taps = jnp.concatenate([grad_taps0, grad_taps1], axis=1)
    shared = jnp.concatenate(
        [norm_gain_grad[0], out_gain_grad[0], grad_taps_bc[:5].reshape(-1)]
    )
    mine = jnp.concatenate(
        [
            grad_taps[:5].reshape(5, seq, own_ch).transpose(1, 0, 2).reshape(seq, 5 * own_ch),
            grad_heads[:3, :HEADS].reshape(3, seq, own_heads).transpose(1, 0, 2).reshape(seq, 3 * own_heads),
        ],
        axis=1,
    )
    shared_size, mine_size = shared.shape[0], mine.shape[1]
    pad = -(shared_size + mine_size) % 1024
    small_out = jnp.concatenate(
        [jnp.broadcast_to(shared[None], (seq, shared_size)), mine, jnp.zeros((seq, pad), f32)], axis=1
    )
    small_out = jnp.broadcast_to(small_out[:, None], (seq, shards, small_out.shape[1]))
    small_sum = jnp.sum(
        exchange(small_out.reshape(seq * shards, 8, -1), ("seq", "wshard")), axis=0
    ).reshape(-1)
    out_owned = out_sum.astype(f32)
    in_owned = jnp.concatenate(
        [gate_sum, whole_rows(x0_half), whole_rows(x1_half)[: XUSED - GW]], axis=0
    ).astype(f32).T
    pos = [0]

    def take(shape):
        size = 1
        for extent in shape:
            size *= extent
        out = small_sum[pos[0] : pos[0] + size].reshape(shape)
        pos[0] += size
        return out

    norm_gain_sum = take((width,))
    out_gain_sum = take((INNER,))
    bc_sum = take((5, BC))
    x_sum = take((5, own_ch))
    head_sum = take((3, own_heads))
    return (
        output[None],
        input_grad[None],
        norm_gain_sum,
        in_owned,
        x_sum[:4],
        x_sum[4],
        bc_sum[:4],
        bc_sum[4],
        head_sum[0],
        head_sum[1],
        head_sum[2],
        out_gain_sum,
        out_owned,
    )


def solution(mesh):
    in_specs = (
        P("wshard", "seq", None),
        P(),
        P("wshard", None),
        P(None, "seq"),
        P("seq"),
        P(),
        P(),
        P("seq"),
        P("seq"),
        P("seq"),
        P(),
        P("wshard", None),
        P("wshard", "seq", None),
    )
    out_specs = (
        P("wshard", "seq", None),
        P("wshard", "seq", None),
        P(),
        P("wshard", None),
        P(None, "seq"),
        P("seq"),
        P(),
        P(),
        P("seq"),
        P("seq"),
        P("seq"),
        P(),
        P("wshard", None),
    )
    return jax.shard_map(local, mesh=mesh, in_specs=in_specs, out_specs=out_specs, check_vma=False)
```

```python
import functools

import jax
import jax.numpy as jnp
from jax import lax
from jax.experimental import pallas as pl
from jax.experimental.pallas import tpu as pltpu
from jax.sharding import PartitionSpec as P

INNER = 2048
STATE = 128
HEADS = 32
TAPS = 4
BC = 2 * STATE
CH = INNER + BC
XCOLS = 2432
XUSED = 2336
Q = 256
HALF = Q // 2
TILE = 256
TILES = INNER // TILE
GROUPS = 2
GT = TILES // GROUPS
GW = INNER // GROUPS
REST = XCOLS - INNER
PIECES = 2 * GT
EDGE = 16
EPS = 1e-05

f32 = jnp.float32
bf16 = jnp.bfloat16
highest = lax.Precision.HIGHEST


def cparams(megabytes=56):
    return pltpu.CompilerParams(
        dimension_semantics=("arbitrary",), vmem_limit_bytes=megabytes * 2**20
    )


def dot(a, b):
    return lax.dot_general(a, b, (((1,), (0,)), ((), ())), preferred_element_type=f32)


def dot_lanes(a, b):
    return lax.dot_general(a, b, (((1,), (1,)), ((), ())), preferred_element_type=f32)


def dot_rows(a, b):
    return lax.dot_general(a, b, (((0,), (0,)), ((), ())), preferred_element_type=f32)


def sigmoid(v):
    return 0.5 * jnp.tanh(0.5 * v) + 0.5


def lane_iota(rows, lanes):
    return lax.broadcasted_iota(jnp.int32, (rows, lanes), 1)


def row_iota(rows, lanes):
    return lax.broadcasted_iota(jnp.int32, (rows, lanes), 0)


def spread(terms, width, first, shift):
    rows = row_iota(terms * HEADS, width) & (HEADS - 1)
    return jnp.where(rows == first + (lane_iota(terms * HEADS, width) >> shift), 1.0, 0.0).astype(bf16)


def halves(value):
    high = value.astype(bf16)
    return high, (value - high.astype(f32)).astype(bf16)


def terms2(value):
    return jnp.concatenate(halves(value), axis=1)


def terms4(value):
    high = value.astype(bf16)
    rest = value - high.astype(f32)
    middle, low = halves(rest)
    return jnp.concatenate([high, middle, low, jnp.zeros_like(high)], axis=1)


def split_dot(value, select):
    high = value.astype(bf16)
    low = (value - high.astype(f32)).astype(bf16)
    return dot(high, select) + dot(low, select)


def fine(product, a, b):
    a_high, a_low = halves(a)
    b_high, b_low = halves(b)
    return product(a_high, b_high) + (product(a_high, b_low) + product(a_low, b_high))


def fine_with(product, a_terms, b):
    a_high, a_low = a_terms
    b_high, b_low = halves(b)
    return product(a_high, b_high) + (product(a_high, b_low) + product(a_low, b_high))


def fine_short(a_terms, b):
    a_high, a_both = a_terms
    b_high, b_low = halves(b)
    return dot(a_both, jnp.concatenate([b_high, b_high], axis=0)) + dot(a_high, b_low)


def head_select(tile):
    lanes = row_iota(TILE, 128) >> 6
    return jnp.where(lanes + tile * (TILE // 64) == lane_iota(TILE, 128), 1.0, 0.0).astype(bf16)


def shifted(current, before):
    joined = jnp.concatenate([before[EDGE - 8 :], current], axis=0)
    rows = current.shape[0]
    return [joined[5 + k : 5 + k + rows] for k in range(TAPS - 1)] + [current]


def conv_of(parts, taps, bias):
    total = bias + taps[0:1] * parts[0]
    for k in range(1, TAPS):
        total = total + taps[k : k + 1] * parts[k]
    return total


def later_rows(grad, after):
    joined = jnp.concatenate([grad, after], axis=0)
    rows = grad.shape[0]
    return [joined[TAPS - 1 - k : TAPS - 1 - k + rows] for k in range(TAPS - 1)] + [grad]


def tap_sums(parts, raw, grad, early):
    first = grad[:8]
    sums = []
    for k in range(TAPS):
        total = jnp.sum(parts[k] * raw, axis=0, keepdims=True)
        if k < TAPS - 1:
            total = total + jnp.sum(first[: TAPS - 1 - k] * early[8 - TAPS + 1 + k :], axis=0, keepdims=True)
        sums.append(total)
    sums.append(jnp.sum(grad, axis=0, keepdims=True))
    sums.append(jnp.zeros((3, grad.shape[1]), f32))
    return jnp.concatenate(sums, axis=0)


def tile_at(j, width=TILE):
    return pl.ds(pl.multiple_of(j * width, width), width)


def assemble(order, pieces, full):
    rows = pieces[0].shape[0]
    for k, piece in enumerate(pieces):
        full[pl.ds(pl.multiple_of(order[k] * rows, rows), rows), :] = piece[...]


def norm_rows(values, gain):
    wide = values.astype(f32)
    scale = lax.rsqrt(jnp.mean(wide * wide, axis=1, keepdims=True) + EPS)
    return (wide * scale * gain).astype(bf16)


def project_kernel(order, tokens, edge, gain, w0, w1, w2, w3, normed, out, out_rest, out_edge, out_edge_rest, full):
    @pl.when(pl.program_id(0) == 0)
    def _():
        assemble(order, (w0, w1, w2, w3), full)
        early = dot(norm_rows(edge[...], gain[...]), full[...]).astype(bf16)
        out_edge[...] = early[:, :GW]
        out_edge_rest[...] = early[:, GW:]

    now = norm_rows(tokens[...], gain[...])
    normed[...] = now
    for start in range(0, GW, TILE):
        out[:, start : start + TILE] = dot(now, full[:, start : start + TILE]).astype(bf16)
    out_rest[...] = dot(now, full[:, GW:]).astype(bf16)


def project_more_kernel(order, normed, edge, gain, w0, w1, w2, w3, out, out_edge, full):
    @pl.when(pl.program_id(0) == 0)
    def _():
        assemble(order, (w0, w1, w2, w3), full)
        out_edge[...] = dot(norm_rows(edge[...], gain[...]), full[...]).astype(bf16)

    for start in range(0, GW, TILE):
        out[:, start : start + TILE] = dot(normed[...], full[:, start : start + TILE]).astype(bf16)


def fixed(shape):
    return pl.BlockSpec(shape, lambda i, *o: (0,) * len(shape), pipeline_mode=pl.Buffered(1))


def kept(shape):
    return pl.BlockSpec(shape, lambda i, *o: (0,) * len(shape))


def rows_of(cols, group=0):
    return pl.BlockSpec((Q, cols), lambda i, *o: (i, group))


def shape_of(shape, dtype=f32):
    return jax.ShapeDtypeStruct(shape, dtype)


def cost(flops, megabytes):
    return pl.CostEstimate(flops=int(flops) // 50, bytes_accessed=int(megabytes * 2**20) // 50, transcendentals=0)


def project(order, tokens, edge, gain, pieces):
    length, width = tokens.shape
    rows = pieces[0].shape[0]
    return pl.pallas_call(
        project_kernel,
        grid_spec=pltpu.PrefetchScalarGridSpec(
            num_scalar_prefetch=1,
            grid=(length // Q,),
            in_specs=[rows_of(width), fixed((EDGE, width)), fixed((1, width))] + [fixed((rows, GW + REST))] * 4,
            out_specs=[rows_of(width), rows_of(GW), rows_of(REST), kept((EDGE, GW)), kept((EDGE, REST))],
            scratch_shapes=[pltpu.VMEM((4 * rows, GW + REST), bf16)],
        ),
        out_shape=[
            shape_of((length, width), bf16),
            shape_of((length, GW), bf16),
            shape_of((length, REST), bf16),
            shape_of((EDGE, GW), bf16),
            shape_of((EDGE, REST), bf16),
        ],
        compiler_params=cparams(),
        cost_estimate=cost(2 * length * width * (GW + REST), 9),
        name="project",
    )(order, tokens, edge, gain, *pieces)


def project_more(order, normed, edge, gain, pieces):
    length, width = normed.shape
    rows = pieces[0].shape[0]
    return pl.pallas_call(
        project_more_kernel,
        grid_spec=pltpu.PrefetchScalarGridSpec(
            num_scalar_prefetch=1,
            grid=(length // Q,),
            in_specs=[rows_of(width), fixed((EDGE, width)), fixed((1, width))] + [fixed((rows, GW))] * 4,
            out_specs=[rows_of(GW), kept((EDGE, GW))],
            scratch_shapes=[pltpu.VMEM((4 * rows, GW), bf16)],
        ),
        out_shape=[shape_of((length, GW), bf16), shape_of((EDGE, GW), bf16)],
        compiler_params=cparams(),
        cost_estimate=cost(2 * length * width * GW, 6),
        name="project_more",
    )(order, normed, edge, gain, *pieces)


def gate_kernel(order, normed, w0, w1, w2, w3, out, full):
    @pl.when(pl.program_id(0) == 0)
    def _():
        assemble(order, (w0, w1, w2, w3), full)

    for j in range(TILES):
        cols = slice(j * TILE, (j + 1) * TILE)
        out[:, cols] = dot(normed[...], full[:, cols]).astype(bf16)


def gate_project(order, normed, pieces):
    length, width = normed.shape
    rows = pieces[0].shape[0]
    return pl.pallas_call(
        gate_kernel,
        grid_spec=pltpu.PrefetchScalarGridSpec(
            num_scalar_prefetch=1,
            grid=(length // Q,),
            in_specs=[rows_of(width)] + [fixed((rows, INNER))] * 4,
            out_specs=rows_of(INNER),
            scratch_shapes=[pltpu.VMEM((4 * rows, INNER), bf16)],
        ),
        out_shape=shape_of((length, INNER), bf16),
        compiler_params=cparams(),
        cost_estimate=cost(2 * length * width * INNER, 10),
        name="gate_project",
    )(order, normed, *pieces)


def factors_kernel(now, prior, edge, taps_bc, bias_bc, heads, bc_act, aux_out, cum_t):
    first = pl.program_id(0) == 0
    early = jnp.where(first, edge[:, :BC], prior[:, :BC]).astype(f32)
    pre = conv_of(shifted(now[:, :BC].astype(f32), early), taps_bc[...], bias_bc[...])
    bc_act[...] = pre * sigmoid(pre)
    raw = now[:, BC : BC + HEADS].astype(f32) + heads[2:3, :HEADS]
    step = jnp.maximum(raw, 0.0) + jnp.log1p(jnp.exp(-jnp.abs(raw)))
    decay = -jnp.exp(heads[0:1, :HEADS]) * step
    lower = jnp.where(row_iota(Q, Q) >= lane_iota(Q, Q), 1.0, 0.0)
    cumulative = jnp.dot(lower, decay, precision=highest, preferred_element_type=f32)
    last = cumulative[Q - 1 : Q]
    aux = jnp.concatenate([cumulative, step, jnp.exp(last - cumulative), jnp.exp(cumulative)], axis=1)
    aux_out[...] = aux
    cum_t[...] = aux.T[:HEADS]


def states_kernel(
    group, now, prior, edge, taps, bias, bc_act, aux, x_act, local, payload, run, total, b_rows
):
    c = pl.program_id(0)
    first = c == 0

    @pl.when(first)
    def _():
        run[...] = jnp.zeros_like(run)
        total[...] = jnp.zeros_like(total)

    b_rows[...] = bc_act[:, :STATE].T
    weight2 = terms2(aux[:, HEADS : 2 * HEADS] * aux[:, 2 * HEADS : 3 * HEADS])
    ends4 = terms4(jnp.concatenate([aux[Q - 8 :, 3 * HEADS :], aux[Q - 8 :, :HEADS]], axis=0))

    def body(j, carry):
        cols = tile_at(j)
        early = jnp.where(first, edge[:, cols], prior[:, cols]).astype(f32)
        pre = conv_of(shifted(now[:, cols].astype(f32), early), taps[:, cols], bias[:, cols])
        x = pre * sigmoid(pre)
        x_act[:, cols] = x
        lead = 4 * (j + group * GT)
        state = fine(dot, b_rows[...], x * dot(weight2, spread(2, TILE, lead, 6)))
        local[0, j] = state
        end = dot(ends4, spread(4, TILE, lead, 6))
        run[j] = end[7:8] * run[j] + state
        total[:, cols] += end[15:16]
        return carry

    lax.fori_loop(0, GT, body, 0, unroll=GT)

    @pl.when(c == pl.num_programs(0) - 1)
    def _():
        for j in range(2 * GT):
            lanes = slice(128 * (j % 2), 128 * (j % 2) + 128)
            payload[j, :STATE, :] = run[j // 2, :, lanes]
            payload[j, STATE:, :] = jnp.broadcast_to(total[:, j * 128 : (j + 1) * 128], (8, 128))


def prior_rows(cols, group=0):
    per = Q // EDGE
    return pl.BlockSpec((EDGE, cols), lambda i, *o: (jnp.maximum(i * per - 1, 0), group))


def at_group(rows, group):
    return pl.BlockSpec((rows, GW), lambda i, *o: (0, group), pipeline_mode=pl.Buffered(1))


def factors(rest, rest_edge, taps_bc, bias_bc, heads):
    length = rest.shape[0]
    return pl.pallas_call(
        factors_kernel,
        grid=(length // Q,),
        in_specs=[
            rows_of(REST), prior_rows(REST), fixed((EDGE, REST)),
            fixed((TAPS, BC)), fixed((1, BC)), fixed((8, 128)),
        ],
        out_specs=[rows_of(BC), rows_of(128), pl.BlockSpec((HEADS, Q), lambda i: (0, i))],
        out_shape=[shape_of((length, BC)), shape_of((length, 128)), shape_of((HEADS, length))],
        compiler_params=cparams(),
        cost_estimate=cost(10**9, 4),
        name="factors",
    )(rest, rest, rest_edge, taps_bc, bias_bc, heads)


def states(group, proj, proj_edge, taps, bias, bc_act, aux):
    length = proj.shape[0]
    chunks = length // Q
    return pl.pallas_call(
        functools.partial(states_kernel, group),
        grid=(chunks,),
        in_specs=[
            rows_of(GW), prior_rows(GW), fixed((EDGE, GW)),
            at_group(TAPS, group), at_group(1, group), rows_of(BC), rows_of(128),
        ],
        out_specs=[
            rows_of(GW),
            pl.BlockSpec((1, GT, STATE, TILE), lambda i: (i, 0, 0, 0)),
            kept((2 * GT, STATE + 8, 128)),
        ],
        out_shape=[
            shape_of((length, GW)),
            shape_of((chunks, GT, STATE, TILE)),
            shape_of((2 * GT, STATE + 8, 128)),
        ],
        scratch_shapes=[
            pltpu.VMEM((GT, STATE, TILE), f32),
            pltpu.VMEM((1, GW), f32),
            pltpu.VMEM((STATE, Q), f32),
        ],
        compiler_params=cparams(),
        cost_estimate=cost(10**10, 10),
        name="states",
    )(proj, proj, proj_edge, taps, bias, bc_act, aux)


def chain_kernel(forward, values, totals, out):
    count = out.shape[0]
    order = range(count) if forward else range(count - 1, -1, -1)
    state = jnp.zeros(out.shape[1:], f32)
    for i in order:
        out[i] = state
        state = jnp.exp(totals[i, 0:1, :]) * state + values[i, :STATE, :]


def chain(forward, values, totals):
    count, _, width = values.shape
    return pl.pallas_call(
        functools.partial(chain_kernel, forward),
        out_shape=jax.ShapeDtypeStruct((count, STATE, width), f32),
        compiler_params=pltpu.CompilerParams(vmem_limit_bytes=56 * 2**20),
        cost_estimate=cost(10**8, 3),
        name="chain",
    )(values, totals)


def within_kernel(group, x_act, bc_act, aux, cum_t, skip, out, scores, columns):
    lower = row_iota(HALF, HALF) >= lane_iota(HALF, HALF)
    for b in range(2):
        rows = slice(b * HALF, (b + 1) * HALF)
        scores[rows, :] = jnp.where(lower, fine(dot_lanes, bc_act[rows, STATE:], bc_act[rows, :STATE]), 0.0)
    cross_high, cross_low = halves(fine(dot_lanes, bc_act[HALF:, STATE:], bc_act[:HALF, :STATE]))
    cross2 = jnp.concatenate([cross_high, cross_low], axis=1)
    cumulative = aux[:, :HEADS]
    middle_row = cumulative[HALF - 1 : HALF]
    step2 = terms2(aux[:, HEADS : 2 * HEADS])
    bridge2 = terms2(jnp.exp(jnp.concatenate([middle_row - cumulative[:HALF], cumulative[HALF:] - middle_row], axis=0)))
    cumulative4 = terms4(cumulative)
    for j in range(GT):
        columns[:, j * 512 : (j + 1) * 512] = dot(cumulative4, spread(4, 512, 4 * (j + group * GT), 7))
    low = lane_iota(HALF, HALF) < 64

    def body(j, carry):
        cols = tile_at(j)
        x = x_act[:, cols]
        select = spread(2, TILE, 4 * (j + group * GT), 6)
        u = x * dot(step2, select)
        bridge = dot(bridge2, select)
        u_high, u_low = halves(u)
        v_high, v_low = halves(u[:HALF] * bridge[:HALF])
        across = dot(cross2, jnp.concatenate([v_high, v_high], axis=0)) + dot(cross_high, v_low)
        across = across * bridge[HALF:]
        direct = skip[:, cols] * x
        for pair in range(2):
            lanes = slice(pair * 128, (pair + 1) * 128)
            place = pl.ds(pl.multiple_of(j * TILE + pair * 128, 128), 128)
            for b in range(2):
                rows = slice(b * HALF, (b + 1) * HALF)
                weights = []
                for i in range(2):
                    head = 4 * j + 2 * pair + i
                    column = columns[rows, pl.ds(pl.multiple_of(head * 128, 128), 128)]
                    row = cum_t[pl.ds(head + 4 * GT * group, 1), :][:, rows]
                    weights.append(jnp.exp(jnp.minimum(column - row, 0.0)) * scores[rows, :])
                w_high, w_low = halves(jnp.concatenate(weights, axis=1))
                top = both_heads(low, u_high[rows, lanes])
                bottom = both_heads(low, u_low[rows, lanes])
                twice = dot(w_high, jnp.concatenate([top, bottom], axis=1))
                y = twice[:, :128] + twice[:, 128:] + dot(w_low, top) + direct[rows, lanes]
                if b == 1:
                    y = y + across[:, lanes]
                out[rows, place] = y
        return carry

    lax.fori_loop(0, GT, body, 0, unroll=GT)


def both_heads(low, value):
    zero = jnp.zeros_like(value)
    return jnp.concatenate([jnp.where(low, value, zero), jnp.where(low, zero, value)], axis=0)


def within(group, x_act, bc_act, aux, cum_t, skip):
    length = x_act.shape[0]
    return pl.pallas_call(
        functools.partial(within_kernel, group),
        grid=(length // Q,),
        in_specs=[
            rows_of(GW), rows_of(BC), rows_of(128),
            pl.BlockSpec((HEADS, Q), lambda i: (0, i)), at_group(1, group),
        ],
        out_specs=rows_of(GW),
        out_shape=shape_of((length, GW)),
        scratch_shapes=[pltpu.VMEM((Q, HALF), f32), pltpu.VMEM((Q, GT * 512), f32)],
        compiler_params=cparams(),
        cost_estimate=cost(10**10, 10),
        name="within",
    )(x_act, bc_act, aux, cum_t, skip)


def within_back_kernel(
    group, x_act, bc_act, aux, cum_t, dy, now, prior, edge, taps, bias, ends, entering,
    out, slope, out_bc, k_dot, scores, grad_scores, grad_cross, columns,
):
    first = pl.program_id(0) == 0
    k_dot[...] = jnp.zeros_like(k_dot)
    out_bc[:, STATE:] = jnp.zeros((Q, STATE), f32)
    upper = row_iota(HALF, HALF) <= lane_iota(HALF, HALF)
    act = bc_act[...].astype(bf16)
    b_act, c_act = act[:, :STATE], act[:, STATE:]
    for b in range(2):
        rows = slice(b * HALF, (b + 1) * HALF)
        scores[rows, :] = jnp.where(upper, dot_lanes(b_act[rows], c_act[rows]), 0.0)
    grad_scores[...] = jnp.zeros_like(grad_scores)
    grad_cross[...] = jnp.zeros_like(grad_cross)
    cross = dot_lanes(b_act[:HALF], c_act[HALF:]).astype(bf16)
    cumulative = aux[:, :HEADS]
    middle_row = cumulative[HALF - 1 : HALF]
    step2 = terms2(aux[:, HEADS : 2 * HEADS])
    decayed2 = terms2(aux[:, 3 * HEADS :])
    bridge2 = terms2(jnp.exp(jnp.concatenate([middle_row - cumulative[:HALF], cumulative[HALF:] - middle_row], axis=0)))
    cumulative4 = terms4(cumulative)
    for j in range(GT):
        columns[:, j * 512 : (j + 1) * 512] = dot(cumulative4, spread(4, 512, 4 * (j + group * GT), 7))
    low = lane_iota(HALF, HALF) < 64

    def body(j, carry):
        cols = tile_at(j)
        lead = 4 * (j + group * GT)
        select = spread(2, TILE, lead, 6)
        x = x_act[:, cols]
        u = x * dot(step2, select)
        bridge = dot(bridge2, select)
        u_low = u.astype(bf16)
        grad = dy[:, cols]
        wide = grad.astype(f32)
        early_raw = jnp.where(first, edge[:, cols], prior[:, cols]).astype(f32)
        pre = conv_of(shifted(now[:, cols].astype(f32), early_raw), taps[:, cols], bias[:, cols])
        sig = sigmoid(pre)
        slope[:, cols] = (sig + x * (1.0 - sig)).astype(bf16)
        k_dot[...] += split_dot(x * wide, head_select(j + group * GT))
        enter = jnp.where(first, entering[j], ends[0, j])
        out_bc[:, STATE:] += fine(dot_lanes, wide * dot(decayed2, select), enter)
        early = (u[:HALF] * bridge[:HALF]).astype(bf16)
        late = (grad[HALF:].astype(f32) * bridge[HALF:]).astype(bf16)
        grad_cross[...] += dot_lanes(early, late)
        across = dot(cross, late) * bridge[:HALF]
        totals = [None, None]
        for pair in range(2):
            lanes = slice(pair * 128, (pair + 1) * 128)
            place = pl.ds(pl.multiple_of(j * TILE + pair * 128, 128), 128)
            for b in range(2):
                rows = slice(b * HALF, (b + 1) * HALF)
                spaced = both_heads(low, grad[rows, lanes])
                products = dot_lanes(u_low[rows, lanes], spaced)
                weights = []
                for i in range(2):
                    head = 4 * j + 2 * pair + i
                    column = columns[rows, pl.ds(pl.multiple_of(head * 128, 128), 128)]
                    row = cum_t[pl.ds(head + 4 * GT * group, 1), :][:, rows]
                    weight = jnp.exp(jnp.minimum(row - column, 0.0))
                    part = weight * products[:, i * 128 : (i + 1) * 128]
                    totals[b] = part if totals[b] is None else totals[b] + part
                    weights.append((weight * scores[rows, :]).astype(bf16))
                du = dot(jnp.concatenate(weights, axis=1), spaced)
                if b == 0:
                    du = du + across[:, lanes]
                out[rows, place] = du.astype(bf16)
        for b in range(2):
            grad_scores[b * HALF : (b + 1) * HALF, :] += totals[b]
        return carry

    lax.fori_loop(0, GT, body, 0, unroll=GT)
    far = grad_cross[...].astype(bf16)
    near0 = jnp.where(upper, grad_scores[:HALF, :], 0.0).astype(bf16)
    near1 = jnp.where(upper, grad_scores[HALF:, :], 0.0).astype(bf16)
    out_bc[:HALF, :STATE] = dot(near0, c_act[:HALF]) + dot(far, c_act[HALF:])
    out_bc[HALF:, :STATE] = dot(near1, c_act[HALF:])
    out_bc[:HALF, STATE:] += dot_rows(near0, b_act[:HALF])
    out_bc[HALF:, STATE:] += dot_rows(near1, b_act[HALF:]) + dot_rows(far, b_act[:HALF])


def within_back(group, x_act, bc_act, aux, cum_t, dy, proj, proj_edge, taps, bias, ends, entering):
    length = x_act.shape[0]
    return pl.pallas_call(
        functools.partial(within_back_kernel, group),
        grid=(length // Q,),
        in_specs=[
            rows_of(GW), rows_of(BC), rows_of(128),
            pl.BlockSpec((HEADS, Q), lambda i: (0, i)), rows_of(GW, group),
            rows_of(GW), prior_rows(GW), fixed((EDGE, GW)),
            at_group(TAPS, group), at_group(1, group),
            pl.BlockSpec((1, GT, STATE, TILE), lambda i: (jnp.maximum(i - 1, 0), group, 0, 0)),
            pl.BlockSpec((GT, STATE, TILE), lambda i: (group, 0, 0), pipeline_mode=pl.Buffered(1)),
        ],
        out_specs=[rows_of(GW), rows_of(GW), rows_of(BC), rows_of(128)],
        out_shape=[
            shape_of((length, GW), bf16), shape_of((length, GW), bf16),
            shape_of((length, BC)), shape_of((length, 128)),
        ],
        scratch_shapes=[
            pltpu.VMEM((Q, HALF), f32),
            pltpu.VMEM((Q, HALF), f32),
            pltpu.VMEM((HALF, HALF), f32),
            pltpu.VMEM((Q, GT * 512), f32),
        ],
        compiler_params=cparams(),
        cost_estimate=cost(2 * 10**10, 14),
        name="within_back",
    )(x_act, bc_act, aux, cum_t, dy, proj, proj, proj_edge, taps, bias, ends, entering)


def middle_kernel(
    order, y_in0, y_in1, bc_act, aux, local0, local1, entering0, entering1, gate, tokens, cot, gain, w0, w1, w2, w3,
    normed_out, output, dy_out, grad_gate, ends, back_states, begin, payload, y_dot, gain_grad,
    full, state, back, before, y_keep, gated_keep, grad_keep,
):
    c = pl.program_id(0)

    @pl.when(c == 0)
    def _():
        assemble(order, (w0, w1, w2, w3), full)
        for g, entering in enumerate((entering0, entering1)):
            for j in range(GT):
                state[g * GT + j, :, :128] = entering[2 * j]
                state[g * GT + j, :, 128:] = entering[2 * j + 1]
        begin[...] = state[...]
        back[...] = jnp.zeros_like(back)
        before[...] = jnp.zeros_like(before)
        gain_grad[...] = jnp.zeros_like(gain_grad)

    keep = aux[...]
    c_high, c_low = halves(bc_act[:, STATE:])
    c_cols = (c_high, jnp.concatenate([c_high, c_low], axis=1))
    c_rows = halves(bc_act[:, STATE:].T)

    decayed2 = terms2(keep[:, 3 * HEADS :])
    ends4 = terms4(jnp.concatenate([keep[Q - 8 :, 3 * HEADS :], keep[Q - 8 :, :HEADS]], axis=0))

    def mix(y_in, local, shift, place, squares):
        j = place + shift
        cols = tile_at(j)
        carried = fine_short(c_cols, state[j])
        y = y_in[:, tile_at(place)] + dot(decayed2, spread(2, TILE, 4 * j, 6)) * carried
        y_keep[:, cols] = y
        raw = gate[:, cols].astype(f32)
        gated = y.astype(bf16).astype(f32) * (raw * sigmoid(raw))
        gated_keep[:, cols] = gated
        moved = dot(ends4, spread(4, TILE, 4 * j, 6))[7:8] * state[j] + local[0, place]
        state[j] = moved
        ends[0, j] = moved
        both = gated * gated
        return squares + (both[:, :128] + both[:, 128:])

    squares = jnp.zeros((Q, 128), f32)
    for g, (y_in, local) in enumerate(((y_in0, local0), (y_in1, local1))):
        squares = lax.fori_loop(0, GT, functools.partial(mix, y_in, local, g * GT), squares, unroll=GT)
    scale = lax.rsqrt(jnp.sum(squares, axis=1, keepdims=True) / INNER + EPS)

    def back_out(j, products):
        cols = tile_at(j)
        gated = gated_keep[:, cols]
        gains = gain[:, cols]
        normed_out[:, cols] = (gated * scale * gains).astype(bf16)
        grad = dot_lanes(cot[...], full[cols, :])
        grad_keep[:, cols] = grad
        gain_grad[:, cols] += jnp.sum(grad * gated * scale, axis=0, keepdims=True)
        both = grad * gains * gated
        return products + (both[:, :128] + both[:, 128:])

    products = lax.fori_loop(0, TILES, back_out, jnp.zeros((Q, 128), f32), unroll=8)
    shared = jnp.sum(products, axis=1, keepdims=True) / INNER * (scale * scale * scale)
    for start in range(0, output.shape[1], TILE):
        cols = slice(start, start + TILE)
        branch = dot(normed_out[...], full[:, cols])
        output[:, cols] = (tokens[:, cols].astype(f32) + branch).astype(bf16)

    def finish(j, y_sum):
        cols = tile_at(j)
        raw = gate[:, cols].astype(f32)
        sig = sigmoid(raw)
        grad_gated = scale * (grad_keep[:, cols] * gain[:, cols]) - gated_keep[:, cols] * shared
        y = y_keep[:, cols]
        dy = (grad_gated * (raw * sig)).astype(bf16)
        dy_out[:, cols] = dy
        mixed = y.astype(bf16).astype(f32)
        grad_gate[:, cols] = (grad_gated * mixed * (sig * (1.0 + raw * (1.0 - sig)))).astype(bf16)
        wide = dy.astype(f32)
        piece = fine_with(dot, c_rows, wide * dot(decayed2, spread(2, TILE, 4 * j, 6)))
        back_states[0, j] = piece
        back[j] += jnp.exp(before[:, cols]) * piece
        before[:, cols] += dot(ends4, spread(4, TILE, 4 * j, 6))[15:16]
        return y_sum + split_dot(wide * y, head_select(j))

    y_dot[...] = lax.fori_loop(0, TILES, finish, jnp.zeros((Q, 128), f32), unroll=8)

    @pl.when(c == pl.num_programs(0) - 1)
    def _():
        for g in range(GROUPS):
            for j in range(GT):
                payload[2 * j, :, g * 128 : (g + 1) * 128] = back[g * GT + j, :, :128]
                payload[2 * j + 1, :, g * 128 : (g + 1) * 128] = back[g * GT + j, :, 128:]


def middle(order, y_in, bc_act, aux, local, entering, gate, tokens, cot, gain, pieces):
    length, width = tokens.shape
    rows = pieces[0].shape[0]
    chunks = length // Q
    per_group = pl.BlockSpec((1, GT, STATE, TILE), lambda i, o: (i, 0, 0, 0))
    per_chunk = pl.BlockSpec((1, TILES, STATE, TILE), lambda i, o: (i, 0, 0, 0))
    return pl.pallas_call(
        middle_kernel,
        grid_spec=pltpu.PrefetchScalarGridSpec(
            num_scalar_prefetch=1,
            grid=(chunks,),
            in_specs=[rows_of(GW)] * 2
            + [rows_of(BC), rows_of(128)]
            + [per_group] * 2
            + [fixed((2 * GT, STATE, 128))] * 2
            + [rows_of(INNER), rows_of(width), rows_of(width), fixed((1, INNER))]
            + [fixed((rows, width))] * 4,
            out_specs=[
                rows_of(INNER), rows_of(width), rows_of(INNER), rows_of(INNER), per_chunk, per_chunk,
                kept((TILES, STATE, TILE)), kept((PIECES, STATE, TILE)), rows_of(128), kept((1, INNER)),
            ],
            scratch_shapes=[
                pltpu.VMEM((4 * rows, width), bf16),
                pltpu.VMEM((TILES, STATE, TILE), f32),
                pltpu.VMEM((TILES, STATE, TILE), f32),
                pltpu.VMEM((1, INNER), f32),
                pltpu.VMEM((Q, INNER), f32),
                pltpu.VMEM((Q, INNER), f32),
                pltpu.VMEM((Q, INNER), f32),
            ],
        ),
        out_shape=[
            shape_of((length, INNER), bf16),
            shape_of((length, width), bf16),
            shape_of((length, INNER), bf16),
            shape_of((length, INNER), bf16),
            shape_of((chunks, TILES, STATE, TILE)),
            shape_of((chunks, TILES, STATE, TILE)),
            shape_of((TILES, STATE, TILE)),
            shape_of((PIECES, STATE, TILE)),
            shape_of((length, 128)),
            shape_of((1, INNER)),
        ],
        compiler_params=cparams(),
        cost_estimate=cost(4 * 10**10, 40),
        name="middle",
    )(order, *y_in, bc_act, aux, *local, *entering, gate, tokens, cot, gain, *pieces)


def back_kernel(
    group, now, edge, taps, skip, dy, du_in, slope, x_act, bc_act, aux, ends, back_states, leaving, *others
):
    last_group = group == GROUPS - 1
    if last_group:
        (rest, rest_prior, rest_edge, taps_bc, bias_bc, heads, y_dot,
         k_dot0, k_dot1, x_before, edge_before, b_before, bc_in0, bc_in1,
         grad, grad_taps, tail, start, grad_taps_bc, grad_heads,
         later, after, x_dot, edge_dot, b_sum) = others
    else:
        (grad, grad_taps, tail, start, x_dot, edge_dot, b_sum, later, after) = others
    step_id = pl.program_id(0)
    first = step_id == pl.num_programs(0) - 1

    @pl.when(step_id == 0)
    def _():
        for j in range(GT):
            later[j, :, :128] = leaving[2 * j, :, group * 128 : (group + 1) * 128]
            later[j, :, 128:] = leaving[2 * j + 1, :, group * 128 : (group + 1) * 128]
        after[...] = jnp.zeros_like(after)
        grad_taps[...] = jnp.zeros_like(grad_taps)
        if last_group:
            grad_taps_bc[...] = jnp.zeros_like(grad_taps_bc)
            grad_heads[...] = jnp.zeros_like(grad_heads)

    keep = aux[...]
    b_act = bc_act[:, :STATE].astype(bf16)
    factors2 = terms2(
        jnp.concatenate([keep[:, HEADS * k : HEADS * (k + 1)] for k in range(1, 3)], axis=0)
    )
    ends4 = terms4(keep[Q - 8 :, 3 * HEADS :])
    x_dot[...] = jnp.zeros_like(x_dot)
    edge_dot[...] = jnp.zeros_like(edge_dot)
    b_sum[...] = jnp.zeros_like(b_sum)

    def through(cols, dv, raw, early, tap_values):
        parts = later_rows(dv, after[:, cols])
        result = conv_of(parts, tap_values, 0.0)
        after[:, cols] = dv[:8]
        grad[:, cols] = result.astype(bf16)

        @pl.when(step_id == 0)
        def _():
            tail[:, cols] = result[Q - EDGE :]

        early = jnp.where(first, early[EDGE - 8 :].astype(f32), 0.0)
        return tap_sums(parts, raw, dv, early)

    def body(j, carry):
        cols = tile_at(j)
        select = spread(2, TILE, 4 * (j + group * GT), 6)
        heads_of = head_select(j + group * GT)
        factors = dot(factors2, select)
        step, tail_decay = factors[:Q], factors[Q:]
        x = x_act[:, cols]
        later_state = later[j]
        du = du_in[:, cols].astype(f32) + tail_decay * dot(b_act, later_state.astype(bf16))
        x_dot[...] += split_dot(x * du, heads_of)
        b_sum[...] += fine(dot_lanes, x * step * tail_decay, later_state)
        meet = jnp.sum(ends[0, j] * later_state, axis=0, keepdims=True)
        edge_dot[...] += split_dot(jnp.broadcast_to(meet, (8, TILE)), heads_of)
        later[j] = dot(ends4, spread(4, TILE, 4 * (j + group * GT), 6))[7:8] * later_state + back_states[0, j]
        dv = (step * du + skip[:, cols] * dy[:, cols].astype(f32)) * slope[:, cols].astype(f32)
        grad_taps[:, cols] += through(cols, dv, now[:, cols].astype(f32), edge[:, cols], taps[:, cols])
        return carry

    lax.fori_loop(0, GT, body, 0, unroll=2 if last_group else GT)

    if last_group:
        band = slice(GW, GW + BC)
        current = rest[:, :BC].astype(f32)
        early = jnp.where(first, rest_edge[:, :BC], rest_prior[:, :BC])
        pre = conv_of(shifted(current, early.astype(f32)), taps_bc[...], bias_bc[...])
        sig = sigmoid(pre)
        grad_act = bc_in0[...] + bc_in1[...]
        grad_act = grad_act + jnp.concatenate([b_sum[...] + b_before[...], jnp.zeros((Q, STATE), f32)], axis=1)
        dv = grad_act * (sig * (1.0 + pre * (1.0 - sig)))
        grad_taps_bc[...] += through(band, dv, current, rest_edge[:, :BC], taps_bc[...])

        step = keep[:, HEADS : 2 * HEADS]
        by_step = x_dot[:, :HEADS] + x_before[:, :HEADS]
        by_skip = k_dot0[:, :HEADS] + k_dot1[:, :HEADS]
        rate = -jnp.exp(heads[0:1, :HEADS])
        by_sum = y_dot[:, :HEADS] - heads[1:2, :HEADS] * by_skip - step * by_step
        upper = jnp.where(row_iota(Q, Q) <= lane_iota(Q, Q), 1.0, 0.0)
        by_decay = jnp.dot(upper, by_sum, precision=highest, preferred_element_type=f32)
        by_decay = by_decay + (edge_dot[0:1, :HEADS] + edge_before[0:1, :HEADS])
        raw = rest[:, BC : BC + HEADS].astype(f32) + heads[2:3, :HEADS]
        grad_dt = (by_step + by_decay * rate) * sigmoid(raw)
        full_dt = jnp.concatenate([grad_dt, jnp.zeros((Q, 128 - HEADS), f32)], axis=1)
        grad[:, GW + BC :] = full_dt.astype(bf16)
        sums = [
            jnp.sum(by_decay * (rate * step), axis=0, keepdims=True),
            jnp.sum(by_skip, axis=0, keepdims=True),
            jnp.sum(grad_dt, axis=0, keepdims=True),
            jnp.zeros((5, HEADS), f32),
        ]
        grad_heads[:, :HEADS] += jnp.concatenate(sums, axis=0)

    @pl.when(first)
    def _():
        start[...] = after[...]


def backward(group, proj, proj_edge, taps, skip, dy, du, slope, x_act, bc_act, aux, ends, back_states, leaving, others=()):
    length = proj.shape[0]
    chunks = length // Q
    per = Q // EDGE
    last_group = group == GROUPS - 1
    at = lambda i: chunks - 1 - i
    block = lambda cols, g=0: pl.BlockSpec((Q, cols), lambda i: (at(i), g))
    per_chunk = pl.BlockSpec((1, GT, STATE, TILE), lambda i: (at(i), group, 0, 0))
    dots = pl.BlockSpec((8, 128), lambda i: (at(i), 0))
    in_specs = [
        block(GW), fixed((EDGE, GW)), at_group(TAPS, group), at_group(1, group),
        block(GW, group), block(GW), block(GW), block(GW), block(BC), block(128),
        per_chunk, per_chunk, fixed((PIECES, STATE, TILE)),
    ]
    width = GW + BC if last_group else GW
    cols = GW + REST if last_group else GW
    out_specs = [block(cols), kept((8, GW)), kept((EDGE, width)), kept((8, width))]
    out_shape = [
        shape_of((length, cols), bf16), shape_of((8, GW)), shape_of((EDGE, width)), shape_of((8, width)),
    ]
    scratch = [pltpu.VMEM((GT, STATE, TILE), f32), pltpu.VMEM((8, width), f32)]
    if last_group:
        in_specs += [
            block(REST),
            pl.BlockSpec((EDGE, REST), lambda i: (jnp.maximum(at(i) * per - 1, 0), 0)),
            fixed((EDGE, REST)), fixed((TAPS, BC)), fixed((1, BC)), fixed((8, 128)),
            block(128), block(128), block(128), block(128), dots, block(STATE), block(BC), block(BC),
        ]
        out_specs += [kept((8, BC)), kept((8, 128))]
        out_shape += [shape_of((8, BC)), shape_of((8, 128))]
        scratch += [pltpu.VMEM((Q, 128), f32), pltpu.VMEM((8, 128), f32), pltpu.VMEM((Q, STATE), f32)]
    else:
        out_specs += [block(128), dots, block(STATE)]
        out_shape += [shape_of((length, 128)), shape_of((8 * chunks, 128)), shape_of((length, STATE))]
    return pl.pallas_call(
        functools.partial(back_kernel, group),
        grid=(chunks,),
        in_specs=in_specs,
        out_specs=out_specs,
        out_shape=out_shape,
        scratch_shapes=scratch,
        compiler_params=cparams(),
        cost_estimate=cost(2 * 10**10, 20),
        name="backward",
    )(proj, proj_edge, taps, skip, dy, du, slope, x_act, bc_act, aux, ends, back_states, leaving, *others)


def quarters(left, order):
    rows = left.shape[1] // 4
    block = [lax.dynamic_slice_in_dim(left, order[k] * rows, rows, axis=1) for k in range(4)]
    return jnp.concatenate([block[1], block[3]], axis=1), jnp.concatenate([block[0], block[2]], axis=1)


def weight_grad(parts, right):
    sent, held = parts
    return dot_rows(right, sent).astype(bf16), dot_rows(right, held).astype(bf16)


def out_weight_sums(parts, right):
    sent, held = parts
    return dot_rows(sent, right).astype(bf16), dot_rows(held, right).astype(bf16)


def input_kernel(
    order, grad_gate, grad_x0, grad_x1, tokens, cot, gain,
    g0, g1, g2, g3, a0, a1, a2, a3, b0, b1, b2, b3, out, gain_grad,
):
    rows = g0.shape[0]

    @pl.when(pl.program_id(0) == 0)
    def _():
        gain_grad[...] = jnp.zeros_like(gain_grad)

    for k, (gate_w, a_w, b_w) in enumerate(((g0, a0, b0), (g1, a1, b1), (g2, a2, b2), (g3, a3, b3))):
        cols = pl.ds(pl.multiple_of(order[k] * rows, rows), rows)
        total = dot_lanes(grad_gate[...], gate_w[...]) + dot_lanes(grad_x0[...], a_w[:, :GW])
        total = total + dot_lanes(grad_x1[:, :GW], b_w[...])
        out[:, cols] = total + dot_lanes(grad_x1[:, GW:], a_w[:, GW:])
    grad = out[...]
    wide = tokens[...].astype(f32)
    width = wide.shape[1]
    scale = lax.rsqrt(jnp.mean(wide * wide, axis=1, keepdims=True) + EPS)
    gain_grad[...] += jnp.sum(grad * wide * scale, axis=0, keepdims=True)
    scaled = grad * gain[...]
    shared = jnp.sum(scaled * wide, axis=1, keepdims=True) / width
    out[...] = cot[...].astype(f32) + (scale * scaled - wide * (scale * scale * scale * shared))


def input_back(order, grad_gate, grad_x0, grad_x1, tokens, cot, gain, gate_pieces, a_pieces, b_pieces):
    length, width = tokens.shape
    rows = width // 4
    return pl.pallas_call(
        input_kernel,
        grid_spec=pltpu.PrefetchScalarGridSpec(
            num_scalar_prefetch=1,
            grid=(length // Q,),
            in_specs=[rows_of(INNER), rows_of(GW), rows_of(GW + REST), rows_of(width), rows_of(width), fixed((1, width))]
            + [fixed((rows, INNER))] * 4
            + [fixed((rows, GW + REST))] * 4
            + [fixed((rows, GW))] * 4,
            out_specs=[rows_of(width), kept((1, width))],
        ),
        out_shape=[shape_of((length, width)), shape_of((1, width))],
        compiler_params=cparams(),
        cost_estimate=cost(2 * length * width * (INNER + XCOLS), 26),
        name="input_back",
    )(order, grad_gate, grad_x0, grad_x1, tokens, cot, gain, *gate_pieces, *a_pieces, *b_pieces)


def swap(value, axis, bit):
    count = lax.axis_size(axis)
    return lax.ppermute(value, axis, [(i, i ^ bit) for i in range(count)])


def exchange(value, axis):
    return lax.all_to_all(value, axis, split_axis=0, concat_axis=0, tiled=True)


def tie(value, *others):
    return lax.optimization_barrier((value, others))[0]


def to_owners(value, groups=1):
    count = lax.axis_size("seq")
    pieces, rows, lanes = value.shape
    if count != pieces:
        lanes //= groups
        width = pieces * lanes // count
        split = value.reshape(pieces, rows, groups, lanes // width, width)
        value = split.transpose(0, 3, 1, 2, 4).reshape(count, rows, groups * width)
    return exchange(value, "seq")


def from_owners(value, groups=1, pieces=PIECES, lanes=128):
    value = exchange(value, "seq")
    count, rows, width = value.shape
    if count == pieces:
        return value
    width //= groups
    split = value.reshape(pieces, lanes // width, rows, groups, width)
    return split.transpose(0, 2, 3, 1, 4).reshape(pieces, rows, groups * lanes)


def send_core(grads):
    sent, held = grads
    return held, swap(sent, "wshard", 1)


def send_x(state, axis=1):
    held, got = state
    own, other = jnp.split(held, 2, axis=axis)
    got_own, got_other = jnp.split(got, 2, axis=axis)
    return (
        own.astype(f32) + got_own.astype(f32),
        swap((other.astype(f32) + got_other.astype(f32)).astype(bf16), "wshard", 2),
    )


def sum_pair(state):
    mine, got = state
    return mine + got.astype(f32)


def fold(value):
    rows, cols = value.shape
    return value.reshape(rows, cols // TILE, TILE).swapaxes(0, 1).reshape(-1, TILE)


def unfold(value, cols):
    return value.reshape(cols // TILE, -1, TILE).swapaxes(0, 1).reshape(-1, cols)


def send_near_pair(even, odd):
    is_even = (lax.axis_index("seq") & 1) == 0
    theirs = jnp.where(is_even, odd, even).astype(bf16)
    return jnp.where(is_even, even, odd), swap(theirs, "seq", 1)


def send_near(state):
    mine, got = state
    total = mine + got.astype(f32)
    half = total.shape[0] // 2
    bit = lax.axis_index("seq") & 1
    theirs = lax.dynamic_slice_in_dim(total, (1 - bit) * half, half, axis=0).astype(bf16)
    return lax.dynamic_slice_in_dim(total, bit * half, half, axis=0), swap(theirs, "seq", 1)


def send_far(state):
    mine, got = state
    total = mine + got.astype(f32)
    group = lax.axis_size("seq") // 2
    place = lax.axis_index("seq") >> 1
    part = total.shape[0] // group
    piece = lambda k: lax.dynamic_slice_in_dim(total, (place ^ k) * part, part, axis=0)
    return piece(0), [swap(piece(k).astype(bf16), "seq", 2 * k) for k in range(1, group)]


def share_far(state):
    mine, got = state
    owned = (mine + sum(piece.astype(f32) for piece in got)).astype(bf16)
    return [owned] + [swap(owned, "seq", 2 * k) for k in range(1, len(got) + 1)]


def in_order(pieces, place, join=True):
    bit = 1
    while bit < len(pieces):
        odd = (place & bit) != 0
        pieces = [jnp.where(odd, pieces[k ^ bit], pieces[k]) for k in range(len(pieces))]
        bit *= 2
    return jnp.concatenate(pieces, axis=0) if join else pieces


def share_near(pieces):
    half = in_order(pieces, lax.axis_index("seq") >> 1)
    return [half, swap(half, "seq", 1)]


def whole_rows(pieces):
    return in_order(pieces, lax.axis_index("seq") & 1)


def local(
    block_in, norm_gain, in_weight, conv_x, conv_x_bias, conv_bc, conv_bc_bias,
    a_log, skip, dt_bias, out_gain, out_weight, cotangent,
):
    tokens = block_in[0]
    cot = cotangent[0]
    length, width = tokens.shape
    seq = lax.axis_size("seq")
    shards = lax.axis_size("wshard")
    own_heads = HEADS // seq
    own_ch = INNER // seq
    me = lax.axis_index("wshard")
    order = jnp.stack([me ^ k for k in range(4)]).astype(jnp.int32)
    place = lax.axis_index("seq")

    a_piece = jnp.concatenate(
        [in_weight[:, INNER : INNER + GW], jnp.pad(in_weight[:, 2 * INNER :], ((0, 0), (0, XCOLS - XUSED)))], axis=1
    )
    b_piece = in_weight[:, INNER + GW : 2 * INNER]
    gate_piece = in_weight[:, :INNER]
    edge = lax.ppermute(tokens[length - EDGE :], "seq", [(i, i + 1) for i in range(seq - 1)])
    small = jnp.concatenate(
        [
            conv_x,
            conv_x_bias[None],
            jnp.pad(jnp.stack([a_log, skip, dt_bias]), ((0, 0), (0, own_ch - own_heads))),
        ],
        axis=0,
    )
    a_across, a_beside = swap(a_piece, "wshard", 2), swap(a_piece, "wshard", 1)
    small_all = exchange(jnp.broadcast_to(small[None], (seq,) + small.shape), "seq")
    x_params = small_all[:, :5].transpose(1, 0, 2).reshape(5, INNER)
    head_params = small_all[:, 5:, :own_heads].transpose(1, 0, 2).reshape(3, HEADS)
    taps, bias = x_params[:4], x_params[4:5]
    heads = jnp.pad(head_params, ((0, 5), (0, 128 - HEADS)))
    skip_row = jnp.repeat(head_params[1], INNER // HEADS)[None]
    bias_bc = conv_bc_bias[None]
    a_across = tie(a_across, small_all, edge, a_beside)
    a_pieces = (a_piece, a_beside, a_across, swap(a_across, "wshard", 1))
    b_piece, gate_piece, out_piece = tie((b_piece, gate_piece, out_weight), a_across)
    b_across, b_beside = swap(b_piece, "wshard", 2), swap(b_piece, "wshard", 1)

    normed, proj0, rest, proj_edge0, rest_edge = project(order, tokens, edge, norm_gain[None], a_pieces)
    gate_across, gate_beside = swap(gate_piece, "wshard", 2), swap(gate_piece, "wshard", 1)
    out_across, out_beside = swap(out_piece, "wshard", 2), swap(out_piece, "wshard", 1)
    bc_act, aux, cum_t = factors(rest, rest_edge, conv_bc, bias_bc, heads)
    b_across = tie(b_across, bc_act)
    b_pieces = (b_piece, b_beside, b_across, swap(b_across, "wshard", 1))
    x_act0, local0, payload0 = states(0, proj0, proj_edge0, taps, bias, bc_act, aux)
    arrived0 = to_owners(payload0)
    proj1, proj_edge1 = project_more(order, tie(normed, payload0), edge, norm_gain[None], b_pieces)
    x_act1, local1, payload1 = states(1, proj1, proj_edge1, taps, bias, bc_act, aux)
    arrived1 = to_owners(payload1)
    y0 = within(0, tie(x_act0, payload1), bc_act, aux, cum_t, skip_row)
    gate_pieces = (gate_piece, gate_beside, gate_across, swap(gate_across, "wshard", 1))
    gate = gate_project(order, tie(normed, y0), gate_pieces)
    entering0 = chain(True, *tie((arrived0, arrived0[:, STATE:, :]), gate))
    totals0, totals1 = arrived0[:, STATE:, :], arrived1[:, STATE:, :]
    back0 = from_owners(entering0)
    entering1 = chain(True, *tie((arrived1, totals1), entering0))
    back1 = from_owners(entering1)
    y1 = within(1, tie(x_act1, entering1), bc_act, aux, cum_t, skip_row)
    entering0, entering1 = tie((back0, back1), y1)
    out_pieces = (out_piece, out_beside, out_across, swap(out_across, "wshard", 1))
    (normed_out, output, dy, grad_gate, ends, back_states, begin, back_payload, y_dot, out_gain_grad) = middle(
        order, (y0, y1), bc_act, aux, (local0, local1), (entering0, entering1), gate, tokens, cot, out_gain[None], out_pieces
    )

    back_arrived = to_owners(back_payload, 2)
    totals = jnp.concatenate([totals0, totals1], axis=2)
    normed_parts = quarters(normed, order)
    out_grads = out_weight_sums(quarters(normed_out, order), cot)
    out_core = send_core(out_grads)
    gate_grads = weight_grad(normed_parts, tie(grad_gate, out_grads))
    gate_core = send_core(gate_grads)
    du0, slope0, grad_bc0, k_dot0 = within_back(
        0, tie(x_act0, gate_grads), bc_act, aux, cum_t, dy, proj0, proj_edge0, taps, bias, ends, begin
    )
    out_x = send_x(tie(out_core, du0), axis=0)
    gate_x = send_x(tie(gate_core, out_x[0]))
    leaving = chain(False, *tie((back_arrived, totals), gate_x[0]))
    leave = from_owners(leaving, 2)
    du1, slope1, grad_bc1, k_dot1 = within_back(
        1, tie(x_act1, leaving), bc_act, aux, cum_t, dy, proj1, proj_edge1, taps, bias, ends, begin
    )
    out_fold = fold(sum_pair(tie(out_x, du1)))
    leave = tie(leave, out_fold)
    grad_x0, grad_taps0, tail0, start0, x_dot0, edge_dot0, b_sum0 = backward(
        0, proj0, proj_edge0, taps, skip_row, dy, du0, slope0, x_act0, bc_act, aux, ends, back_states, leave
    )
    all_taps = jnp.concatenate([taps[:, GW:], conv_bc], axis=1)
    backwards = [(i, i - 1) for i in range(1, seq)]

    def fix(grad, tail, start, tap_values):
        fixes = [
            tail[EDGE - 3 + a] + sum(tap_values[k] * start[a - k] for k in range(a + 1)) for a in range(3)
        ]
        fixed_rows = jnp.concatenate([tail[: EDGE - 3], jnp.stack(fixes)], axis=0).astype(bf16)
        return lax.dynamic_update_slice(grad, fixed_rows, (length - EDGE, 0))

    after0 = lax.ppermute(start0, "seq", backwards)
    gate_pair = sum_pair(tie(gate_x, grad_x0))
    early_near = send_near_pair(gate_pair, out_fold)
    grad_x0 = fix(tie(grad_x0, early_near[0]), tail0, after0, taps[:, :GW])
    x0_grads = weight_grad(normed_parts, grad_x0)
    x0_core = send_core(x0_grads)
    x0_x = send_x(x0_core)
    grad_x1, grad_taps1, tail1, start1, grad_taps_bc, grad_heads = backward(
        1, proj1, proj_edge1, taps, skip_row, tie(dy, x0_x[0]), du1, slope1, x_act1, bc_act, aux, ends, back_states,
        leave,
        (rest, rest, rest_edge, conv_bc, bias_bc, heads, y_dot, k_dot0, k_dot1, x_dot0, edge_dot0, b_sum0, grad_bc0, grad_bc1),
    )
    x0_near = send_near(tie(x0_x, grad_x1))
    early_far = send_far(tie(early_near, x0_near[0]))
    after1 = lax.ppermute(tie(start1, x0_near[0]), "seq", backwards)
    grad_x1 = fix(tie(grad_x1, early_far[0]), tail1, after1, all_taps)
    x1_grads = weight_grad(normed_parts, grad_x1)
    x1_core = send_core(x1_grads)
    x0_far = send_far(tie(x0_near, x1_grads))
    x1_x = send_x(tie(x1_core, x0_far[0]))
    early_all = share_far(tie(early_far, x1_x[0]))
    x0_all = share_far(tie(x0_far, early_all[0]))
    input_grad, norm_gain_grad = input_back(
        order, tie(grad_gate, x0_all[0]), grad_x0, grad_x1, tokens, cot, norm_gain[None], gate_pieces, a_pieces, b_pieces
    )
    x1_near = send_near(tie(x1_x, input_grad))
    norm_gain_grad = tie(norm_gain_grad, x1_near[0])
    grad_taps = jnp.concatenate([grad_taps0, grad_taps1], axis=1)
    shared = jnp.concatenate(
        [norm_gain_grad[0], out_gain_grad[0], grad_taps_bc[:5].reshape(-1)]
    )
    mine = jnp.concatenate(
        [
            grad_taps[:5].reshape(5, seq, own_ch).transpose(1, 0, 2).reshape(seq, 5 * own_ch),
            grad_heads[:3, :HEADS].reshape(3, seq, own_heads).transpose(1, 0, 2).reshape(seq, 3 * own_heads),
        ],
        axis=1,
    )
    shared_size, mine_size = shared.shape[0], mine.shape[1]
    pad = -(shared_size + mine_size) % 1024
    small_out = jnp.concatenate(
        [jnp.broadcast_to(shared[None], (seq, shared_size)), mine, jnp.zeros((seq, pad), f32)], axis=1
    )
    small_out = jnp.broadcast_to(small_out[:, None], (seq, shards, small_out.shape[1]))
    small_sum = jnp.sum(
        exchange(small_out.reshape(seq * shards, 8, -1), ("seq", "wshard")), axis=0
    ).reshape(-1)
    early_half = share_near(tie(early_all, small_out))
    x0_half = share_near(tie(x0_all, early_half[0]))
    x1_far = send_far(tie(x1_near, x0_half[0]))
    x1_all = share_far(x1_far)
    x1_half = share_near(tie(x1_all, small_sum, early_half[1]))
    gate_sum, out_sum = in_order(early_half, place & 1, join=False)
    out_owned = unfold(out_sum, width).astype(f32)
    in_owned = jnp.concatenate(
        [gate_sum, whole_rows(x0_half), whole_rows(x1_half)[: XUSED - GW]], axis=0
    ).astype(f32).T
    pos = [0]

    def take(shape):
        size = 1
        for extent in shape:
            size *= extent
        out = small_sum[pos[0] : pos[0] + size].reshape(shape)
        pos[0] += size
        return out

    norm_gain_sum = take((width,))
    out_gain_sum = take((INNER,))
    bc_sum = take((5, BC))
    x_sum = take((5, own_ch))
    head_sum = take((3, own_heads))
    return (
        output[None],
        input_grad[None],
        norm_gain_sum,
        in_owned,
        x_sum[:4],
        x_sum[4],
        bc_sum[:4],
        bc_sum[4],
        head_sum[0],
        head_sum[1],
        head_sum[2],
        out_gain_sum,
        out_owned,
    )


def solution(mesh):
    in_specs = (
        P("wshard", "seq", None),
        P(),
        P("wshard", None),
        P(None, "seq"),
        P("seq"),
        P(),
        P(),
        P("seq"),
        P("seq"),
        P("seq"),
        P(),
        P("wshard", None),
        P("wshard", "seq", None),
    )
    out_specs = (
        P("wshard", "seq", None),
        P("wshard", "seq", None),
        P(),
        P("wshard", None),
        P(None, "seq"),
        P("seq"),
        P(),
        P(),
        P("seq"),
        P("seq"),
        P("seq"),
        P(),
        P("wshard", None),
    )
    return jax.shard_map(local, mesh=mesh, in_specs=in_specs, out_specs=out_specs, check_vma=False)
```

```python
import functools

import jax
import jax.numpy as jnp
from jax import lax
from jax.experimental import pallas as pl
from jax.experimental.pallas import tpu as pltpu
from jax.sharding import PartitionSpec as P

INNER = 2048
STATE = 128
HEADS = 32
TAPS = 4
BC = 2 * STATE
CH = INNER + BC
XCOLS = 2432
XUSED = 2336
Q = 256
HALF = Q // 2
TILE = 256
TILES = INNER // TILE
GROUPS = 2
GT = TILES // GROUPS
GW = INNER // GROUPS
REST = XCOLS - INNER
PIECES = 2 * GT
EDGE = 16
EPS = 1e-05

f32 = jnp.float32
bf16 = jnp.bfloat16
highest = lax.Precision.HIGHEST


def cparams(megabytes=56):
    return pltpu.CompilerParams(
        dimension_semantics=("arbitrary",), vmem_limit_bytes=megabytes * 2**20
    )


def dot(a, b):
    return lax.dot_general(a, b, (((1,), (0,)), ((), ())), preferred_element_type=f32)


def dot_lanes(a, b):
    return lax.dot_general(a, b, (((1,), (1,)), ((), ())), preferred_element_type=f32)


def dot_rows(a, b):
    return lax.dot_general(a, b, (((0,), (0,)), ((), ())), preferred_element_type=f32)


def sigmoid(v):
    return 0.5 * jnp.tanh(0.5 * v) + 0.5


def lane_iota(rows, lanes):
    return lax.broadcasted_iota(jnp.int32, (rows, lanes), 1)


def row_iota(rows, lanes):
    return lax.broadcasted_iota(jnp.int32, (rows, lanes), 0)


def spread(terms, width, first, shift):
    rows = row_iota(terms * HEADS, width) & (HEADS - 1)
    return jnp.where(rows == first + (lane_iota(terms * HEADS, width) >> shift), 1.0, 0.0).astype(bf16)


def halves(value):
    high = value.astype(bf16)
    return high, (value - high.astype(f32)).astype(bf16)


def terms2(value):
    return jnp.concatenate(halves(value), axis=1)


def terms4(value):
    high = value.astype(bf16)
    rest = value - high.astype(f32)
    middle, low = halves(rest)
    return jnp.concatenate([high, middle, low, jnp.zeros_like(high)], axis=1)


def split_dot(value, select):
    high = value.astype(bf16)
    low = (value - high.astype(f32)).astype(bf16)
    return dot(high, select) + dot(low, select)


def fine(product, a, b):
    a_high, a_low = halves(a)
    b_high, b_low = halves(b)
    return product(a_high, b_high) + (product(a_high, b_low) + product(a_low, b_high))


def fine_with(product, a_terms, b):
    a_high, a_low = a_terms
    b_high, b_low = halves(b)
    return product(a_high, b_high) + (product(a_high, b_low) + product(a_low, b_high))


def fine_short(a_terms, b):
    a_high, a_both = a_terms
    b_high, b_low = halves(b)
    return dot(a_both, jnp.concatenate([b_high, b_high], axis=0)) + dot(a_high, b_low)


def head_select(tile):
    lanes = row_iota(TILE, 128) >> 6
    return jnp.where(lanes + tile * (TILE // 64) == lane_iota(TILE, 128), 1.0, 0.0).astype(bf16)


def shifted(current, before):
    joined = jnp.concatenate([before[EDGE - 8 :], current], axis=0)
    rows = current.shape[0]
    return [joined[5 + k : 5 + k + rows] for k in range(TAPS - 1)] + [current]


def conv_of(parts, taps, bias):
    total = bias + taps[0:1] * parts[0]
    for k in range(1, TAPS):
        total = total + taps[k : k + 1] * parts[k]
    return total


def later_rows(grad, after):
    joined = jnp.concatenate([grad, after], axis=0)
    rows = grad.shape[0]
    return [joined[TAPS - 1 - k : TAPS - 1 - k + rows] for k in range(TAPS - 1)] + [grad]


def tap_sums(parts, raw, grad, early):
    first = grad[:8]
    sums = []
    for k in range(TAPS):
        total = jnp.sum(parts[k] * raw, axis=0, keepdims=True)
        if k < TAPS - 1:
            total = total + jnp.sum(first[: TAPS - 1 - k] * early[8 - TAPS + 1 + k :], axis=0, keepdims=True)
        sums.append(total)
    sums.append(jnp.sum(grad, axis=0, keepdims=True))
    sums.append(jnp.zeros((3, grad.shape[1]), f32))
    return jnp.concatenate(sums, axis=0)


def tile_at(j, width=TILE):
    return pl.ds(pl.multiple_of(j * width, width), width)


def assemble(order, pieces, full):
    rows = pieces[0].shape[0]
    for k, piece in enumerate(pieces):
        full[pl.ds(pl.multiple_of(order[k] * rows, rows), rows), :] = piece[...]


def norm_rows(values, gain):
    wide = values.astype(f32)
    scale = lax.rsqrt(jnp.mean(wide * wide, axis=1, keepdims=True) + EPS)
    return (wide * scale * gain).astype(bf16)


def project_kernel(order, tokens, edge, gain, w0, w1, w2, w3, normed, out, out_rest, out_edge, out_edge_rest, full):
    @pl.when(pl.program_id(0) == 0)
    def _():
        assemble(order, (w0, w1, w2, w3), full)
        early = dot(norm_rows(edge[...], gain[...]), full[...]).astype(bf16)
        out_edge[...] = early[:, :GW]
        out_edge_rest[...] = early[:, GW:]

    now = norm_rows(tokens[...], gain[...])
    normed[...] = now
    for start in range(0, GW, TILE):
        out[:, start : start + TILE] = dot(now, full[:, start : start + TILE]).astype(bf16)
    out_rest[...] = dot(now, full[:, GW:]).astype(bf16)


def project_more_kernel(order, normed, edge, gain, w0, w1, w2, w3, out, out_edge, full):
    @pl.when(pl.program_id(0) == 0)
    def _():
        assemble(order, (w0, w1, w2, w3), full)
        out_edge[...] = dot(norm_rows(edge[...], gain[...]), full[...]).astype(bf16)

    for start in range(0, GW, TILE):
        out[:, start : start + TILE] = dot(normed[...], full[:, start : start + TILE]).astype(bf16)


def fixed(shape):
    return pl.BlockSpec(shape, lambda i, *o: (0,) * len(shape), pipeline_mode=pl.Buffered(1))


def kept(shape):
    return pl.BlockSpec(shape, lambda i, *o: (0,) * len(shape))


def rows_of(cols, group=0):
    return pl.BlockSpec((Q, cols), lambda i, *o: (i, group))


def shape_of(shape, dtype=f32):
    return jax.ShapeDtypeStruct(shape, dtype)


def cost(flops, megabytes):
    return pl.CostEstimate(flops=int(flops) // 1, bytes_accessed=int(megabytes * 2**20) // 1, transcendentals=0)


def project(order, tokens, edge, gain, pieces):
    length, width = tokens.shape
    rows = pieces[0].shape[0]
    return pl.pallas_call(
        project_kernel,
        grid_spec=pltpu.PrefetchScalarGridSpec(
            num_scalar_prefetch=1,
            grid=(length // Q,),
            in_specs=[rows_of(width), fixed((EDGE, width)), fixed((1, width))] + [fixed((rows, GW + REST))] * 4,
            out_specs=[rows_of(width), rows_of(GW), rows_of(REST), kept((EDGE, GW)), kept((EDGE, REST))],
            scratch_shapes=[pltpu.VMEM((4 * rows, GW + REST), bf16)],
        ),
        out_shape=[
            shape_of((length, width), bf16),
            shape_of((length, GW), bf16),
            shape_of((length, REST), bf16),
            shape_of((EDGE, GW), bf16),
            shape_of((EDGE, REST), bf16),
        ],
        compiler_params=cparams(),
        cost_estimate=cost(2 * length * width * (GW + REST), 9),
        name="project",
    )(order, tokens, edge, gain, *pieces)


def project_more(order, normed, edge, gain, pieces):
    length, width = normed.shape
    rows = pieces[0].shape[0]
    return pl.pallas_call(
        project_more_kernel,
        grid_spec=pltpu.PrefetchScalarGridSpec(
            num_scalar_prefetch=1,
            grid=(length // Q,),
            in_specs=[rows_of(width), fixed((EDGE, width)), fixed((1, width))] + [fixed((rows, GW))] * 4,
            out_specs=[rows_of(GW), kept((EDGE, GW))],
            scratch_shapes=[pltpu.VMEM((4 * rows, GW), bf16)],
        ),
        out_shape=[shape_of((length, GW), bf16), shape_of((EDGE, GW), bf16)],
        compiler_params=cparams(),
        cost_estimate=cost(2 * length * width * GW, 6),
        name="project_more",
    )(order, normed, edge, gain, *pieces)


def gate_kernel(order, normed, w0, w1, w2, w3, out, full):
    @pl.when(pl.program_id(0) == 0)
    def _():
        assemble(order, (w0, w1, w2, w3), full)

    for j in range(TILES):
        cols = slice(j * TILE, (j + 1) * TILE)
        out[:, cols] = dot(normed[...], full[:, cols]).astype(bf16)


def gate_project(order, normed, pieces):
    length, width = normed.shape
    rows = pieces[0].shape[0]
    return pl.pallas_call(
        gate_kernel,
        grid_spec=pltpu.PrefetchScalarGridSpec(
            num_scalar_prefetch=1,
            grid=(length // Q,),
            in_specs=[rows_of(width)] + [fixed((rows, INNER))] * 4,
            out_specs=rows_of(INNER),
            scratch_shapes=[pltpu.VMEM((4 * rows, INNER), bf16)],
        ),
        out_shape=shape_of((length, INNER), bf16),
        compiler_params=cparams(),
        cost_estimate=cost(2 * length * width * INNER, 10),
        name="gate_project",
    )(order, normed, *pieces)


def factors_kernel(now, prior, edge, taps_bc, bias_bc, heads, bc_act, aux_out, cum_t):
    first = pl.program_id(0) == 0
    early = jnp.where(first, edge[:, :BC], prior[:, :BC]).astype(f32)
    pre = conv_of(shifted(now[:, :BC].astype(f32), early), taps_bc[...], bias_bc[...])
    bc_act[...] = pre * sigmoid(pre)
    raw = now[:, BC : BC + HEADS].astype(f32) + heads[2:3, :HEADS]
    step = jnp.maximum(raw, 0.0) + jnp.log1p(jnp.exp(-jnp.abs(raw)))
    decay = -jnp.exp(heads[0:1, :HEADS]) * step
    lower = jnp.where(row_iota(Q, Q) >= lane_iota(Q, Q), 1.0, 0.0)
    cumulative = jnp.dot(lower, decay, precision=highest, preferred_element_type=f32)
    last = cumulative[Q - 1 : Q]
    aux = jnp.concatenate([cumulative, step, jnp.exp(last - cumulative), jnp.exp(cumulative)], axis=1)
    aux_out[...] = aux
    cum_t[...] = aux.T[:HEADS]


def states_kernel(
    group, now, prior, edge, taps, bias, bc_act, aux, x_act, local, payload, run, total, b_rows
):
    c = pl.program_id(0)
    first = c == 0

    @pl.when(first)
    def _():
        run[...] = jnp.zeros_like(run)
        total[...] = jnp.zeros_like(total)

    b_rows[...] = bc_act[:, :STATE].T
    weight2 = terms2(aux[:, HEADS : 2 * HEADS] * aux[:, 2 * HEADS : 3 * HEADS])
    ends4 = terms4(jnp.concatenate([aux[Q - 8 :, 3 * HEADS :], aux[Q - 8 :, :HEADS]], axis=0))

    def body(j, carry):
        cols = tile_at(j)
        early = jnp.where(first, edge[:, cols], prior[:, cols]).astype(f32)
        pre = conv_of(shifted(now[:, cols].astype(f32), early), taps[:, cols], bias[:, cols])
        x = pre * sigmoid(pre)
        x_act[:, cols] = x
        lead = 4 * (j + group * GT)
        state = fine(dot, b_rows[...], x * dot(weight2, spread(2, TILE, lead, 6)))
        local[0, j] = state
        end = dot(ends4, spread(4, TILE, lead, 6))
        run[j] = end[7:8] * run[j] + state
        total[:, cols] += end[15:16]
        return carry

    lax.fori_loop(0, GT, body, 0, unroll=GT)

    @pl.when(c == pl.num_programs(0) - 1)
    def _():
        for j in range(2 * GT):
            lanes = slice(128 * (j % 2), 128 * (j % 2) + 128)
            payload[j, :STATE, :] = run[j // 2, :, lanes]
            payload[j, STATE:, :] = jnp.broadcast_to(total[:, j * 128 : (j + 1) * 128], (8, 128))


def prior_rows(cols, group=0):
    per = Q // EDGE
    return pl.BlockSpec((EDGE, cols), lambda i, *o: (jnp.maximum(i * per - 1, 0), group))


def at_group(rows, group):
    return pl.BlockSpec((rows, GW), lambda i, *o: (0, group), pipeline_mode=pl.Buffered(1))


def factors(rest, rest_edge, taps_bc, bias_bc, heads):
    length = rest.shape[0]
    return pl.pallas_call(
        factors_kernel,
        grid=(length // Q,),
        in_specs=[
            rows_of(REST), prior_rows(REST), fixed((EDGE, REST)),
            fixed((TAPS, BC)), fixed((1, BC)), fixed((8, 128)),
        ],
        out_specs=[rows_of(BC), rows_of(128), pl.BlockSpec((HEADS, Q), lambda i: (0, i))],
        out_shape=[shape_of((length, BC)), shape_of((length, 128)), shape_of((HEADS, length))],
        compiler_params=cparams(),
        cost_estimate=cost(10**9, 4),
        name="factors",
    )(rest, rest, rest_edge, taps_bc, bias_bc, heads)


def states(group, proj, proj_edge, taps, bias, bc_act, aux):
    length = proj.shape[0]
    chunks = length // Q
    return pl.pallas_call(
        functools.partial(states_kernel, group),
        grid=(chunks,),
        in_specs=[
            rows_of(GW), prior_rows(GW), fixed((EDGE, GW)),
            at_group(TAPS, group), at_group(1, group), rows_of(BC), rows_of(128),
        ],
        out_specs=[
            rows_of(GW),
            pl.BlockSpec((1, GT, STATE, TILE), lambda i: (i, 0, 0, 0)),
            kept((2 * GT, STATE + 8, 128)),
        ],
        out_shape=[
            shape_of((length, GW)),
            shape_of((chunks, GT, STATE, TILE)),
            shape_of((2 * GT, STATE + 8, 128)),
        ],
        scratch_shapes=[
            pltpu.VMEM((GT, STATE, TILE), f32),
            pltpu.VMEM((1, GW), f32),
            pltpu.VMEM((STATE, Q), f32),
        ],
        compiler_params=cparams(),
        cost_estimate=cost(10**10, 10),
        name="states",
    )(proj, proj, proj_edge, taps, bias, bc_act, aux)


def chain_kernel(forward, values, totals, out):
    count = out.shape[0]
    order = range(count) if forward else range(count - 1, -1, -1)
    state = jnp.zeros(out.shape[1:], f32)
    for i in order:
        out[i] = state
        state = jnp.exp(totals[i, 0:1, :]) * state + values[i, :STATE, :]


def chain(forward, values, totals):
    count, _, width = values.shape
    return pl.pallas_call(
        functools.partial(chain_kernel, forward),
        out_shape=jax.ShapeDtypeStruct((count, STATE, width), f32),
        compiler_params=pltpu.CompilerParams(vmem_limit_bytes=56 * 2**20),
        cost_estimate=cost(10**8, 3),
        name="chain",
    )(values, totals)


def within_kernel(group, x_act, bc_act, aux, cum_t, skip, out, scores, columns):
    lower = row_iota(HALF, HALF) >= lane_iota(HALF, HALF)
    for b in range(2):
        rows = slice(b * HALF, (b + 1) * HALF)
        scores[rows, :] = jnp.where(lower, fine(dot_lanes, bc_act[rows, STATE:], bc_act[rows, :STATE]), 0.0)
    cross_high, cross_low = halves(fine(dot_lanes, bc_act[HALF:, STATE:], bc_act[:HALF, :STATE]))
    cross2 = jnp.concatenate([cross_high, cross_low], axis=1)
    cumulative = aux[:, :HEADS]
    middle_row = cumulative[HALF - 1 : HALF]
    step2 = terms2(aux[:, HEADS : 2 * HEADS])
    bridge2 = terms2(jnp.exp(jnp.concatenate([middle_row - cumulative[:HALF], cumulative[HALF:] - middle_row], axis=0)))
    cumulative4 = terms4(cumulative)
    for j in range(GT):
        columns[:, j * 512 : (j + 1) * 512] = dot(cumulative4, spread(4, 512, 4 * (j + group * GT), 7))
    low = lane_iota(HALF, HALF) < 64

    def body(j, carry):
        cols = tile_at(j)
        x = x_act[:, cols]
        select = spread(2, TILE, 4 * (j + group * GT), 6)
        u = x * dot(step2, select)
        bridge = dot(bridge2, select)
        u_high, u_low = halves(u)
        v_high, v_low = halves(u[:HALF] * bridge[:HALF])
        across = dot(cross2, jnp.concatenate([v_high, v_high], axis=0)) + dot(cross_high, v_low)
        across = across * bridge[HALF:]
        direct = skip[:, cols] * x
        for pair in range(2):
            lanes = slice(pair * 128, (pair + 1) * 128)
            place = pl.ds(pl.multiple_of(j * TILE + pair * 128, 128), 128)
            for b in range(2):
                rows = slice(b * HALF, (b + 1) * HALF)
                weights = []
                for i in range(2):
                    head = 4 * j + 2 * pair + i
                    column = columns[rows, pl.ds(pl.multiple_of(head * 128, 128), 128)]
                    row = cum_t[pl.ds(head + 4 * GT * group, 1), :][:, rows]
                    weights.append(jnp.exp(jnp.minimum(column - row, 0.0)) * scores[rows, :])
                w_high, w_low = halves(jnp.concatenate(weights, axis=1))
                top = both_heads(low, u_high[rows, lanes])
                bottom = both_heads(low, u_low[rows, lanes])
                twice = dot(w_high, jnp.concatenate([top, bottom], axis=1))
                y = twice[:, :128] + twice[:, 128:] + dot(w_low, top) + direct[rows, lanes]
                if b == 1:
                    y = y + across[:, lanes]
                out[rows, place] = y
        return carry

    lax.fori_loop(0, GT, body, 0, unroll=GT)


def both_heads(low, value):
    zero = jnp.zeros_like(value)
    return jnp.concatenate([jnp.where(low, value, zero), jnp.where(low, zero, value)], axis=0)


def within(group, x_act, bc_act, aux, cum_t, skip):
    length = x_act.shape[0]
    return pl.pallas_call(
        functools.partial(within_kernel, group),
        grid=(length // Q,),
        in_specs=[
            rows_of(GW), rows_of(BC), rows_of(128),
            pl.BlockSpec((HEADS, Q), lambda i: (0, i)), at_group(1, group),
        ],
        out_specs=rows_of(GW),
        out_shape=shape_of((length, GW)),
        scratch_shapes=[pltpu.VMEM((Q, HALF), f32), pltpu.VMEM((Q, GT * 512), f32)],
        compiler_params=cparams(),
        cost_estimate=cost(10**10, 10),
        name="within",
    )(x_act, bc_act, aux, cum_t, skip)


def within_back_kernel(
    group, x_act, bc_act, aux, cum_t, dy, now, prior, edge, taps, bias, ends, entering,
    out, slope, out_bc, k_dot, scores, grad_scores, grad_cross, columns,
):
    first = pl.program_id(0) == 0
    k_dot[...] = jnp.zeros_like(k_dot)
    out_bc[:, STATE:] = jnp.zeros((Q, STATE), f32)
    upper = row_iota(HALF, HALF) <= lane_iota(HALF, HALF)
    act = bc_act[...].astype(bf16)
    b_act, c_act = act[:, :STATE], act[:, STATE:]
    for b in range(2):
        rows = slice(b * HALF, (b + 1) * HALF)
        scores[rows, :] = jnp.where(upper, dot_lanes(b_act[rows], c_act[rows]), 0.0)
    grad_scores[...] = jnp.zeros_like(grad_scores)
    grad_cross[...] = jnp.zeros_like(grad_cross)
    cross = dot_lanes(b_act[:HALF], c_act[HALF:]).astype(bf16)
    cumulative = aux[:, :HEADS]
    middle_row = cumulative[HALF - 1 : HALF]
    step2 = terms2(aux[:, HEADS : 2 * HEADS])
    decayed2 = terms2(aux[:, 3 * HEADS :])
    bridge2 = terms2(jnp.exp(jnp.concatenate([middle_row - cumulative[:HALF], cumulative[HALF:] - middle_row], axis=0)))
    cumulative4 = terms4(cumulative)
    for j in range(GT):
        columns[:, j * 512 : (j + 1) * 512] = dot(cumulative4, spread(4, 512, 4 * (j + group * GT), 7))
    low = lane_iota(HALF, HALF) < 64

    def body(j, carry):
        cols = tile_at(j)
        lead = 4 * (j + group * GT)
        select = spread(2, TILE, lead, 6)
        x = x_act[:, cols]
        u = x * dot(step2, select)
        bridge = dot(bridge2, select)
        u_low = u.astype(bf16)
        grad = dy[:, cols]
        wide = grad.astype(f32)
        early_raw = jnp.where(first, edge[:, cols], prior[:, cols]).astype(f32)
        pre = conv_of(shifted(now[:, cols].astype(f32), early_raw), taps[:, cols], bias[:, cols])
        sig = sigmoid(pre)
        slope[:, cols] = (sig + x * (1.0 - sig)).astype(bf16)
        k_dot[...] += split_dot(x * wide, head_select(j + group * GT))
        enter = jnp.where(first, entering[j], ends[0, j])
        out_bc[:, STATE:] += fine(dot_lanes, wide * dot(decayed2, select), enter)
        early = (u[:HALF] * bridge[:HALF]).astype(bf16)
        late = (grad[HALF:].astype(f32) * bridge[HALF:]).astype(bf16)
        grad_cross[...] += dot_lanes(early, late)
        across = dot(cross, late) * bridge[:HALF]
        totals = [None, None]
        for pair in range(2):
            lanes = slice(pair * 128, (pair + 1) * 128)
            place = pl.ds(pl.multiple_of(j * TILE + pair * 128, 128), 128)
            for b in range(2):
                rows = slice(b * HALF, (b + 1) * HALF)
                spaced = both_heads(low, grad[rows, lanes])
                products = dot_lanes(u_low[rows, lanes], spaced)
                weights = []
                for i in range(2):
                    head = 4 * j + 2 * pair + i
                    column = columns[rows, pl.ds(pl.multiple_of(head * 128, 128), 128)]
                    row = cum_t[pl.ds(head + 4 * GT * group, 1), :][:, rows]
                    weight = jnp.exp(jnp.minimum(row - column, 0.0))
                    part = weight * products[:, i * 128 : (i + 1) * 128]
                    totals[b] = part if totals[b] is None else totals[b] + part
                    weights.append((weight * scores[rows, :]).astype(bf16))
                du = dot(jnp.concatenate(weights, axis=1), spaced)
                if b == 0:
                    du = du + across[:, lanes]
                out[rows, place] = du.astype(bf16)
        for b in range(2):
            grad_scores[b * HALF : (b + 1) * HALF, :] += totals[b]
        return carry

    lax.fori_loop(0, GT, body, 0, unroll=GT)
    far = grad_cross[...].astype(bf16)
    near0 = jnp.where(upper, grad_scores[:HALF, :], 0.0).astype(bf16)
    near1 = jnp.where(upper, grad_scores[HALF:, :], 0.0).astype(bf16)
    out_bc[:HALF, :STATE] = dot(near0, c_act[:HALF]) + dot(far, c_act[HALF:])
    out_bc[HALF:, :STATE] = dot(near1, c_act[HALF:])
    out_bc[:HALF, STATE:] += dot_rows(near0, b_act[:HALF])
    out_bc[HALF:, STATE:] += dot_rows(near1, b_act[HALF:]) + dot_rows(far, b_act[:HALF])


def within_back(group, x_act, bc_act, aux, cum_t, dy, proj, proj_edge, taps, bias, ends, entering):
    length = x_act.shape[0]
    return pl.pallas_call(
        functools.partial(within_back_kernel, group),
        grid=(length // Q,),
        in_specs=[
            rows_of(GW), rows_of(BC), rows_of(128),
            pl.BlockSpec((HEADS, Q), lambda i: (0, i)), rows_of(GW, group),
            rows_of(GW), prior_rows(GW), fixed((EDGE, GW)),
            at_group(TAPS, group), at_group(1, group),
            pl.BlockSpec((1, GT, STATE, TILE), lambda i: (jnp.maximum(i - 1, 0), group, 0, 0)),
            pl.BlockSpec((GT, STATE, TILE), lambda i: (group, 0, 0), pipeline_mode=pl.Buffered(1)),
        ],
        out_specs=[rows_of(GW), rows_of(GW), rows_of(BC), rows_of(128)],
        out_shape=[
            shape_of((length, GW), bf16), shape_of((length, GW), bf16),
            shape_of((length, BC)), shape_of((length, 128)),
        ],
        scratch_shapes=[
            pltpu.VMEM((Q, HALF), f32),
            pltpu.VMEM((Q, HALF), f32),
            pltpu.VMEM((HALF, HALF), f32),
            pltpu.VMEM((Q, GT * 512), f32),
        ],
        compiler_params=cparams(),
        cost_estimate=cost(2 * 10**10, 14),
        name="within_back",
    )(x_act, bc_act, aux, cum_t, dy, proj, proj, proj_edge, taps, bias, ends, entering)


def middle_kernel(
    order, y_in0, y_in1, bc_act, aux, local0, local1, entering0, entering1, gate, tokens, cot, gain, w0, w1, w2, w3,
    normed_out, output, dy_out, grad_gate, ends, back_states, begin, payload, y_dot, gain_grad,
    full, state, back, before, y_keep, gated_keep, grad_keep,
):
    c = pl.program_id(0)

    @pl.when(c == 0)
    def _():
        assemble(order, (w0, w1, w2, w3), full)
        for g, entering in enumerate((entering0, entering1)):
            for j in range(GT):
                state[g * GT + j, :, :128] = entering[2 * j]
                state[g * GT + j, :, 128:] = entering[2 * j + 1]
        begin[...] = state[...]
        back[...] = jnp.zeros_like(back)
        before[...] = jnp.zeros_like(before)
        gain_grad[...] = jnp.zeros_like(gain_grad)

    keep = aux[...]
    c_high, c_low = halves(bc_act[:, STATE:])
    c_cols = (c_high, jnp.concatenate([c_high, c_low], axis=1))
    c_rows = halves(bc_act[:, STATE:].T)

    decayed2 = terms2(keep[:, 3 * HEADS :])
    ends4 = terms4(jnp.concatenate([keep[Q - 8 :, 3 * HEADS :], keep[Q - 8 :, :HEADS]], axis=0))

    def mix(y_in, local, shift, place, squares):
        j = place + shift
        cols = tile_at(j)
        carried = fine_short(c_cols, state[j])
        y = y_in[:, tile_at(place)] + dot(decayed2, spread(2, TILE, 4 * j, 6)) * carried
        y_keep[:, cols] = y
        raw = gate[:, cols].astype(f32)
        gated = y.astype(bf16).astype(f32) * (raw * sigmoid(raw))
        gated_keep[:, cols] = gated
        moved = dot(ends4, spread(4, TILE, 4 * j, 6))[7:8] * state[j] + local[0, place]
        state[j] = moved
        ends[0, j] = moved
        both = gated * gated
        return squares + (both[:, :128] + both[:, 128:])

    squares = jnp.zeros((Q, 128), f32)
    for g, (y_in, local) in enumerate(((y_in0, local0), (y_in1, local1))):
        squares = lax.fori_loop(0, GT, functools.partial(mix, y_in, local, g * GT), squares, unroll=GT)
    scale = lax.rsqrt(jnp.sum(squares, axis=1, keepdims=True) / INNER + EPS)

    def back_out(j, products):
        cols = tile_at(j)
        gated = gated_keep[:, cols]
        gains = gain[:, cols]
        normed_out[:, cols] = (gated * scale * gains).astype(bf16)
        grad = dot_lanes(cot[...], full[cols, :])
        grad_keep[:, cols] = grad
        gain_grad[:, cols] += jnp.sum(grad * gated * scale, axis=0, keepdims=True)
        both = grad * gains * gated
        return products + (both[:, :128] + both[:, 128:])

    products = lax.fori_loop(0, TILES, back_out, jnp.zeros((Q, 128), f32), unroll=8)
    shared = jnp.sum(products, axis=1, keepdims=True) / INNER * (scale * scale * scale)
    for start in range(0, output.shape[1], TILE):
        cols = slice(start, start + TILE)
        branch = dot(normed_out[...], full[:, cols])
        output[:, cols] = (tokens[:, cols].astype(f32) + branch).astype(bf16)

    def finish(j, y_sum):
        cols = tile_at(j)
        raw = gate[:, cols].astype(f32)
        sig = sigmoid(raw)
        grad_gated = scale * (grad_keep[:, cols] * gain[:, cols]) - gated_keep[:, cols] * shared
        y = y_keep[:, cols]
        dy = (grad_gated * (raw * sig)).astype(bf16)
        dy_out[:, cols] = dy
        mixed = y.astype(bf16).astype(f32)
        grad_gate[:, cols] = (grad_gated * mixed * (sig * (1.0 + raw * (1.0 - sig)))).astype(bf16)
        wide = dy.astype(f32)
        piece = fine_with(dot, c_rows, wide * dot(decayed2, spread(2, TILE, 4 * j, 6)))
        back_states[0, j] = piece
        back[j] += jnp.exp(before[:, cols]) * piece
        before[:, cols] += dot(ends4, spread(4, TILE, 4 * j, 6))[15:16]
        return y_sum + split_dot(wide * y, head_select(j))

    y_dot[...] = lax.fori_loop(0, TILES, finish, jnp.zeros((Q, 128), f32), unroll=8)

    @pl.when(c == pl.num_programs(0) - 1)
    def _():
        for g in range(GROUPS):
            for j in range(GT):
                payload[2 * j, :, g * 128 : (g + 1) * 128] = back[g * GT + j, :, :128]
                payload[2 * j + 1, :, g * 128 : (g + 1) * 128] = back[g * GT + j, :, 128:]


def middle(order, y_in, bc_act, aux, local, entering, gate, tokens, cot, gain, pieces):
    length, width = tokens.shape
    rows = pieces[0].shape[0]
    chunks = length // Q
    per_group = pl.BlockSpec((1, GT, STATE, TILE), lambda i, o: (i, 0, 0, 0))
    per_chunk = pl.BlockSpec((1, TILES, STATE, TILE), lambda i, o: (i, 0, 0, 0))
    return pl.pallas_call(
        middle_kernel,
        grid_spec=pltpu.PrefetchScalarGridSpec(
            num_scalar_prefetch=1,
            grid=(chunks,),
            in_specs=[rows_of(GW)] * 2
            + [rows_of(BC), rows_of(128)]
            + [per_group] * 2
            + [fixed((2 * GT, STATE, 128))] * 2
            + [rows_of(INNER), rows_of(width), rows_of(width), fixed((1, INNER))]
            + [fixed((rows, width))] * 4,
            out_specs=[
                rows_of(INNER), rows_of(width), rows_of(INNER), rows_of(INNER), per_chunk, per_chunk,
                kept((TILES, STATE, TILE)), kept((PIECES, STATE, TILE)), rows_of(128), kept((1, INNER)),
            ],
            scratch_shapes=[
                pltpu.VMEM((4 * rows, width), bf16),
                pltpu.VMEM((TILES, STATE, TILE), f32),
                pltpu.VMEM((TILES, STATE, TILE), f32),
                pltpu.VMEM((1, INNER), f32),
                pltpu.VMEM((Q, INNER), f32),
                pltpu.VMEM((Q, INNER), f32),
                pltpu.VMEM((Q, INNER), f32),
            ],
        ),
        out_shape=[
            shape_of((length, INNER), bf16),
            shape_of((length, width), bf16),
            shape_of((length, INNER), bf16),
            shape_of((length, INNER), bf16),
            shape_of((chunks, TILES, STATE, TILE)),
            shape_of((chunks, TILES, STATE, TILE)),
            shape_of((TILES, STATE, TILE)),
            shape_of((PIECES, STATE, TILE)),
            shape_of((length, 128)),
            shape_of((1, INNER)),
        ],
        compiler_params=cparams(),
        cost_estimate=cost(4 * 10**10, 40),
        name="middle",
    )(order, *y_in, bc_act, aux, *local, *entering, gate, tokens, cot, gain, *pieces)


def back_kernel(
    group, now, edge, taps, skip, dy, du_in, slope, x_act, bc_act, aux, ends, back_states, leaving, *others
):
    last_group = group == GROUPS - 1
    if last_group:
        (rest, rest_prior, rest_edge, taps_bc, bias_bc, heads, y_dot,
         k_dot0, k_dot1, x_before, edge_before, b_before, bc_in0, bc_in1,
         grad, grad_taps, tail, start, grad_taps_bc, grad_heads,
         later, after, x_dot, edge_dot, b_sum) = others
    else:
        (grad, grad_taps, tail, start, x_dot, edge_dot, b_sum, later, after) = others
    step_id = pl.program_id(0)
    first = step_id == pl.num_programs(0) - 1

    @pl.when(step_id == 0)
    def _():
        for j in range(GT):
            later[j, :, :128] = leaving[2 * j, :, group * 128 : (group + 1) * 128]
            later[j, :, 128:] = leaving[2 * j + 1, :, group * 128 : (group + 1) * 128]
        after[...] = jnp.zeros_like(after)
        grad_taps[...] = jnp.zeros_like(grad_taps)
        if last_group:
            grad_taps_bc[...] = jnp.zeros_like(grad_taps_bc)
            grad_heads[...] = jnp.zeros_like(grad_heads)

    keep = aux[...]
    b_act = bc_act[:, :STATE].astype(bf16)
    factors2 = terms2(
        jnp.concatenate([keep[:, HEADS * k : HEADS * (k + 1)] for k in range(1, 3)], axis=0)
    )
    ends4 = terms4(keep[Q - 8 :, 3 * HEADS :])
    x_dot[...] = jnp.zeros_like(x_dot)
    edge_dot[...] = jnp.zeros_like(edge_dot)
    b_sum[...] = jnp.zeros_like(b_sum)

    def through(cols, dv, raw, early, tap_values):
        parts = later_rows(dv, after[:, cols])
        result = conv_of(parts, tap_values, 0.0)
        after[:, cols] = dv[:8]
        grad[:, cols] = result.astype(bf16)

        @pl.when(step_id == 0)
        def _():
            tail[:, cols] = result[Q - EDGE :]

        early = jnp.where(first, early[EDGE - 8 :].astype(f32), 0.0)
        return tap_sums(parts, raw, dv, early)

    def body(j, carry):
        cols = tile_at(j)
        select = spread(2, TILE, 4 * (j + group * GT), 6)
        heads_of = head_select(j + group * GT)
        factors = dot(factors2, select)
        step, tail_decay = factors[:Q], factors[Q:]
        x = x_act[:, cols]
        later_state = later[j]
        du = du_in[:, cols].astype(f32) + tail_decay * dot(b_act, later_state.astype(bf16))
        x_dot[...] += split_dot(x * du, heads_of)
        b_sum[...] += fine(dot_lanes, x * step * tail_decay, later_state)
        meet = jnp.sum(ends[0, j] * later_state, axis=0, keepdims=True)
        edge_dot[...] += split_dot(jnp.broadcast_to(meet, (8, TILE)), heads_of)
        later[j] = dot(ends4, spread(4, TILE, 4 * (j + group * GT), 6))[7:8] * later_state + back_states[0, j]
        dv = (step * du + skip[:, cols] * dy[:, cols].astype(f32)) * slope[:, cols].astype(f32)
        grad_taps[:, cols] += through(cols, dv, now[:, cols].astype(f32), edge[:, cols], taps[:, cols])
        return carry

    lax.fori_loop(0, GT, body, 0, unroll=2 if last_group else GT)

    if last_group:
        band = slice(GW, GW + BC)
        current = rest[:, :BC].astype(f32)
        early = jnp.where(first, rest_edge[:, :BC], rest_prior[:, :BC])
        pre = conv_of(shifted(current, early.astype(f32)), taps_bc[...], bias_bc[...])
        sig = sigmoid(pre)
        grad_act = bc_in0[...] + bc_in1[...]
        grad_act = grad_act + jnp.concatenate([b_sum[...] + b_before[...], jnp.zeros((Q, STATE), f32)], axis=1)
        dv = grad_act * (sig * (1.0 + pre * (1.0 - sig)))
        grad_taps_bc[...] += through(band, dv, current, rest_edge[:, :BC], taps_bc[...])

        step = keep[:, HEADS : 2 * HEADS]
        by_step = x_dot[:, :HEADS] + x_before[:, :HEADS]
        by_skip = k_dot0[:, :HEADS] + k_dot1[:, :HEADS]
        rate = -jnp.exp(heads[0:1, :HEADS])
        by_sum = y_dot[:, :HEADS] - heads[1:2, :HEADS] * by_skip - step * by_step
        upper = jnp.where(row_iota(Q, Q) <= lane_iota(Q, Q), 1.0, 0.0)
        by_decay = jnp.dot(upper, by_sum, precision=highest, preferred_element_type=f32)
        by_decay = by_decay + (edge_dot[0:1, :HEADS] + edge_before[0:1, :HEADS])
        raw = rest[:, BC : BC + HEADS].astype(f32) + heads[2:3, :HEADS]
        grad_dt = (by_step + by_decay * rate) * sigmoid(raw)
        full_dt = jnp.concatenate([grad_dt, jnp.zeros((Q, 128 - HEADS), f32)], axis=1)
        grad[:, GW + BC :] = full_dt.astype(bf16)
        sums = [
            jnp.sum(by_decay * (rate * step), axis=0, keepdims=True),
            jnp.sum(by_skip, axis=0, keepdims=True),
            jnp.sum(grad_dt, axis=0, keepdims=True),
            jnp.zeros((5, HEADS), f32),
        ]
        grad_heads[:, :HEADS] += jnp.concatenate(sums, axis=0)

    @pl.when(first)
    def _():
        start[...] = after[...]


def backward(group, proj, proj_edge, taps, skip, dy, du, slope, x_act, bc_act, aux, ends, back_states, leaving, others=()):
    length = proj.shape[0]
    chunks = length // Q
    per = Q // EDGE
    last_group = group == GROUPS - 1
    at = lambda i: chunks - 1 - i
    block = lambda cols, g=0: pl.BlockSpec((Q, cols), lambda i: (at(i), g))
    per_chunk = pl.BlockSpec((1, GT, STATE, TILE), lambda i: (at(i), group, 0, 0))
    dots = pl.BlockSpec((8, 128), lambda i: (at(i), 0))
    in_specs = [
        block(GW), fixed((EDGE, GW)), at_group(TAPS, group), at_group(1, group),
        block(GW, group), block(GW), block(GW), block(GW), block(BC), block(128),
        per_chunk, per_chunk, fixed((PIECES, STATE, TILE)),
    ]
    width = GW + BC if last_group else GW
    cols = GW + REST if last_group else GW
    out_specs = [block(cols), kept((8, GW)), kept((EDGE, width)), kept((8, width))]
    out_shape = [
        shape_of((length, cols), bf16), shape_of((8, GW)), shape_of((EDGE, width)), shape_of((8, width)),
    ]
    scratch = [pltpu.VMEM((GT, STATE, TILE), f32), pltpu.VMEM((8, width), f32)]
    if last_group:
        in_specs += [
            block(REST),
            pl.BlockSpec((EDGE, REST), lambda i: (jnp.maximum(at(i) * per - 1, 0), 0)),
            fixed((EDGE, REST)), fixed((TAPS, BC)), fixed((1, BC)), fixed((8, 128)),
            block(128), block(128), block(128), block(128), dots, block(STATE), block(BC), block(BC),
        ]
        out_specs += [kept((8, BC)), kept((8, 128))]
        out_shape += [shape_of((8, BC)), shape_of((8, 128))]
        scratch += [pltpu.VMEM((Q, 128), f32), pltpu.VMEM((8, 128), f32), pltpu.VMEM((Q, STATE), f32)]
    else:
        out_specs += [block(128), dots, block(STATE)]
        out_shape += [shape_of((length, 128)), shape_of((8 * chunks, 128)), shape_of((length, STATE))]
    return pl.pallas_call(
        functools.partial(back_kernel, group),
        grid=(chunks,),
        in_specs=in_specs,
        out_specs=out_specs,
        out_shape=out_shape,
        scratch_shapes=scratch,
        compiler_params=cparams(),
        cost_estimate=cost(2 * 10**10, 20),
        name="backward",
    )(proj, proj_edge, taps, skip, dy, du, slope, x_act, bc_act, aux, ends, back_states, leaving, *others)


def quarters(left, order):
    rows = left.shape[1] // 4
    block = [lax.dynamic_slice_in_dim(left, order[k] * rows, rows, axis=1) for k in range(4)]
    return jnp.concatenate([block[1], block[3]], axis=1), jnp.concatenate([block[0], block[2]], axis=1)


def weight_grad(parts, right):
    sent, held = parts
    return dot_rows(right, sent).astype(bf16), dot_rows(right, held).astype(bf16)


def out_weight_sums(parts, right):
    sent, held = parts
    return dot_rows(sent, right).astype(bf16), dot_rows(held, right).astype(bf16)


def input_kernel(
    order, grad_gate, grad_x0, grad_x1, tokens, cot, gain,
    g0, g1, g2, g3, a0, a1, a2, a3, b0, b1, b2, b3, out, gain_grad,
):
    rows = g0.shape[0]

    @pl.when(pl.program_id(0) == 0)
    def _():
        gain_grad[...] = jnp.zeros_like(gain_grad)

    for k, (gate_w, a_w, b_w) in enumerate(((g0, a0, b0), (g1, a1, b1), (g2, a2, b2), (g3, a3, b3))):
        cols = pl.ds(pl.multiple_of(order[k] * rows, rows), rows)
        total = dot_lanes(grad_gate[...], gate_w[...]) + dot_lanes(grad_x0[...], a_w[:, :GW])
        total = total + dot_lanes(grad_x1[:, :GW], b_w[...])
        out[:, cols] = total + dot_lanes(grad_x1[:, GW:], a_w[:, GW:])
    grad = out[...]
    wide = tokens[...].astype(f32)
    width = wide.shape[1]
    scale = lax.rsqrt(jnp.mean(wide * wide, axis=1, keepdims=True) + EPS)
    gain_grad[...] += jnp.sum(grad * wide * scale, axis=0, keepdims=True)
    scaled = grad * gain[...]
    shared = jnp.sum(scaled * wide, axis=1, keepdims=True) / width
    out[...] = cot[...].astype(f32) + (scale * scaled - wide * (scale * scale * scale * shared))


def input_back(order, grad_gate, grad_x0, grad_x1, tokens, cot, gain, gate_pieces, a_pieces, b_pieces):
    length, width = tokens.shape
    rows = width // 4
    return pl.pallas_call(
        input_kernel,
        grid_spec=pltpu.PrefetchScalarGridSpec(
            num_scalar_prefetch=1,
            grid=(length // Q,),
            in_specs=[rows_of(INNER), rows_of(GW), rows_of(GW + REST), rows_of(width), rows_of(width), fixed((1, width))]
            + [fixed((rows, INNER))] * 4
            + [fixed((rows, GW + REST))] * 4
            + [fixed((rows, GW))] * 4,
            out_specs=[rows_of(width), kept((1, width))],
        ),
        out_shape=[shape_of((length, width)), shape_of((1, width))],
        compiler_params=cparams(),
        cost_estimate=cost(2 * length * width * (INNER + XCOLS), 26),
        name="input_back",
    )(order, grad_gate, grad_x0, grad_x1, tokens, cot, gain, *gate_pieces, *a_pieces, *b_pieces)


def swap(value, axis, bit):
    count = lax.axis_size(axis)
    return lax.ppermute(value, axis, [(i, i ^ bit) for i in range(count)])


def exchange(value, axis):
    return lax.all_to_all(value, axis, split_axis=0, concat_axis=0, tiled=True)


def tie(value, *others):
    return lax.optimization_barrier((value, others))[0]


def to_owners(value, groups=1):
    count = lax.axis_size("seq")
    pieces, rows, lanes = value.shape
    if count != pieces:
        lanes //= groups
        width = pieces * lanes // count
        split = value.reshape(pieces, rows, groups, lanes // width, width)
        value = split.transpose(0, 3, 1, 2, 4).reshape(count, rows, groups * width)
    return exchange(value, "seq")


def from_owners(value, groups=1, pieces=PIECES, lanes=128):
    value = exchange(value, "seq")
    count, rows, width = value.shape
    if count == pieces:
        return value
    width //= groups
    split = value.reshape(pieces, lanes // width, rows, groups, width)
    return split.transpose(0, 2, 3, 1, 4).reshape(pieces, rows, groups * lanes)


def send_core(grads):
    sent, held = grads
    return held, swap(sent, "wshard", 1)


def send_x(state, axis=1):
    held, got = state
    own, other = jnp.split(held, 2, axis=axis)
    got_own, got_other = jnp.split(got, 2, axis=axis)
    return (
        own.astype(f32) + got_own.astype(f32),
        swap((other.astype(f32) + got_other.astype(f32)).astype(bf16), "wshard", 2),
    )


def sum_pair(state):
    mine, got = state
    return mine + got.astype(f32)


def fold(value):
    rows, cols = value.shape
    return value.reshape(rows, cols // TILE, TILE).swapaxes(0, 1).reshape(-1, TILE)


def unfold(value, cols):
    return value.reshape(cols // TILE, -1, TILE).swapaxes(0, 1).reshape(-1, cols)


def send_near_pair(even, odd):
    is_even = (lax.axis_index("seq") & 1) == 0
    theirs = jnp.where(is_even, odd, even).astype(bf16)
    return jnp.where(is_even, even, odd), swap(theirs, "seq", 1)


def send_near(state):
    mine, got = state
    total = mine + got.astype(f32)
    half = total.shape[0] // 2
    bit = lax.axis_index("seq") & 1
    theirs = lax.dynamic_slice_in_dim(total, (1 - bit) * half, half, axis=0).astype(bf16)
    return lax.dynamic_slice_in_dim(total, bit * half, half, axis=0), swap(theirs, "seq", 1)


def send_far(state):
    mine, got = state
    total = mine + got.astype(f32)
    group = lax.axis_size("seq") // 2
    place = lax.axis_index("seq") >> 1
    part = total.shape[0] // group
    piece = lambda k: lax.dynamic_slice_in_dim(total, (place ^ k) * part, part, axis=0)
    return piece(0), [swap(piece(k).astype(bf16), "seq", 2 * k) for k in range(1, group)]


def share_far(state):
    mine, got = state
    owned = (mine + sum(piece.astype(f32) for piece in got)).astype(bf16)
    return [owned] + [swap(owned, "seq", 2 * k) for k in range(1, len(got) + 1)]


def in_order(pieces, place, join=True):
    bit = 1
    while bit < len(pieces):
        odd = (place & bit) != 0
        pieces = [jnp.where(odd, pieces[k ^ bit], pieces[k]) for k in range(len(pieces))]
        bit *= 2
    return jnp.concatenate(pieces, axis=0) if join else pieces


def share_near(pieces):
    half = in_order(pieces, lax.axis_index("seq") >> 1)
    return [half, swap(half, "seq", 1)]


def whole_rows(pieces):
    return in_order(pieces, lax.axis_index("seq") & 1)


def local(
    block_in, norm_gain, in_weight, conv_x, conv_x_bias, conv_bc, conv_bc_bias,
    a_log, skip, dt_bias, out_gain, out_weight, cotangent,
):
    tokens = block_in[0]
    cot = cotangent[0]
    length, width = tokens.shape
    seq = lax.axis_size("seq")
    shards = lax.axis_size("wshard")
    own_heads = HEADS // seq
    own_ch = INNER // seq
    me = lax.axis_index("wshard")
    order = jnp.stack([me ^ k for k in range(4)]).astype(jnp.int32)
    place = lax.axis_index("seq")

    a_piece = jnp.concatenate(
        [in_weight[:, INNER : INNER + GW], jnp.pad(in_weight[:, 2 * INNER :], ((0, 0), (0, XCOLS - XUSED)))], axis=1
    )
    b_piece = in_weight[:, INNER + GW : 2 * INNER]
    gate_piece = in_weight[:, :INNER]
    edge = lax.ppermute(tokens[length - EDGE :], "seq", [(i, i + 1) for i in range(seq - 1)])
    small = jnp.concatenate(
        [
            conv_x,
            conv_x_bias[None],
            jnp.pad(jnp.stack([a_log, skip, dt_bias]), ((0, 0), (0, own_ch - own_heads))),
        ],
        axis=0,
    )
    a_across, a_beside = swap(a_piece, "wshard", 2), swap(a_piece, "wshard", 1)
    small_all = exchange(jnp.broadcast_to(small[None], (seq,) + small.shape), "seq")
    x_params = small_all[:, :5].transpose(1, 0, 2).reshape(5, INNER)
    head_params = small_all[:, 5:, :own_heads].transpose(1, 0, 2).reshape(3, HEADS)
    taps, bias = x_params[:4], x_params[4:5]
    heads = jnp.pad(head_params, ((0, 5), (0, 128 - HEADS)))
    skip_row = jnp.repeat(head_params[1], INNER // HEADS)[None]
    bias_bc = conv_bc_bias[None]
    a_across = tie(a_across, small_all, edge, a_beside)
    a_pieces = (a_piece, a_beside, a_across, swap(a_across, "wshard", 1))
    b_piece, gate_piece, out_piece = tie((b_piece, gate_piece, out_weight), a_across)
    b_across, b_beside = swap(b_piece, "wshard", 2), swap(b_piece, "wshard", 1)

    normed, proj0, rest, proj_edge0, rest_edge = project(order, tokens, edge, norm_gain[None], a_pieces)
    gate_across, gate_beside = swap(gate_piece, "wshard", 2), swap(gate_piece, "wshard", 1)
    out_across, out_beside = swap(out_piece, "wshard", 2), swap(out_piece, "wshard", 1)
    bc_act, aux, cum_t = factors(rest, rest_edge, conv_bc, bias_bc, heads)
    b_across = tie(b_across, bc_act)
    b_pieces = (b_piece, b_beside, b_across, swap(b_across, "wshard", 1))
    x_act0, local0, payload0 = states(0, proj0, proj_edge0, taps, bias, bc_act, aux)
    arrived0 = to_owners(payload0)
    proj1, proj_edge1 = project_more(order, tie(normed, payload0), edge, norm_gain[None], b_pieces)
    x_act1, local1, payload1 = states(1, proj1, proj_edge1, taps, bias, bc_act, aux)
    arrived1 = to_owners(payload1)
    y0 = within(0, tie(x_act0, payload1), bc_act, aux, cum_t, skip_row)
    gate_pieces = (gate_piece, gate_beside, gate_across, swap(gate_across, "wshard", 1))
    gate = gate_project(order, tie(normed, y0), gate_pieces)
    entering0 = chain(True, *tie((arrived0, arrived0[:, STATE:, :]), gate))
    totals0, totals1 = arrived0[:, STATE:, :], arrived1[:, STATE:, :]
    back0 = from_owners(entering0)
    entering1 = chain(True, *tie((arrived1, totals1), entering0))
    back1 = from_owners(entering1)
    y1 = within(1, tie(x_act1, entering1), bc_act, aux, cum_t, skip_row)
    entering0, entering1 = tie((back0, back1), y1)
    out_pieces = (out_piece, out_beside, out_across, swap(out_across, "wshard", 1))
    (normed_out, output, dy, grad_gate, ends, back_states, begin, back_payload, y_dot, out_gain_grad) = middle(
        order, (y0, y1), bc_act, aux, (local0, local1), (entering0, entering1), gate, tokens, cot, out_gain[None], out_pieces
    )

    back_arrived = to_owners(back_payload, 2)
    totals = jnp.concatenate([totals0, totals1], axis=2)
    normed_parts = quarters(normed, order)
    out_grads = out_weight_sums(quarters(normed_out, order), cot)
    out_core = send_core(out_grads)
    gate_grads = weight_grad(normed_parts, tie(grad_gate, out_grads))
    gate_core = send_core(gate_grads)
    du0, slope0, grad_bc0, k_dot0 = within_back(
        0, tie(x_act0, gate_grads), bc_act, aux, cum_t, dy, proj0, proj_edge0, taps, bias, ends, begin
    )
    out_x = send_x(tie(out_core, du0), axis=0)
    gate_x = send_x(tie(gate_core, out_x[0]))
    leaving = chain(False, *tie((back_arrived, totals), gate_x[0]))
    leave = from_owners(leaving, 2)
    du1, slope1, grad_bc1, k_dot1 = within_back(
        1, tie(x_act1, leaving), bc_act, aux, cum_t, dy, proj1, proj_edge1, taps, bias, ends, begin
    )
    out_fold = fold(sum_pair(tie(out_x, du1)))
    leave = tie(leave, out_fold)
    grad_x0, grad_taps0, tail0, start0, x_dot0, edge_dot0, b_sum0 = backward(
        0, proj0, proj_edge0, taps, skip_row, dy, du0, slope0, x_act0, bc_act, aux, ends, back_states, leave
    )
    all_taps = jnp.concatenate([taps[:, GW:], conv_bc], axis=1)
    backwards = [(i, i - 1) for i in range(1, seq)]

    def fix(grad, tail, start, tap_values):
        fixes = [
            tail[EDGE - 3 + a] + sum(tap_values[k] * start[a - k] for k in range(a + 1)) for a in range(3)
        ]
        fixed_rows = jnp.concatenate([tail[: EDGE - 3], jnp.stack(fixes)], axis=0).astype(bf16)
        return lax.dynamic_update_slice(grad, fixed_rows, (length - EDGE, 0))

    after0 = lax.ppermute(start0, "seq", backwards)
    gate_pair = sum_pair(tie(gate_x, grad_x0))
    early_near = send_near_pair(gate_pair, out_fold)
    grad_x0 = fix(tie(grad_x0, early_near[0]), tail0, after0, taps[:, :GW])
    x0_grads = weight_grad(normed_parts, grad_x0)
    x0_core = send_core(x0_grads)
    x0_x = send_x(x0_core)
    grad_x1, grad_taps1, tail1, start1, grad_taps_bc, grad_heads = backward(
        1, proj1, proj_edge1, taps, skip_row, tie(dy, x0_x[0]), du1, slope1, x_act1, bc_act, aux, ends, back_states,
        leave,
        (rest, rest, rest_edge, conv_bc, bias_bc, heads, y_dot, k_dot0, k_dot1, x_dot0, edge_dot0, b_sum0, grad_bc0, grad_bc1),
    )
    x0_near = send_near(tie(x0_x, grad_x1))
    early_far = send_far(tie(early_near, x0_near[0]))
    after1 = lax.ppermute(tie(start1, x0_near[0]), "seq", backwards)
    grad_x1 = fix(tie(grad_x1, early_far[0]), tail1, after1, all_taps)
    x1_grads = weight_grad(normed_parts, grad_x1)
    x1_core = send_core(x1_grads)
    x0_far = send_far(tie(x0_near, x1_grads))
    x1_x = send_x(tie(x1_core, x0_far[0]))
    early_all = share_far(tie(early_far, x1_x[0]))
    x0_all = share_far(tie(x0_far, early_all[0]))
    input_grad, norm_gain_grad = input_back(
        order, tie(grad_gate, x0_all[0]), grad_x0, grad_x1, tokens, cot, norm_gain[None], gate_pieces, a_pieces, b_pieces
    )
    x1_near = send_near(tie(x1_x, input_grad))
    norm_gain_grad = tie(norm_gain_grad, x1_near[0])
    grad_taps = jnp.concatenate([grad_taps0, grad_taps1], axis=1)
    shared = jnp.concatenate(
        [norm_gain_grad[0], out_gain_grad[0], grad_taps_bc[:5].reshape(-1)]
    )
    mine = jnp.concatenate(
        [
            grad_taps[:5].reshape(5, seq, own_ch).transpose(1, 0, 2).reshape(seq, 5 * own_ch),
            grad_heads[:3, :HEADS].reshape(3, seq, own_heads).transpose(1, 0, 2).reshape(seq, 3 * own_heads),
        ],
        axis=1,
    )
    shared_size, mine_size = shared.shape[0], mine.shape[1]
    pad = -(shared_size + mine_size) % 1024
    small_out = jnp.concatenate(
        [jnp.broadcast_to(shared[None], (seq, shared_size)), mine, jnp.zeros((seq, pad), f32)], axis=1
    )
    small_out = jnp.broadcast_to(small_out[:, None], (seq, shards, small_out.shape[1]))
    small_sum = jnp.sum(
        exchange(small_out.reshape(seq * shards, 8, -1), ("seq", "wshard")), axis=0
    ).reshape(-1)
    early_half = share_near(tie(early_all, small_out))
    x0_half = share_near(tie(x0_all, early_half[0]))
    x1_far = send_far(tie(x1_near, x0_half[0]))
    x1_all = share_far(x1_far)
    x1_half = share_near(tie(x1_all, small_sum, early_half[1]))
    gate_sum, out_sum = in_order(early_half, place & 1, join=False)
    out_owned = unfold(out_sum, width).astype(f32)
    in_owned = jnp.concatenate(
        [gate_sum, whole_rows(x0_half), whole_rows(x1_half)[: XUSED - GW]], axis=0
    ).astype(f32).T
    pos = [0]

    def take(shape):
        size = 1
        for extent in shape:
            size *= extent
        out = small_sum[pos[0] : pos[0] + size].reshape(shape)
        pos[0] += size
        return out

    norm_gain_sum = take((width,))
    out_gain_sum = take((INNER,))
    bc_sum = take((5, BC))
    x_sum = take((5, own_ch))
    head_sum = take((3, own_heads))
    return (
        output[None],
        input_grad[None],
        norm_gain_sum,
        in_owned,
        x_sum[:4],
        x_sum[4],
        bc_sum[:4],
        bc_sum[4],
        head_sum[0],
        head_sum[1],
        head_sum[2],
        out_gain_sum,
        out_owned,
    )


def solution(mesh):
    in_specs = (
        P("wshard", "seq", None),
        P(),
        P("wshard", None),
        P(None, "seq"),
        P("seq"),
        P(),
        P(),
        P("seq"),
        P("seq"),
        P("seq"),
        P(),
        P("wshard", None),
        P("wshard", "seq", None),
    )
    out_specs = (
        P("wshard", "seq", None),
        P("wshard", "seq", None),
        P(),
        P("wshard", None),
        P(None, "seq"),
        P("seq"),
        P(),
        P(),
        P("seq"),
        P("seq"),
        P("seq"),
        P(),
        P("wshard", None),
    )
    return jax.shard_map(local, mesh=mesh, in_specs=in_specs, out_specs=out_specs, check_vma=False)
```

```python
import functools

import jax
import jax.numpy as jnp
from jax import lax
from jax.experimental import pallas as pl
from jax.experimental.pallas import tpu as pltpu
from jax.sharding import PartitionSpec as P

INNER = 2048
STATE = 128
HEADS = 32
TAPS = 4
BC = 2 * STATE
CH = INNER + BC
XCOLS = 2432
XUSED = 2336
Q = 256
HALF = Q // 2
TILE = 256
TILES = INNER // TILE
GROUPS = 2
GT = TILES // GROUPS
GW = INNER // GROUPS
REST = XCOLS - INNER
PIECES = 2 * GT
EDGE = 16
EPS = 1e-05

f32 = jnp.float32
bf16 = jnp.bfloat16
highest = lax.Precision.HIGHEST


def cparams(megabytes=56):
    return pltpu.CompilerParams(
        dimension_semantics=("arbitrary",), vmem_limit_bytes=megabytes * 2**20
    )


def dot(a, b):
    return lax.dot_general(a, b, (((1,), (0,)), ((), ())), preferred_element_type=f32)


def dot_lanes(a, b):
    return lax.dot_general(a, b, (((1,), (1,)), ((), ())), preferred_element_type=f32)


def dot_rows(a, b):
    return lax.dot_general(a, b, (((0,), (0,)), ((), ())), preferred_element_type=f32)


def sigmoid(v):
    return 0.5 * jnp.tanh(0.5 * v) + 0.5


def lane_iota(rows, lanes):
    return lax.broadcasted_iota(jnp.int32, (rows, lanes), 1)


def row_iota(rows, lanes):
    return lax.broadcasted_iota(jnp.int32, (rows, lanes), 0)


def spread(terms, width, first, shift):
    rows = row_iota(terms * HEADS, width) & (HEADS - 1)
    return jnp.where(rows == first + (lane_iota(terms * HEADS, width) >> shift), 1.0, 0.0).astype(bf16)


def halves(value):
    high = value.astype(bf16)
    return high, (value - high.astype(f32)).astype(bf16)


def terms2(value):
    return jnp.concatenate(halves(value), axis=1)


def terms4(value):
    high = value.astype(bf16)
    rest = value - high.astype(f32)
    middle, low = halves(rest)
    return jnp.concatenate([high, middle, low, jnp.zeros_like(high)], axis=1)


def split_dot(value, select):
    high = value.astype(bf16)
    low = (value - high.astype(f32)).astype(bf16)
    return dot(high, select) + dot(low, select)


def fine(product, a, b):
    a_high, a_low = halves(a)
    b_high, b_low = halves(b)
    return product(a_high, b_high) + (product(a_high, b_low) + product(a_low, b_high))


def fine_with(product, a_terms, b):
    a_high, a_low = a_terms
    b_high, b_low = halves(b)
    return product(a_high, b_high) + (product(a_high, b_low) + product(a_low, b_high))


def fine_short(a_terms, b):
    a_high, a_both = a_terms
    b_high, b_low = halves(b)
    return dot(a_both, jnp.concatenate([b_high, b_high], axis=0)) + dot(a_high, b_low)


def head_select(tile):
    lanes = row_iota(TILE, 128) >> 6
    return jnp.where(lanes + tile * (TILE // 64) == lane_iota(TILE, 128), 1.0, 0.0).astype(bf16)


def shifted(current, before):
    joined = jnp.concatenate([before[EDGE - 8 :], current], axis=0)
    rows = current.shape[0]
    return [joined[5 + k : 5 + k + rows] for k in range(TAPS - 1)] + [current]


def conv_of(parts, taps, bias):
    total = bias + taps[0:1] * parts[0]
    for k in range(1, TAPS):
        total = total + taps[k : k + 1] * parts[k]
    return total


def later_rows(grad, after):
    joined = jnp.concatenate([grad, after], axis=0)
    rows = grad.shape[0]
    return [joined[TAPS - 1 - k : TAPS - 1 - k + rows] for k in range(TAPS - 1)] + [grad]


def tap_sums(parts, raw, grad, early):
    first = grad[:8]
    sums = []
    for k in range(TAPS):
        total = jnp.sum(parts[k] * raw, axis=0, keepdims=True)
        if k < TAPS - 1:
            total = total + jnp.sum(first[: TAPS - 1 - k] * early[8 - TAPS + 1 + k :], axis=0, keepdims=True)
        sums.append(total)
    sums.append(jnp.sum(grad, axis=0, keepdims=True))
    sums.append(jnp.zeros((3, grad.shape[1]), f32))
    return jnp.concatenate(sums, axis=0)


def tile_at(j, width=TILE):
    return pl.ds(pl.multiple_of(j * width, width), width)


def assemble(order, pieces, full):
    rows = pieces[0].shape[0]
    for k, piece in enumerate(pieces):
        full[pl.ds(pl.multiple_of(order[k] * rows, rows), rows), :] = piece[...]


def norm_rows(values, gain):
    wide = values.astype(f32)
    scale = lax.rsqrt(jnp.mean(wide * wide, axis=1, keepdims=True) + EPS)
    return (wide * scale * gain).astype(bf16)


def project_kernel(order, tokens, edge, gain, w0, w1, w2, w3, normed, out, out_rest, out_edge, out_edge_rest, full):
    @pl.when(pl.program_id(0) == 0)
    def _():
        assemble(order, (w0, w1, w2, w3), full)
        early = dot(norm_rows(edge[...], gain[...]), full[...]).astype(bf16)
        out_edge[...] = early[:, :GW]
        out_edge_rest[...] = early[:, GW:]

    now = norm_rows(tokens[...], gain[...])
    normed[...] = now
    for start in range(0, GW, TILE):
        out[:, start : start + TILE] = dot(now, full[:, start : start + TILE]).astype(bf16)
    out_rest[...] = dot(now, full[:, GW:]).astype(bf16)


def project_more_kernel(order, normed, edge, gain, w0, w1, w2, w3, out, out_edge, full):
    @pl.when(pl.program_id(0) == 0)
    def _():
        assemble(order, (w0, w1, w2, w3), full)
        out_edge[...] = dot(norm_rows(edge[...], gain[...]), full[...]).astype(bf16)

    for start in range(0, GW, TILE):
        out[:, start : start + TILE] = dot(normed[...], full[:, start : start + TILE]).astype(bf16)


def fixed(shape):
    return pl.BlockSpec(shape, lambda i, *o: (0,) * len(shape), pipeline_mode=pl.Buffered(1))


def kept(shape):
    return pl.BlockSpec(shape, lambda i, *o: (0,) * len(shape))


def rows_of(cols, group=0):
    return pl.BlockSpec((Q, cols), lambda i, *o: (i, group))


def shape_of(shape, dtype=f32):
    return jax.ShapeDtypeStruct(shape, dtype)


def cost(flops, megabytes):
    return pl.CostEstimate(flops=int(flops) // 1, bytes_accessed=int(megabytes * 2**20) // 1, transcendentals=0)


def project(order, tokens, edge, gain, pieces):
    length, width = tokens.shape
    rows = pieces[0].shape[0]
    return pl.pallas_call(
        project_kernel,
        grid_spec=pltpu.PrefetchScalarGridSpec(
            num_scalar_prefetch=1,
            grid=(length // Q,),
            in_specs=[rows_of(width), fixed((EDGE, width)), fixed((1, width))] + [fixed((rows, GW + REST))] * 4,
            out_specs=[rows_of(width), rows_of(GW), rows_of(REST), kept((EDGE, GW)), kept((EDGE, REST))],
            scratch_shapes=[pltpu.VMEM((4 * rows, GW + REST), bf16)],
        ),
        out_shape=[
            shape_of((length, width), bf16),
            shape_of((length, GW), bf16),
            shape_of((length, REST), bf16),
            shape_of((EDGE, GW), bf16),
            shape_of((EDGE, REST), bf16),
        ],
        compiler_params=cparams(),
        cost_estimate=cost(4 * length * width * (GW + REST), 9),
        name="project",
    )(order, tokens, edge, gain, *pieces)


def project_more(order, normed, edge, gain, pieces):
    length, width = normed.shape
    rows = pieces[0].shape[0]
    return pl.pallas_call(
        project_more_kernel,
        grid_spec=pltpu.PrefetchScalarGridSpec(
            num_scalar_prefetch=1,
            grid=(length // Q,),
            in_specs=[rows_of(width), fixed((EDGE, width)), fixed((1, width))] + [fixed((rows, GW))] * 4,
            out_specs=[rows_of(GW), kept((EDGE, GW))],
            scratch_shapes=[pltpu.VMEM((4 * rows, GW), bf16)],
        ),
        out_shape=[shape_of((length, GW), bf16), shape_of((EDGE, GW), bf16)],
        compiler_params=cparams(),
        cost_estimate=cost(4 * length * width * GW, 6),
        name="project_more",
    )(order, normed, edge, gain, *pieces)


def gate_kernel(order, normed, w0, w1, w2, w3, out, full):
    @pl.when(pl.program_id(0) == 0)
    def _():
        assemble(order, (w0, w1, w2, w3), full)

    for j in range(TILES):
        cols = slice(j * TILE, (j + 1) * TILE)
        out[:, cols] = dot(normed[...], full[:, cols]).astype(bf16)


def gate_project(order, normed, pieces):
    length, width = normed.shape
    rows = pieces[0].shape[0]
    return pl.pallas_call(
        gate_kernel,
        grid_spec=pltpu.PrefetchScalarGridSpec(
            num_scalar_prefetch=1,
            grid=(length // Q,),
            in_specs=[rows_of(width)] + [fixed((rows, INNER))] * 4,
            out_specs=rows_of(INNER),
            scratch_shapes=[pltpu.VMEM((4 * rows, INNER), bf16)],
        ),
        out_shape=shape_of((length, INNER), bf16),
        compiler_params=cparams(),
        cost_estimate=cost(4 * length * width * INNER, 10),
        name="gate_project",
    )(order, normed, *pieces)


def factors_kernel(now, prior, edge, taps_bc, bias_bc, heads, bc_act, aux_out, cum_t):
    first = pl.program_id(0) == 0
    early = jnp.where(first, edge[:, :BC], prior[:, :BC]).astype(f32)
    pre = conv_of(shifted(now[:, :BC].astype(f32), early), taps_bc[...], bias_bc[...])
    bc_act[...] = pre * sigmoid(pre)
    raw = now[:, BC : BC + HEADS].astype(f32) + heads[2:3, :HEADS]
    step = jnp.maximum(raw, 0.0) + jnp.log1p(jnp.exp(-jnp.abs(raw)))
    decay = -jnp.exp(heads[0:1, :HEADS]) * step
    lower = jnp.where(row_iota(Q, Q) >= lane_iota(Q, Q), 1.0, 0.0)
    cumulative = jnp.dot(lower, decay, precision=highest, preferred_element_type=f32)
    last = cumulative[Q - 1 : Q]
    aux = jnp.concatenate([cumulative, step, jnp.exp(last - cumulative), jnp.exp(cumulative)], axis=1)
    aux_out[...] = aux
    cum_t[...] = aux.T[:HEADS]


def states_kernel(
    group, now, prior, edge, taps, bias, bc_act, aux, x_act, local, payload, run, total, b_rows
):
    c = pl.program_id(0)
    first = c == 0

    @pl.when(first)
    def _():
        run[...] = jnp.zeros_like(run)
        total[...] = jnp.zeros_like(total)

    b_rows[...] = bc_act[:, :STATE].T
    weight2 = terms2(aux[:, HEADS : 2 * HEADS] * aux[:, 2 * HEADS : 3 * HEADS])
    ends4 = terms4(jnp.concatenate([aux[Q - 8 :, 3 * HEADS :], aux[Q - 8 :, :HEADS]], axis=0))

    def body(j, carry):
        cols = tile_at(j)
        early = jnp.where(first, edge[:, cols], prior[:, cols]).astype(f32)
        pre = conv_of(shifted(now[:, cols].astype(f32), early), taps[:, cols], bias[:, cols])
        x = pre * sigmoid(pre)
        x_act[:, cols] = x
        lead = 4 * (j + group * GT)
        state = fine(dot, b_rows[...], x * dot(weight2, spread(2, TILE, lead, 6)))
        local[0, j] = state
        end = dot(ends4, spread(4, TILE, lead, 6))
        run[j] = end[7:8] * run[j] + state
        total[:, cols] += end[15:16]
        return carry

    lax.fori_loop(0, GT, body, 0, unroll=GT)

    @pl.when(c == pl.num_programs(0) - 1)
    def _():
        for j in range(2 * GT):
            lanes = slice(128 * (j % 2), 128 * (j % 2) + 128)
            payload[j, :STATE, :] = run[j // 2, :, lanes]
            payload[j, STATE:, :] = jnp.broadcast_to(total[:, j * 128 : (j + 1) * 128], (8, 128))


def prior_rows(cols, group=0):
    per = Q // EDGE
    return pl.BlockSpec((EDGE, cols), lambda i, *o: (jnp.maximum(i * per - 1, 0), group))


def at_group(rows, group):
    return pl.BlockSpec((rows, GW), lambda i, *o: (0, group), pipeline_mode=pl.Buffered(1))


def factors(rest, rest_edge, taps_bc, bias_bc, heads):
    length = rest.shape[0]
    return pl.pallas_call(
        factors_kernel,
        grid=(length // Q,),
        in_specs=[
            rows_of(REST), prior_rows(REST), fixed((EDGE, REST)),
            fixed((TAPS, BC)), fixed((1, BC)), fixed((8, 128)),
        ],
        out_specs=[rows_of(BC), rows_of(128), pl.BlockSpec((HEADS, Q), lambda i: (0, i))],
        out_shape=[shape_of((length, BC)), shape_of((length, 128)), shape_of((HEADS, length))],
        compiler_params=cparams(),
        cost_estimate=cost(5 * 10**9, 4),
        name="factors",
    )(rest, rest, rest_edge, taps_bc, bias_bc, heads)


def states(group, proj, proj_edge, taps, bias, bc_act, aux):
    length = proj.shape[0]
    chunks = length // Q
    return pl.pallas_call(
        functools.partial(states_kernel, group),
        grid=(chunks,),
        in_specs=[
            rows_of(GW), prior_rows(GW), fixed((EDGE, GW)),
            at_group(TAPS, group), at_group(1, group), rows_of(BC), rows_of(128),
        ],
        out_specs=[
            rows_of(GW),
            pl.BlockSpec((1, GT, STATE, TILE), lambda i: (i, 0, 0, 0)),
            kept((2 * GT, STATE + 8, 128)),
        ],
        out_shape=[
            shape_of((length, GW)),
            shape_of((chunks, GT, STATE, TILE)),
            shape_of((2 * GT, STATE + 8, 128)),
        ],
        scratch_shapes=[
            pltpu.VMEM((GT, STATE, TILE), f32),
            pltpu.VMEM((1, GW), f32),
            pltpu.VMEM((STATE, Q), f32),
        ],
        compiler_params=cparams(),
        cost_estimate=cost(10**10, 10),
        name="states",
    )(proj, proj, proj_edge, taps, bias, bc_act, aux)


def chain_kernel(forward, values, totals, out):
    count = out.shape[0]
    order = range(count) if forward else range(count - 1, -1, -1)
    state = jnp.zeros(out.shape[1:], f32)
    for i in order:
        out[i] = state
        state = jnp.exp(totals[i, 0:1, :]) * state + values[i, :STATE, :]


def chain(forward, values, totals):
    count, _, width = values.shape
    return pl.pallas_call(
        functools.partial(chain_kernel, forward),
        out_shape=jax.ShapeDtypeStruct((count, STATE, width), f32),
        compiler_params=pltpu.CompilerParams(vmem_limit_bytes=56 * 2**20),
        cost_estimate=cost(10**8, 3),
        name="chain",
    )(values, totals)


def within_kernel(group, x_act, bc_act, aux, cum_t, skip, out, scores, columns):
    lower = row_iota(HALF, HALF) >= lane_iota(HALF, HALF)
    for b in range(2):
        rows = slice(b * HALF, (b + 1) * HALF)
        scores[rows, :] = jnp.where(lower, fine(dot_lanes, bc_act[rows, STATE:], bc_act[rows, :STATE]), 0.0)
    cross_high, cross_low = halves(fine(dot_lanes, bc_act[HALF:, STATE:], bc_act[:HALF, :STATE]))
    cross2 = jnp.concatenate([cross_high, cross_low], axis=1)
    cumulative = aux[:, :HEADS]
    middle_row = cumulative[HALF - 1 : HALF]
    step2 = terms2(aux[:, HEADS : 2 * HEADS])
    bridge2 = terms2(jnp.exp(jnp.concatenate([middle_row - cumulative[:HALF], cumulative[HALF:] - middle_row], axis=0)))
    cumulative4 = terms4(cumulative)
    for j in range(GT):
        columns[:, j * 512 : (j + 1) * 512] = dot(cumulative4, spread(4, 512, 4 * (j + group * GT), 7))
    low = lane_iota(HALF, HALF) < 64

    def body(j, carry):
        cols = tile_at(j)
        x = x_act[:, cols]
        select = spread(2, TILE, 4 * (j + group * GT), 6)
        u = x * dot(step2, select)
        bridge = dot(bridge2, select)
        u_high, u_low = halves(u)
        v_high, v_low = halves(u[:HALF] * bridge[:HALF])
        across = dot(cross2, jnp.concatenate([v_high, v_high], axis=0)) + dot(cross_high, v_low)
        across = across * bridge[HALF:]
        direct = skip[:, cols] * x
        for pair in range(2):
            lanes = slice(pair * 128, (pair + 1) * 128)
            place = pl.ds(pl.multiple_of(j * TILE + pair * 128, 128), 128)
            for b in range(2):
                rows = slice(b * HALF, (b + 1) * HALF)
                weights = []
                for i in range(2):
                    head = 4 * j + 2 * pair + i
                    column = columns[rows, pl.ds(pl.multiple_of(head * 128, 128), 128)]
                    row = cum_t[pl.ds(head + 4 * GT * group, 1), :][:, rows]
                    weights.append(jnp.exp(jnp.minimum(column - row, 0.0)) * scores[rows, :])
                w_high, w_low = halves(jnp.concatenate(weights, axis=1))
                top = both_heads(low, u_high[rows, lanes])
                bottom = both_heads(low, u_low[rows, lanes])
                twice = dot(w_high, jnp.concatenate([top, bottom], axis=1))
                y = twice[:, :128] + twice[:, 128:] + dot(w_low, top) + direct[rows, lanes]
                if b == 1:
                    y = y + across[:, lanes]
                out[rows, place] = y
        return carry

    lax.fori_loop(0, GT, body, 0, unroll=GT)


def both_heads(low, value):
    zero = jnp.zeros_like(value)
    return jnp.concatenate([jnp.where(low, value, zero), jnp.where(low, zero, value)], axis=0)


def within(group, x_act, bc_act, aux, cum_t, skip):
    length = x_act.shape[0]
    return pl.pallas_call(
        functools.partial(within_kernel, group),
        grid=(length // Q,),
        in_specs=[
            rows_of(GW), rows_of(BC), rows_of(128),
            pl.BlockSpec((HEADS, Q), lambda i: (0, i)), at_group(1, group),
        ],
        out_specs=rows_of(GW),
        out_shape=shape_of((length, GW)),
        scratch_shapes=[pltpu.VMEM((Q, HALF), f32), pltpu.VMEM((Q, GT * 512), f32)],
        compiler_params=cparams(),
        cost_estimate=cost(10**10, 10),
        name="within",
    )(x_act, bc_act, aux, cum_t, skip)


def within_back_kernel(
    group, x_act, bc_act, aux, cum_t, dy, now, prior, edge, taps, bias, ends, entering,
    out, slope, out_bc, k_dot, scores, grad_scores, grad_cross, columns,
):
    first = pl.program_id(0) == 0
    k_dot[...] = jnp.zeros_like(k_dot)
    out_bc[:, STATE:] = jnp.zeros((Q, STATE), f32)
    upper = row_iota(HALF, HALF) <= lane_iota(HALF, HALF)
    act = bc_act[...].astype(bf16)
    b_act, c_act = act[:, :STATE], act[:, STATE:]
    for b in range(2):
        rows = slice(b * HALF, (b + 1) * HALF)
        scores[rows, :] = jnp.where(upper, dot_lanes(b_act[rows], c_act[rows]), 0.0)
    grad_scores[...] = jnp.zeros_like(grad_scores)
    grad_cross[...] = jnp.zeros_like(grad_cross)
    cross = dot_lanes(b_act[:HALF], c_act[HALF:]).astype(bf16)
    cumulative = aux[:, :HEADS]
    middle_row = cumulative[HALF - 1 : HALF]
    step2 = terms2(aux[:, HEADS : 2 * HEADS])
    decayed2 = terms2(aux[:, 3 * HEADS :])
    bridge2 = terms2(jnp.exp(jnp.concatenate([middle_row - cumulative[:HALF], cumulative[HALF:] - middle_row], axis=0)))
    cumulative4 = terms4(cumulative)
    for j in range(GT):
        columns[:, j * 512 : (j + 1) * 512] = dot(cumulative4, spread(4, 512, 4 * (j + group * GT), 7))
    low = lane_iota(HALF, HALF) < 64

    def body(j, carry):
        cols = tile_at(j)
        lead = 4 * (j + group * GT)
        select = spread(2, TILE, lead, 6)
        x = x_act[:, cols]
        u = x * dot(step2, select)
        bridge = dot(bridge2, select)
        u_low = u.astype(bf16)
        grad = dy[:, cols]
        wide = grad.astype(f32)
        early_raw = jnp.where(first, edge[:, cols], prior[:, cols]).astype(f32)
        pre = conv_of(shifted(now[:, cols].astype(f32), early_raw), taps[:, cols], bias[:, cols])
        sig = sigmoid(pre)
        slope[:, cols] = (sig + x * (1.0 - sig)).astype(bf16)
        k_dot[...] += split_dot(x * wide, head_select(j + group * GT))
        enter = jnp.where(first, entering[j], ends[0, j])
        out_bc[:, STATE:] += fine(dot_lanes, wide * dot(decayed2, select), enter)
        early = (u[:HALF] * bridge[:HALF]).astype(bf16)
        late = (grad[HALF:].astype(f32) * bridge[HALF:]).astype(bf16)
        grad_cross[...] += dot_lanes(early, late)
        across = dot(cross, late) * bridge[:HALF]
        totals = [None, None]
        for pair in range(2):
            lanes = slice(pair * 128, (pair + 1) * 128)
            place = pl.ds(pl.multiple_of(j * TILE + pair * 128, 128), 128)
            for b in range(2):
                rows = slice(b * HALF, (b + 1) * HALF)
                spaced = both_heads(low, grad[rows, lanes])
                products = dot_lanes(u_low[rows, lanes], spaced)
                weights = []
                for i in range(2):
                    head = 4 * j + 2 * pair + i
                    column = columns[rows, pl.ds(pl.multiple_of(head * 128, 128), 128)]
                    row = cum_t[pl.ds(head + 4 * GT * group, 1), :][:, rows]
                    weight = jnp.exp(jnp.minimum(row - column, 0.0))
                    part = weight * products[:, i * 128 : (i + 1) * 128]
                    totals[b] = part if totals[b] is None else totals[b] + part
                    weights.append((weight * scores[rows, :]).astype(bf16))
                du = dot(jnp.concatenate(weights, axis=1), spaced)
                if b == 0:
                    du = du + across[:, lanes]
                out[rows, place] = du.astype(bf16)
        for b in range(2):
            grad_scores[b * HALF : (b + 1) * HALF, :] += totals[b]
        return carry

    lax.fori_loop(0, GT, body, 0, unroll=GT)
    far = grad_cross[...].astype(bf16)
    near0 = jnp.where(upper, grad_scores[:HALF, :], 0.0).astype(bf16)
    near1 = jnp.where(upper, grad_scores[HALF:, :], 0.0).astype(bf16)
    out_bc[:HALF, :STATE] = dot(near0, c_act[:HALF]) + dot(far, c_act[HALF:])
    out_bc[HALF:, :STATE] = dot(near1, c_act[HALF:])
    out_bc[:HALF, STATE:] += dot_rows(near0, b_act[:HALF])
    out_bc[HALF:, STATE:] += dot_rows(near1, b_act[HALF:]) + dot_rows(far, b_act[:HALF])


def within_back(group, x_act, bc_act, aux, cum_t, dy, proj, proj_edge, taps, bias, ends, entering):
    length = x_act.shape[0]
    return pl.pallas_call(
        functools.partial(within_back_kernel, group),
        grid=(length // Q,),
        in_specs=[
            rows_of(GW), rows_of(BC), rows_of(128),
            pl.BlockSpec((HEADS, Q), lambda i: (0, i)), rows_of(GW, group),
            rows_of(GW), prior_rows(GW), fixed((EDGE, GW)),
            at_group(TAPS, group), at_group(1, group),
            pl.BlockSpec((1, GT, STATE, TILE), lambda i: (jnp.maximum(i - 1, 0), group, 0, 0)),
            pl.BlockSpec((GT, STATE, TILE), lambda i: (group, 0, 0), pipeline_mode=pl.Buffered(1)),
        ],
        out_specs=[rows_of(GW), rows_of(GW), rows_of(BC), rows_of(128)],
        out_shape=[
            shape_of((length, GW), bf16), shape_of((length, GW), bf16),
            shape_of((length, BC)), shape_of((length, 128)),
        ],
        scratch_shapes=[
            pltpu.VMEM((Q, HALF), f32),
            pltpu.VMEM((Q, HALF), f32),
            pltpu.VMEM((HALF, HALF), f32),
            pltpu.VMEM((Q, GT * 512), f32),
        ],
        compiler_params=cparams(),
        cost_estimate=cost(2 * 10**10, 14),
        name="within_back",
    )(x_act, bc_act, aux, cum_t, dy, proj, proj, proj_edge, taps, bias, ends, entering)


def middle_kernel(
    order, y_in0, y_in1, bc_act, aux, local0, local1, entering0, entering1, gate, tokens, cot, gain, w0, w1, w2, w3,
    normed_out, output, dy_out, grad_gate, ends, back_states, begin, payload, y_dot, gain_grad,
    full, state, back, before, y_keep, gated_keep, grad_keep,
):
    c = pl.program_id(0)

    @pl.when(c == 0)
    def _():
        assemble(order, (w0, w1, w2, w3), full)
        for g, entering in enumerate((entering0, entering1)):
            for j in range(GT):
                state[g * GT + j, :, :128] = entering[2 * j]
                state[g * GT + j, :, 128:] = entering[2 * j + 1]
        begin[...] = state[...]
        back[...] = jnp.zeros_like(back)
        before[...] = jnp.zeros_like(before)
        gain_grad[...] = jnp.zeros_like(gain_grad)

    keep = aux[...]
    c_high, c_low = halves(bc_act[:, STATE:])
    c_cols = (c_high, jnp.concatenate([c_high, c_low], axis=1))
    c_rows = halves(bc_act[:, STATE:].T)

    decayed2 = terms2(keep[:, 3 * HEADS :])
    ends4 = terms4(jnp.concatenate([keep[Q - 8 :, 3 * HEADS :], keep[Q - 8 :, :HEADS]], axis=0))

    def mix(y_in, local, shift, place, squares):
        j = place + shift
        cols = tile_at(j)
        carried = fine_short(c_cols, state[j])
        y = y_in[:, tile_at(place)] + dot(decayed2, spread(2, TILE, 4 * j, 6)) * carried
        y_keep[:, cols] = y
        raw = gate[:, cols].astype(f32)
        gated = y.astype(bf16).astype(f32) * (raw * sigmoid(raw))
        gated_keep[:, cols] = gated
        moved = dot(ends4, spread(4, TILE, 4 * j, 6))[7:8] * state[j] + local[0, place]
        state[j] = moved
        ends[0, j] = moved
        both = gated * gated
        return squares + (both[:, :128] + both[:, 128:])

    squares = jnp.zeros((Q, 128), f32)
    for g, (y_in, local) in enumerate(((y_in0, local0), (y_in1, local1))):
        squares = lax.fori_loop(0, GT, functools.partial(mix, y_in, local, g * GT), squares, unroll=GT)
    scale = lax.rsqrt(jnp.sum(squares, axis=1, keepdims=True) / INNER + EPS)

    def back_out(j, products):
        cols = tile_at(j)
        gated = gated_keep[:, cols]
        gains = gain[:, cols]
        normed_out[:, cols] = (gated * scale * gains).astype(bf16)
        grad = dot_lanes(cot[...], full[cols, :])
        grad_keep[:, cols] = grad
        gain_grad[:, cols] += jnp.sum(grad * gated * scale, axis=0, keepdims=True)
        both = grad * gains * gated
        return products + (both[:, :128] + both[:, 128:])

    products = lax.fori_loop(0, TILES, back_out, jnp.zeros((Q, 128), f32), unroll=8)
    shared = jnp.sum(products, axis=1, keepdims=True) / INNER * (scale * scale * scale)
    for start in range(0, output.shape[1], TILE):
        cols = slice(start, start + TILE)
        branch = dot(normed_out[...], full[:, cols])
        output[:, cols] = (tokens[:, cols].astype(f32) + branch).astype(bf16)

    def finish(j, y_sum):
        cols = tile_at(j)
        raw = gate[:, cols].astype(f32)
        sig = sigmoid(raw)
        grad_gated = scale * (grad_keep[:, cols] * gain[:, cols]) - gated_keep[:, cols] * shared
        y = y_keep[:, cols]
        dy = (grad_gated * (raw * sig)).astype(bf16)
        dy_out[:, cols] = dy
        mixed = y.astype(bf16).astype(f32)
        grad_gate[:, cols] = (grad_gated * mixed * (sig * (1.0 + raw * (1.0 - sig)))).astype(bf16)
        wide = dy.astype(f32)
        piece = fine_with(dot, c_rows, wide * dot(decayed2, spread(2, TILE, 4 * j, 6)))
        back_states[0, j] = piece
        back[j] += jnp.exp(before[:, cols]) * piece
        before[:, cols] += dot(ends4, spread(4, TILE, 4 * j, 6))[15:16]
        return y_sum + split_dot(wide * y, head_select(j))

    y_dot[...] = lax.fori_loop(0, TILES, finish, jnp.zeros((Q, 128), f32), unroll=8)

    @pl.when(c == pl.num_programs(0) - 1)
    def _():
        for g in range(GROUPS):
            for j in range(GT):
                payload[2 * j, :, g * 128 : (g + 1) * 128] = back[g * GT + j, :, :128]
                payload[2 * j + 1, :, g * 128 : (g + 1) * 128] = back[g * GT + j, :, 128:]


def middle(order, y_in, bc_act, aux, local, entering, gate, tokens, cot, gain, pieces):
    length, width = tokens.shape
    rows = pieces[0].shape[0]
    chunks = length // Q
    per_group = pl.BlockSpec((1, GT, STATE, TILE), lambda i, o: (i, 0, 0, 0))
    per_chunk = pl.BlockSpec((1, TILES, STATE, TILE), lambda i, o: (i, 0, 0, 0))
    return pl.pallas_call(
        middle_kernel,
        grid_spec=pltpu.PrefetchScalarGridSpec(
            num_scalar_prefetch=1,
            grid=(chunks,),
            in_specs=[rows_of(GW)] * 2
            + [rows_of(BC), rows_of(128)]
            + [per_group] * 2
            + [fixed((2 * GT, STATE, 128))] * 2
            + [rows_of(INNER), rows_of(width), rows_of(width), fixed((1, INNER))]
            + [fixed((rows, width))] * 4,
            out_specs=[
                rows_of(INNER), rows_of(width), rows_of(INNER), rows_of(INNER), per_chunk, per_chunk,
                kept((TILES, STATE, TILE)), kept((PIECES, STATE, TILE)), rows_of(128), kept((1, INNER)),
            ],
            scratch_shapes=[
                pltpu.VMEM((4 * rows, width), bf16),
                pltpu.VMEM((TILES, STATE, TILE), f32),
                pltpu.VMEM((TILES, STATE, TILE), f32),
                pltpu.VMEM((1, INNER), f32),
                pltpu.VMEM((Q, INNER), f32),
                pltpu.VMEM((Q, INNER), f32),
                pltpu.VMEM((Q, INNER), f32),
            ],
        ),
        out_shape=[
            shape_of((length, INNER), bf16),
            shape_of((length, width), bf16),
            shape_of((length, INNER), bf16),
            shape_of((length, INNER), bf16),
            shape_of((chunks, TILES, STATE, TILE)),
            shape_of((chunks, TILES, STATE, TILE)),
            shape_of((TILES, STATE, TILE)),
            shape_of((PIECES, STATE, TILE)),
            shape_of((length, 128)),
            shape_of((1, INNER)),
        ],
        compiler_params=cparams(),
        cost_estimate=cost(4 * 10**10, 40),
        name="middle",
    )(order, *y_in, bc_act, aux, *local, *entering, gate, tokens, cot, gain, *pieces)


def back_kernel(
    group, now, edge, taps, skip, dy, du_in, slope, x_act, bc_act, aux, ends, back_states, leaving, *others
):
    last_group = group == GROUPS - 1
    if last_group:
        (rest, rest_prior, rest_edge, taps_bc, bias_bc, heads, y_dot,
         k_dot0, k_dot1, x_before, edge_before, b_before, bc_in0, bc_in1,
         grad, grad_taps, tail, start, grad_taps_bc, grad_heads,
         later, after, x_dot, edge_dot, b_sum) = others
    else:
        (grad, grad_taps, tail, start, x_dot, edge_dot, b_sum, later, after) = others
    step_id = pl.program_id(0)
    first = step_id == pl.num_programs(0) - 1

    @pl.when(step_id == 0)
    def _():
        for j in range(GT):
            later[j, :, :128] = leaving[2 * j, :, group * 128 : (group + 1) * 128]
            later[j, :, 128:] = leaving[2 * j + 1, :, group * 128 : (group + 1) * 128]
        after[...] = jnp.zeros_like(after)
        grad_taps[...] = jnp.zeros_like(grad_taps)
        if last_group:
            grad_taps_bc[...] = jnp.zeros_like(grad_taps_bc)
            grad_heads[...] = jnp.zeros_like(grad_heads)

    keep = aux[...]
    b_act = bc_act[:, :STATE].astype(bf16)
    factors2 = terms2(
        jnp.concatenate([keep[:, HEADS * k : HEADS * (k + 1)] for k in range(1, 3)], axis=0)
    )
    ends4 = terms4(keep[Q - 8 :, 3 * HEADS :])
    x_dot[...] = jnp.zeros_like(x_dot)
    edge_dot[...] = jnp.zeros_like(edge_dot)
    b_sum[...] = jnp.zeros_like(b_sum)

    def through(cols, dv, raw, early, tap_values):
        parts = later_rows(dv, after[:, cols])
        result = conv_of(parts, tap_values, 0.0)
        after[:, cols] = dv[:8]
        grad[:, cols] = result.astype(bf16)

        @pl.when(step_id == 0)
        def _():
            tail[:, cols] = result[Q - EDGE :]

        early = jnp.where(first, early[EDGE - 8 :].astype(f32), 0.0)
        return tap_sums(parts, raw, dv, early)

    def body(j, carry):
        cols = tile_at(j)
        select = spread(2, TILE, 4 * (j + group * GT), 6)
        heads_of = head_select(j + group * GT)
        factors = dot(factors2, select)
        step, tail_decay = factors[:Q], factors[Q:]
        x = x_act[:, cols]
        later_state = later[j]
        du = du_in[:, cols].astype(f32) + tail_decay * dot(b_act, later_state.astype(bf16))
        x_dot[...] += split_dot(x * du, heads_of)
        b_sum[...] += fine(dot_lanes, x * step * tail_decay, later_state)
        meet = jnp.sum(ends[0, j] * later_state, axis=0, keepdims=True)
        edge_dot[...] += split_dot(jnp.broadcast_to(meet, (8, TILE)), heads_of)
        later[j] = dot(ends4, spread(4, TILE, 4 * (j + group * GT), 6))[7:8] * later_state + back_states[0, j]
        dv = (step * du + skip[:, cols] * dy[:, cols].astype(f32)) * slope[:, cols].astype(f32)
        grad_taps[:, cols] += through(cols, dv, now[:, cols].astype(f32), edge[:, cols], taps[:, cols])
        return carry

    lax.fori_loop(0, GT, body, 0, unroll=2 if last_group else GT)

    if last_group:
        band = slice(GW, GW + BC)
        current = rest[:, :BC].astype(f32)
        early = jnp.where(first, rest_edge[:, :BC], rest_prior[:, :BC])
        pre = conv_of(shifted(current, early.astype(f32)), taps_bc[...], bias_bc[...])
        sig = sigmoid(pre)
        grad_act = bc_in0[...] + bc_in1[...]
        grad_act = grad_act + jnp.concatenate([b_sum[...] + b_before[...], jnp.zeros((Q, STATE), f32)], axis=1)
        dv = grad_act * (sig * (1.0 + pre * (1.0 - sig)))
        grad_taps_bc[...] += through(band, dv, current, rest_edge[:, :BC], taps_bc[...])

        step = keep[:, HEADS : 2 * HEADS]
        by_step = x_dot[:, :HEADS] + x_before[:, :HEADS]
        by_skip = k_dot0[:, :HEADS] + k_dot1[:, :HEADS]
        rate = -jnp.exp(heads[0:1, :HEADS])
        by_sum = y_dot[:, :HEADS] - heads[1:2, :HEADS] * by_skip - step * by_step
        upper = jnp.where(row_iota(Q, Q) <= lane_iota(Q, Q), 1.0, 0.0)
        by_decay = jnp.dot(upper, by_sum, precision=highest, preferred_element_type=f32)
        by_decay = by_decay + (edge_dot[0:1, :HEADS] + edge_before[0:1, :HEADS])
        raw = rest[:, BC : BC + HEADS].astype(f32) + heads[2:3, :HEADS]
        grad_dt = (by_step + by_decay * rate) * sigmoid(raw)
        full_dt = jnp.concatenate([grad_dt, jnp.zeros((Q, 128 - HEADS), f32)], axis=1)
        grad[:, GW + BC :] = full_dt.astype(bf16)
        sums = [
            jnp.sum(by_decay * (rate * step), axis=0, keepdims=True),
            jnp.sum(by_skip, axis=0, keepdims=True),
            jnp.sum(grad_dt, axis=0, keepdims=True),
            jnp.zeros((5, HEADS), f32),
        ]
        grad_heads[:, :HEADS] += jnp.concatenate(sums, axis=0)

    @pl.when(first)
    def _():
        start[...] = after[...]


def backward(group, proj, proj_edge, taps, skip, dy, du, slope, x_act, bc_act, aux, ends, back_states, leaving, others=()):
    length = proj.shape[0]
    chunks = length // Q
    per = Q // EDGE
    last_group = group == GROUPS - 1
    at = lambda i: chunks - 1 - i
    block = lambda cols, g=0: pl.BlockSpec((Q, cols), lambda i: (at(i), g))
    per_chunk = pl.BlockSpec((1, GT, STATE, TILE), lambda i: (at(i), group, 0, 0))
    dots = pl.BlockSpec((8, 128), lambda i: (at(i), 0))
    in_specs = [
        block(GW), fixed((EDGE, GW)), at_group(TAPS, group), at_group(1, group),
        block(GW, group), block(GW), block(GW), block(GW), block(BC), block(128),
        per_chunk, per_chunk, fixed((PIECES, STATE, TILE)),
    ]
    width = GW + BC if last_group else GW
    cols = GW + REST if last_group else GW
    out_specs = [block(cols), kept((8, GW)), kept((EDGE, width)), kept((8, width))]
    out_shape = [
        shape_of((length, cols), bf16), shape_of((8, GW)), shape_of((EDGE, width)), shape_of((8, width)),
    ]
    scratch = [pltpu.VMEM((GT, STATE, TILE), f32), pltpu.VMEM((8, width), f32)]
    if last_group:
        in_specs += [
            block(REST),
            pl.BlockSpec((EDGE, REST), lambda i: (jnp.maximum(at(i) * per - 1, 0), 0)),
            fixed((EDGE, REST)), fixed((TAPS, BC)), fixed((1, BC)), fixed((8, 128)),
            block(128), block(128), block(128), block(128), dots, block(STATE), block(BC), block(BC),
        ]
        out_specs += [kept((8, BC)), kept((8, 128))]
        out_shape += [shape_of((8, BC)), shape_of((8, 128))]
        scratch += [pltpu.VMEM((Q, 128), f32), pltpu.VMEM((8, 128), f32), pltpu.VMEM((Q, STATE), f32)]
    else:
        out_specs += [block(128), dots, block(STATE)]
        out_shape += [shape_of((length, 128)), shape_of((8 * chunks, 128)), shape_of((length, STATE))]
    return pl.pallas_call(
        functools.partial(back_kernel, group),
        grid=(chunks,),
        in_specs=in_specs,
        out_specs=out_specs,
        out_shape=out_shape,
        scratch_shapes=scratch,
        compiler_params=cparams(),
        cost_estimate=cost(2 * 10**10, 20),
        name="backward",
    )(proj, proj_edge, taps, skip, dy, du, slope, x_act, bc_act, aux, ends, back_states, leaving, *others)


def quarters(left, order):
    rows = left.shape[1] // 4
    block = [lax.dynamic_slice_in_dim(left, order[k] * rows, rows, axis=1) for k in range(4)]
    return jnp.concatenate([block[1], block[3]], axis=1), jnp.concatenate([block[0], block[2]], axis=1)


def weight_grad(parts, right):
    sent, held = parts
    return dot_rows(right, sent).astype(bf16), dot_rows(right, held).astype(bf16)


def out_weight_sums(parts, right):
    sent, held = parts
    return dot_rows(sent, right).astype(bf16), dot_rows(held, right).astype(bf16)


def input_kernel(
    order, grad_gate, grad_x0, grad_x1, tokens, cot, gain,
    g0, g1, g2, g3, a0, a1, a2, a3, b0, b1, b2, b3, out, gain_grad,
):
    rows = g0.shape[0]

    @pl.when(pl.program_id(0) == 0)
    def _():
        gain_grad[...] = jnp.zeros_like(gain_grad)

    for k, (gate_w, a_w, b_w) in enumerate(((g0, a0, b0), (g1, a1, b1), (g2, a2, b2), (g3, a3, b3))):
        cols = pl.ds(pl.multiple_of(order[k] * rows, rows), rows)
        total = dot_lanes(grad_gate[...], gate_w[...]) + dot_lanes(grad_x0[...], a_w[:, :GW])
        total = total + dot_lanes(grad_x1[:, :GW], b_w[...])
        out[:, cols] = total + dot_lanes(grad_x1[:, GW:], a_w[:, GW:])
    grad = out[...]
    wide = tokens[...].astype(f32)
    width = wide.shape[1]
    scale = lax.rsqrt(jnp.mean(wide * wide, axis=1, keepdims=True) + EPS)
    gain_grad[...] += jnp.sum(grad * wide * scale, axis=0, keepdims=True)
    scaled = grad * gain[...]
    shared = jnp.sum(scaled * wide, axis=1, keepdims=True) / width
    out[...] = cot[...].astype(f32) + (scale * scaled - wide * (scale * scale * scale * shared))


def input_back(order, grad_gate, grad_x0, grad_x1, tokens, cot, gain, gate_pieces, a_pieces, b_pieces):
    length, width = tokens.shape
    rows = width // 4
    return pl.pallas_call(
        input_kernel,
        grid_spec=pltpu.PrefetchScalarGridSpec(
            num_scalar_prefetch=1,
            grid=(length // Q,),
            in_specs=[rows_of(INNER), rows_of(GW), rows_of(GW + REST), rows_of(width), rows_of(width), fixed((1, width))]
            + [fixed((rows, INNER))] * 4
            + [fixed((rows, GW + REST))] * 4
            + [fixed((rows, GW))] * 4,
            out_specs=[rows_of(width), kept((1, width))],
        ),
        out_shape=[shape_of((length, width)), shape_of((1, width))],
        compiler_params=cparams(),
        cost_estimate=cost(4 * length * width * (INNER + XCOLS), 26),
        name="input_back",
    )(order, grad_gate, grad_x0, grad_x1, tokens, cot, gain, *gate_pieces, *a_pieces, *b_pieces)


def swap(value, axis, bit):
    count = lax.axis_size(axis)
    return lax.ppermute(value, axis, [(i, i ^ bit) for i in range(count)])


def exchange(value, axis):
    return lax.all_to_all(value, axis, split_axis=0, concat_axis=0, tiled=True)


def tie(value, *others):
    return lax.optimization_barrier((value, others))[0]


def to_owners(value, groups=1):
    count = lax.axis_size("seq")
    pieces, rows, lanes = value.shape
    if count != pieces:
        lanes //= groups
        width = pieces * lanes // count
        split = value.reshape(pieces, rows, groups, lanes // width, width)
        value = split.transpose(0, 3, 1, 2, 4).reshape(count, rows, groups * width)
    return exchange(value, "seq")


def from_owners(value, groups=1, pieces=PIECES, lanes=128):
    value = exchange(value, "seq")
    count, rows, width = value.shape
    if count == pieces:
        return value
    width //= groups
    split = value.reshape(pieces, lanes // width, rows, groups, width)
    return split.transpose(0, 2, 3, 1, 4).reshape(pieces, rows, groups * lanes)


def send_core(grads):
    sent, held = grads
    return held, swap(sent, "wshard", 1)


def send_x(state, axis=1):
    held, got = state
    own, other = jnp.split(held, 2, axis=axis)
    got_own, got_other = jnp.split(got, 2, axis=axis)
    return (
        own.astype(f32) + got_own.astype(f32),
        swap((other.astype(f32) + got_other.astype(f32)).astype(bf16), "wshard", 2),
    )


def sum_pair(state):
    mine, got = state
    return mine + got.astype(f32)


def fold(value):
    rows, cols = value.shape
    return value.reshape(rows, cols // TILE, TILE).swapaxes(0, 1).reshape(-1, TILE)


def unfold(value, cols):
    return value.reshape(cols // TILE, -1, TILE).swapaxes(0, 1).reshape(-1, cols)


def send_near_pair(even, odd):
    is_even = (lax.axis_index("seq") & 1) == 0
    theirs = jnp.where(is_even, odd, even).astype(bf16)
    return jnp.where(is_even, even, odd), swap(theirs, "seq", 1)


def send_near(state):
    mine, got = state
    total = mine + got.astype(f32)
    half = total.shape[0] // 2
    bit = lax.axis_index("seq") & 1
    theirs = lax.dynamic_slice_in_dim(total, (1 - bit) * half, half, axis=0).astype(bf16)
    return lax.dynamic_slice_in_dim(total, bit * half, half, axis=0), swap(theirs, "seq", 1)


def send_far(state):
    mine, got = state
    total = mine + got.astype(f32)
    group = lax.axis_size("seq") // 2
    place = lax.axis_index("seq") >> 1
    part = total.shape[0] // group
    piece = lambda k: lax.dynamic_slice_in_dim(total, (place ^ k) * part, part, axis=0)
    return piece(0), [swap(piece(k).astype(bf16), "seq", 2 * k) for k in range(1, group)]


def share_far(state):
    mine, got = state
    owned = (mine + sum(piece.astype(f32) for piece in got)).astype(bf16)
    return [owned] + [swap(owned, "seq", 2 * k) for k in range(1, len(got) + 1)]


def in_order(pieces, place, join=True):
    bit = 1
    while bit < len(pieces):
        odd = (place & bit) != 0
        pieces = [jnp.where(odd, pieces[k ^ bit], pieces[k]) for k in range(len(pieces))]
        bit *= 2
    return jnp.concatenate(pieces, axis=0) if join else pieces


def share_near(pieces):
    half = in_order(pieces, lax.axis_index("seq") >> 1)
    return [half, swap(half, "seq", 1)]


def whole_rows(pieces):
    return in_order(pieces, lax.axis_index("seq") & 1)


def local(
    block_in, norm_gain, in_weight, conv_x, conv_x_bias, conv_bc, conv_bc_bias,
    a_log, skip, dt_bias, out_gain, out_weight, cotangent,
):
    tokens = block_in[0]
    cot = cotangent[0]
    length, width = tokens.shape
    seq = lax.axis_size("seq")
    shards = lax.axis_size("wshard")
    own_heads = HEADS // seq
    own_ch = INNER // seq
    me = lax.axis_index("wshard")
    order = jnp.stack([me ^ k for k in range(4)]).astype(jnp.int32)
    place = lax.axis_index("seq")

    a_piece = jnp.concatenate(
        [in_weight[:, INNER : INNER + GW], jnp.pad(in_weight[:, 2 * INNER :], ((0, 0), (0, XCOLS - XUSED)))], axis=1
    )
    b_piece = in_weight[:, INNER + GW : 2 * INNER]
    gate_piece = in_weight[:, :INNER]
    edge = lax.ppermute(tokens[length - EDGE :], "seq", [(i, i + 1) for i in range(seq - 1)])
    small = jnp.concatenate(
        [
            conv_x,
            conv_x_bias[None],
            jnp.pad(jnp.stack([a_log, skip, dt_bias]), ((0, 0), (0, own_ch - own_heads))),
        ],
        axis=0,
    )
    a_across, a_beside = swap(a_piece, "wshard", 2), swap(a_piece, "wshard", 1)
    small_all = exchange(jnp.broadcast_to(small[None], (seq,) + small.shape), "seq")
    x_params = small_all[:, :5].transpose(1, 0, 2).reshape(5, INNER)
    head_params = small_all[:, 5:, :own_heads].transpose(1, 0, 2).reshape(3, HEADS)
    taps, bias = x_params[:4], x_params[4:5]
    heads = jnp.pad(head_params, ((0, 5), (0, 128 - HEADS)))
    skip_row = jnp.repeat(head_params[1], INNER // HEADS)[None]
    bias_bc = conv_bc_bias[None]
    a_across = tie(a_across, small_all, edge, a_beside)
    a_pieces = (a_piece, a_beside, a_across, swap(a_across, "wshard", 1))
    b_piece, gate_piece, out_piece = tie((b_piece, gate_piece, out_weight), a_across)
    b_across, b_beside = swap(b_piece, "wshard", 2), swap(b_piece, "wshard", 1)

    normed, proj0, rest, proj_edge0, rest_edge = project(order, tokens, edge, norm_gain[None], a_pieces)
    gate_across, gate_beside = swap(gate_piece, "wshard", 2), swap(gate_piece, "wshard", 1)
    out_across, out_beside = swap(out_piece, "wshard", 2), swap(out_piece, "wshard", 1)
    bc_act, aux, cum_t = factors(rest, rest_edge, conv_bc, bias_bc, heads)
    b_across = tie(b_across, bc_act)
    b_pieces = (b_piece, b_beside, b_across, swap(b_across, "wshard", 1))
    x_act0, local0, payload0 = states(0, proj0, proj_edge0, taps, bias, bc_act, aux)
    arrived0 = to_owners(payload0)
    proj1, proj_edge1 = project_more(order, tie(normed, payload0), edge, norm_gain[None], b_pieces)
    x_act1, local1, payload1 = states(1, proj1, proj_edge1, taps, bias, bc_act, aux)
    arrived1 = to_owners(payload1)
    y0 = within(0, tie(x_act0, payload1), bc_act, aux, cum_t, skip_row)
    gate_pieces = (gate_piece, gate_beside, gate_across, swap(gate_across, "wshard", 1))
    gate = gate_project(order, tie(normed, y0), gate_pieces)
    entering0 = chain(True, *tie((arrived0, arrived0[:, STATE:, :]), gate))
    totals0, totals1 = arrived0[:, STATE:, :], arrived1[:, STATE:, :]
    back0 = from_owners(entering0)
    entering1 = chain(True, *tie((arrived1, totals1), entering0))
    back1 = from_owners(entering1)
    y1 = within(1, tie(x_act1, entering1), bc_act, aux, cum_t, skip_row)
    entering0, entering1 = tie((back0, back1), y1)
    out_pieces = (out_piece, out_beside, out_across, swap(out_across, "wshard", 1))
    (normed_out, output, dy, grad_gate, ends, back_states, begin, back_payload, y_dot, out_gain_grad) = middle(
        order, (y0, y1), bc_act, aux, (local0, local1), (entering0, entering1), gate, tokens, cot, out_gain[None], out_pieces
    )

    back_arrived = to_owners(back_payload, 2)
    totals = jnp.concatenate([totals0, totals1], axis=2)
    normed_parts = quarters(normed, order)
    out_grads = out_weight_sums(quarters(normed_out, order), cot)
    out_core = send_core(out_grads)
    gate_grads = weight_grad(normed_parts, tie(grad_gate, out_grads))
    gate_core = send_core(gate_grads)
    du0, slope0, grad_bc0, k_dot0 = within_back(
        0, tie(x_act0, gate_grads), bc_act, aux, cum_t, dy, proj0, proj_edge0, taps, bias, ends, begin
    )
    out_x = send_x(tie(out_core, du0), axis=0)
    gate_x = send_x(tie(gate_core, out_x[0]))
    leaving = chain(False, *tie((back_arrived, totals), gate_x[0]))
    leave = from_owners(leaving, 2)
    du1, slope1, grad_bc1, k_dot1 = within_back(
        1, tie(x_act1, leaving), bc_act, aux, cum_t, dy, proj1, proj_edge1, taps, bias, ends, begin
    )
    out_fold = fold(sum_pair(tie(out_x, du1)))
    leave = tie(leave, out_fold)
    grad_x0, grad_taps0, tail0, start0, x_dot0, edge_dot0, b_sum0 = backward(
        0, proj0, proj_edge0, taps, skip_row, dy, du0, slope0, x_act0, bc_act, aux, ends, back_states, leave
    )
    all_taps = jnp.concatenate([taps[:, GW:], conv_bc], axis=1)
    backwards = [(i, i - 1) for i in range(1, seq)]

    def fix(grad, tail, start, tap_values):
        fixes = [
            tail[EDGE - 3 + a] + sum(tap_values[k] * start[a - k] for k in range(a + 1)) for a in range(3)
        ]
        fixed_rows = jnp.concatenate([tail[: EDGE - 3], jnp.stack(fixes)], axis=0).astype(bf16)
        return lax.dynamic_update_slice(grad, fixed_rows, (length - EDGE, 0))

    after0 = lax.ppermute(start0, "seq", backwards)
    gate_pair = sum_pair(tie(gate_x, grad_x0))
    early_near = send_near_pair(gate_pair, out_fold)
    grad_x0 = fix(tie(grad_x0, early_near[0]), tail0, after0, taps[:, :GW])
    x0_grads = weight_grad(normed_parts, grad_x0)
    x0_core = send_core(x0_grads)
    x0_x = send_x(x0_core)
    grad_x1, grad_taps1, tail1, start1, grad_taps_bc, grad_heads = backward(
        1, proj1, proj_edge1, taps, skip_row, tie(dy, x0_x[0]), du1, slope1, x_act1, bc_act, aux, ends, back_states,
        leave,
        (rest, rest, rest_edge, conv_bc, bias_bc, heads, y_dot, k_dot0, k_dot1, x_dot0, edge_dot0, b_sum0, grad_bc0, grad_bc1),
    )
    x0_near = send_near(tie(x0_x, grad_x1))
    early_far = send_far(tie(early_near, x0_near[0]))
    after1 = lax.ppermute(tie(start1, x0_near[0]), "seq", backwards)
    grad_x1 = fix(tie(grad_x1, early_far[0]), tail1, after1, all_taps)
    x1_grads = weight_grad(normed_parts, grad_x1)
    x1_core = send_core(x1_grads)
    x0_far = send_far(tie(x0_near, x1_grads))
    x1_x = send_x(tie(x1_core, x0_far[0]))
    early_all = share_far(tie(early_far, x1_x[0]))
    x0_all = share_far(tie(x0_far, early_all[0]))
    input_grad, norm_gain_grad = input_back(
        order, tie(grad_gate, x0_all[0]), grad_x0, grad_x1, tokens, cot, norm_gain[None], gate_pieces, a_pieces, b_pieces
    )
    x1_near = send_near(tie(x1_x, input_grad))
    norm_gain_grad = tie(norm_gain_grad, x1_near[0])
    grad_taps = jnp.concatenate([grad_taps0, grad_taps1], axis=1)
    shared = jnp.concatenate(
        [norm_gain_grad[0], out_gain_grad[0], grad_taps_bc[:5].reshape(-1)]
    )
    mine = jnp.concatenate(
        [
            grad_taps[:5].reshape(5, seq, own_ch).transpose(1, 0, 2).reshape(seq, 5 * own_ch),
            grad_heads[:3, :HEADS].reshape(3, seq, own_heads).transpose(1, 0, 2).reshape(seq, 3 * own_heads),
        ],
        axis=1,
    )
    shared_size, mine_size = shared.shape[0], mine.shape[1]
    pad = -(shared_size + mine_size) % 1024
    small_out = jnp.concatenate(
        [jnp.broadcast_to(shared[None], (seq, shared_size)), mine, jnp.zeros((seq, pad), f32)], axis=1
    )
    small_out = jnp.broadcast_to(small_out[:, None], (seq, shards, small_out.shape[1]))
    small_sum = jnp.sum(
        exchange(small_out.reshape(seq * shards, 8, -1), ("seq", "wshard")), axis=0
    ).reshape(-1)
    early_half = share_near(tie(early_all, small_out))
    x0_half = share_near(tie(x0_all, early_half[0]))
    x1_far = send_far(tie(x1_near, x0_half[0]))
    x1_all = share_far(x1_far)
    x1_half = share_near(tie(x1_all, small_sum, early_half[1]))
    gate_sum, out_sum = in_order(early_half, place & 1, join=False)
    out_owned = unfold(out_sum, width).astype(f32)
    in_owned = jnp.concatenate(
        [gate_sum, whole_rows(x0_half), whole_rows(x1_half)[: XUSED - GW]], axis=0
    ).astype(f32).T
    pos = [0]

    def take(shape):
        size = 1
        for extent in shape:
            size *= extent
        out = small_sum[pos[0] : pos[0] + size].reshape(shape)
        pos[0] += size
        return out

    norm_gain_sum = take((width,))
    out_gain_sum = take((INNER,))
    bc_sum = take((5, BC))
    x_sum = take((5, own_ch))
    head_sum = take((3, own_heads))
    return (
        output[None],
        input_grad[None],
        norm_gain_sum,
        in_owned,
        x_sum[:4],
        x_sum[4],
        bc_sum[:4],
        bc_sum[4],
        head_sum[0],
        head_sum[1],
        head_sum[2],
        out_gain_sum,
        out_owned,
    )


def solution(mesh):
    in_specs = (
        P("wshard", "seq", None),
        P(),
        P("wshard", None),
        P(None, "seq"),
        P("seq"),
        P(),
        P(),
        P("seq"),
        P("seq"),
        P("seq"),
        P(),
        P("wshard", None),
        P("wshard", "seq", None),
    )
    out_specs = (
        P("wshard", "seq", None),
        P("wshard", "seq", None),
        P(),
        P("wshard", None),
        P(None, "seq"),
        P("seq"),
        P(),
        P(),
        P("seq"),
        P("seq"),
        P("seq"),
        P(),
        P("wshard", None),
    )
    return jax.shard_map(local, mesh=mesh, in_specs=in_specs, out_specs=out_specs, check_vma=False)
```
